128 devices in a mesh: tm: 8 (over y, core), height: 8 (over z, x_hi), width: 2 (over x_lo).
Axes of the slice: x: 4 (x_hi: 2, x_lo: 2; x = x_hi * 2 + x_lo), y: 4, z: 4, core: 2. Of those that a mesh axis runs over, the one named last changes fastest.
Arguments:
- features: bfloat16 [16, 16, 128, 256], P('tm', ('height', 'width')), may hold values from -6 to 6
- conv_first: bfloat16 [3, 3, 3, 256, 256], replicated, may hold values from -0.078125 to 0.078125
- conv_second: bfloat16 [3, 3, 3, 256, 256], replicated, may hold values from -0.078125 to 0.078125
- up_kernel: bfloat16 [4, 4, 256, 256], replicated, may hold values from -0.1875 to 0.1875
- cotangent: bfloat16 [16, 32, 256, 256], P('tm', 'height', 'width'), may hold values from -6 to 6
Outputs:
- grad_features: bfloat16 [16, 16, 128, 256], P('tm', ('height', 'width'))
- grad_first: float32 [1769472], P(('tm', 'height', 'width'))
- grad_second: float32 [1769472], P(('tm', 'height', 'width'))
- grad_up: float32 [1048576], P(('tm', 'height', 'width'))
The draws below stay inside these ranges and needn't reach their ends.
All inputs are finite; a program needn't handle non-finite values.
Results may differ from the reference program's by a relative error of at most 0.006.
Values may be sent and summed in bfloat16 or wider, within the bound.
No kernel may reach another device: no remote copies, remote signals or barrier semaphores. Data moves between devices by JAX's collectives and lax.ppermute only.
A program may use at most 128 MiB of HBM per device.

```python
import jax
import jax.numpy as jnp
from jax import lax

C = 256
COLUMNS = 128
FRAMES = 16
ROWS = 16


def block_levels(rng, dims, shards, least, top_value):
    def one(position, blocks):
        draws = jax.random.uniform(jax.random.fold_in(jax.random.fold_in(rng, 6), position), (blocks,), jnp.float32, least / len(shards), top_value / len(shards))
        return jnp.repeat(jnp.exp(draws), dims[position] // blocks).reshape((-1,) + (1,) * (len(dims) - position - 1))

    factor_of = one(*shards[0])
    for cut in shards[1:]:
        factor_of = factor_of * one(*cut)
    return factor_of


def gaussian(rng, dims, deviation, most, cuts=(), held_as=jnp.bfloat16):
    result = jax.random.normal(rng, dims, jnp.float32) * deviation
    if len(cuts) > 0:
        result = block_levels(rng, dims, cuts, -0.22, 0.18) * result
    return jnp.clip(result, min=-most, max=most).astype(held_as)


def setup_inputs(seed: int = 0) -> dict:
    streams_of = jax.random.split(jax.random.key(seed), 6)
    return {
        "features": gaussian(streams_of[0], (FRAMES, ROWS, COLUMNS, C), 1.0, 6.0, ((0, 8), (1, 16))),
        "conv_first": gaussian(streams_of[1], (3, 3, 3, C, C), (27 * C) ** -0.5, 0.078125),
        "conv_second": gaussian(streams_of[2], (3, 3, 3, C, C), (27 * C) ** -0.5, 0.078125),
        "up_kernel": gaussian(streams_of[3], (4, 4, C, C), (4 * C) ** -0.5, 0.1875),
        "cotangent": gaussian(streams_of[4], (FRAMES, 2 * ROWS, 2 * COLUMNS, C), 1.0, 6.0, ((0, 8), (1, 8), (2, 2))),
    }


def silu_slope(values):
    sigma = jax.nn.sigmoid(values)
    return sigma * (1.0 + values * (1.0 - sigma))

def conv_taps(padded, kernel, frame_count, row_count, column_count):
    channels = padded.shape[-1]
    outputs = kernel.shape[-1]
    summed = jnp.zeros((frame_count * row_count * column_count, outputs), jnp.float32)
    for tap_t in range(3):
        for tap_h in range(3):
            patches = jnp.concatenate([padded[tap_t:tap_t + frame_count, tap_h:tap_h + row_count, tap_w:tap_w + column_count] for tap_w in range(3)], axis=-1)
            summed = summed + jnp.dot(patches.reshape(-1, 3 * channels), kernel[tap_t, tap_h].reshape(3 * channels, outputs), preferred_element_type=jnp.float32)
    return summed.reshape(frame_count, row_count, column_count, outputs)

def kernel_grads(padded, gradient, frame_count, row_count, column_count):
    channels = padded.shape[-1]
    flattened = gradient.reshape(-1, gradient.shape[-1])
    pieces = []
    for tap_t in range(3):
        for tap_h in range(3):
            patches = jnp.concatenate([padded[tap_t:tap_t + frame_count, tap_h:tap_h + row_count, tap_w:tap_w + column_count] for tap_w in range(3)], axis=-1)
            pieces.append(lax.dot_general(patches.reshape(-1, 3 * channels), flattened, (((0,), (0,)), ((), ())), preferred_element_type=jnp.float32))
    return jnp.stack(pieces).reshape(-1)

def reverse_kernel(kernel):
    return jnp.transpose(jnp.flip(kernel, (0, 1, 2)), (0, 1, 2, 4, 3))

def upsample_back(padded_cot, activation, up_kernel, row_count, column_count):
    frame_count = activation.shape[0]
    channels = activation.shape[-1]
    parity_view = padded_cot.reshape(frame_count, row_count + 1, 2, column_count + 1, 2, channels)
    act_flat = activation.reshape(-1, channels)
    summed = jnp.zeros((act_flat.shape[0], channels), jnp.float32)
    pieces = []
    for tap_y in range(4):
        joined = jnp.concatenate([parity_view[:, tap_y // 2:tap_y // 2 + row_count, tap_y % 2, tap_x // 2:tap_x // 2 + column_count, tap_x % 2] for tap_x in range(4)], axis=-1)
        joined = joined.reshape(-1, 4 * channels)
        summed = summed + jnp.dot(joined, jnp.transpose(up_kernel[tap_y], (0, 2, 1)).reshape(4 * channels, channels), preferred_element_type=jnp.float32)
        product = lax.dot_general(act_flat, joined, (((0,), (0,)), ((), ())), preferred_element_type=jnp.float32)
        pieces.append(jnp.transpose(product.reshape(channels, 4, channels), (1, 0, 2)))
    grad_act = summed.reshape(frame_count, row_count, column_count, channels)
    return (grad_act, jnp.stack(pieces).reshape(-1))

def reference(features, conv_first, conv_second, up_kernel, cotangent):
    frame_count, row_count, column_count, channels = features.shape
    front = ((2, 0), (1, 1), (1, 1), (0, 0))
    back = ((0, 2), (1, 1), (1, 1), (0, 0))
    padded_in = jnp.pad(features, front)
    first_pre = conv_taps(padded_in, conv_first, frame_count, row_count, column_count)
    first_act = jax.nn.silu(first_pre).astype(jnp.bfloat16)
    padded_act = jnp.pad(first_act, front)
    summed = features.astype(jnp.float32) + conv_taps(padded_act, conv_second, frame_count, row_count, column_count)
    up_act = jax.nn.silu(summed).astype(jnp.bfloat16)
    padded_cot = jnp.pad(cotangent, ((0, 0), (1, 1), (1, 1), (0, 0)))
    grad_full, up_sum = upsample_back(padded_cot, up_act, up_kernel, row_count, column_count)
    grad_act = lax.optimization_barrier(grad_full.astype(jnp.bfloat16))
    grad_summed = (grad_act.astype(jnp.float32) * silu_slope(summed)).astype(jnp.bfloat16)
    second_sum = kernel_grads(padded_act, grad_summed, frame_count, row_count, column_count)
    grad_inner = conv_taps(jnp.pad(grad_summed, back), reverse_kernel(conv_second), frame_count, row_count, column_count)
    grad_hidden = (grad_inner * silu_slope(first_pre)).astype(jnp.bfloat16)
    first_sum = kernel_grads(padded_in, grad_hidden, frame_count, row_count, column_count)
    grad_features = (grad_summed.astype(jnp.float32) + conv_taps(jnp.pad(grad_hidden, back), reverse_kernel(conv_first), frame_count, row_count, column_count)).astype(jnp.bfloat16)
    factor = 1.0 / jnp.sqrt(jnp.float32(frame_count * row_count * column_count))
    return (grad_features, first_sum * factor, second_sum * factor, up_sum * factor)
```

```python
import functools
import math

import jax
import jax.numpy as jnp
from jax import lax
from jax.experimental import pallas as pl
from jax.experimental.pallas import tpu as pltpu
from jax.sharding import Mesh, PartitionSpec as P

F32 = jnp.float32
BF16 = jnp.bfloat16
VMEM_LIMIT = 48 * 1024 * 1024

FR = 4
ROWS = 16
WIN = 16
OWN = 8
EDGE = 4
CH = 256
TAPS = 27
SHARE = 54


def slope_of(values, sigma):
    return sigma * (1.0 + values * (1.0 - sigma))


def nt(lhs, rhs):
    return lax.dot_general(lhs, rhs, (((1,), (1,)), ((), ())), preferred_element_type=F32)


def nn(lhs, rhs):
    return jnp.dot(lhs, rhs, preferred_element_type=F32)


def fill_table(table, slot, block, forward):
    wide = block.astype(F32)
    before = pltpu.roll(wide, 1, axis=1).astype(BF16)
    after = pltpu.roll(wide, WIN - 1, axis=1).astype(BF16)
    table[slot, 1 : ROWS + 1, :, 0:CH] = before if forward else after
    table[slot, 1 : ROWS + 1, :, CH : 2 * CH] = block
    table[slot, 1 : ROWS + 1, :, 2 * CH : 3 * CH] = after if forward else before


def fill_own_table(table, slot, block):
    wide = block.astype(F32)
    for tap in range(3):
        moved = pltpu.roll(wide, WIN - (EDGE + 1 - tap), axis=1)
        table[slot, 1 : ROWS + 1, :, tap * CH : (tap + 1) * CH] = moved[:, :OWN].astype(BF16)


def clear_border(table):
    frames, _, columns, lanes = table.shape
    border = jnp.zeros((frames, columns, lanes), BF16)
    table[:, 0] = border
    table[:, ROWS + 1] = border


def own_columns(block):
    return pltpu.roll(block.astype(F32), WIN - EDGE, axis=1)[:, :OWN]


def first_kernel(halo, block, weights, mask, act, slope, table, total):
    step = pl.program_id(0)

    @pl.when(step == 0)
    def _():
        clear_border(table)
        for frame in range(2):
            fill_table(table, frame, halo[:, frame], True)
        for frame in range(FR):
            fill_table(table, 2 + frame, block[frame // 2, :, frame % 2], True)
        total[...] = jnp.zeros_like(total)

    for tap in range(3):
        lhs = table[pl.ds(step, FR), tap : tap + ROWS].reshape(FR * ROWS * WIN, 3 * CH)
        total[...] += nn(lhs, weights[0, tap].reshape(3 * CH, CH))

    @pl.when(step == 2)
    def _():
        inside = mask[...]
        for frame in range(FR):
            rows = ROWS * WIN
            values = total[frame * rows : (frame + 1) * rows].reshape(ROWS, WIN, CH)
            sigma = jax.nn.sigmoid(values)
            act[frame] = (values * sigma * inside).astype(BF16)
            slope[frame] = slope_of(values, sigma)


def second_kernel(halo, block, features, grad_act, weights, mask, grad_sum, up_act, table, total):
    step = pl.program_id(0)

    @pl.when(step == 0)
    def _():
        clear_border(table)
        for frame in range(2):
            fill_table(table, frame, halo[frame], True)
        for frame in range(FR):
            fill_table(table, 2 + frame, block[frame], True)
        total[...] = jnp.zeros_like(total)

    for tap in range(3):
        lhs = table[pl.ds(step, FR), tap : tap + ROWS].reshape(FR * ROWS * WIN, 3 * CH)
        total[...] += nn(lhs, weights[0, tap].reshape(3 * CH, CH))

    @pl.when(step == 2)
    def _():
        inside = mask[...]
        for frame in range(FR):
            rows = ROWS * WIN
            values = total[frame * rows : (frame + 1) * rows].reshape(ROWS, WIN, CH)
            values = values + features[frame // 2, :, frame % 2].astype(F32)
            sigma = jax.nn.sigmoid(values)
            up_act[frame] = (values * sigma).astype(BF16)
            grad = grad_act[frame].astype(F32) * slope_of(values, sigma) * inside
            grad_sum[frame] = grad.astype(BF16)


def hidden_kernel(block, later, slope, weights, mask, grad_hidden, table, total):
    step = pl.program_id(0)

    @pl.when(step == 0)
    def _():
        clear_border(table)
        for frame in range(FR):
            fill_table(table, frame, block[frame], False)
        for frame in range(2):
            fill_table(table, FR + frame, later[frame], False)
        total[...] = jnp.zeros_like(total)

    for tap in range(3):
        part = None
        for column in range(3):
            lhs = table[pl.ds(2 - step, FR), 2 - tap : 2 - tap + ROWS, :, column * CH : (column + 1) * CH]
            more = nt(lhs.reshape(FR * ROWS * WIN, CH), weights[0, tap, column])
            part = more if part is None else part + more
        total[...] += part

    @pl.when(step == 2)
    def _():
        inside = mask[...]
        for frame in range(FR):
            rows = ROWS * WIN
            values = total[frame * rows : (frame + 1) * rows].reshape(ROWS, WIN, CH)
            grad_hidden[frame] = (values * slope[frame] * inside).astype(BF16)


def features_kernel(core_ref, block, later, grad_sum, weights, grad_features, table, total):
    step = pl.program_id(0)
    core = core_ref[0]

    @pl.when(step == 0)
    def _():
        clear_border(table)
        for frame in range(FR):
            fill_own_table(table, frame, block[frame])
        for frame in range(2):
            fill_own_table(table, FR + frame, later[frame])
        total[...] = jnp.zeros_like(total)

    for tap in range(3):
        part = None
        for column in range(3):
            lhs = table[
                pl.ds(2 * core + 2 - step, 2), 2 - tap : 2 - tap + ROWS, :, column * CH : (column + 1) * CH
            ]
            more = nt(lhs.reshape(2 * ROWS * OWN, CH), weights[0, tap, column])
            part = more if part is None else part + more
        total[...] += part

    @pl.when(step == 2)
    def _():
        for frame in range(2):
            rows = ROWS * OWN
            values = total[frame * rows : (frame + 1) * rows].reshape(ROWS, OWN, CH)
            values = values + own_columns(grad_sum[2 * core + frame])
            grad_features[:, frame] = values.astype(BF16)


def cotangent_kernel(core_ref, mine, other, weights, grad_act, table):
    core = core_ref[0]
    border = jnp.zeros((FR, WIN, 4 * CH), BF16)
    table[:, 0, 0] = border
    table[:, ROWS, 1] = border
    for source, which in ((mine, core), (other, 1 - core)):
        for frame in range(2):
            slot = 2 * which + frame
            for parity in range(2):
                fine = source[:, frame, :, parity].reshape(ROWS, WIN, 2 * CH)
                even, odd = fine[:, :, :CH], fine[:, :, CH:]
                before = pltpu.roll(odd.astype(F32), 1, axis=1).astype(BF16)
                after = pltpu.roll(even.astype(F32), WIN - 1, axis=1).astype(BF16)
                low = 0 if parity == 0 else 1
                put = (slot, slice(low, low + ROWS), 1 - parity)
                table[put + (slice(None), slice(0, CH))] = before
                table[put + (slice(None), slice(CH, 2 * CH))] = even
                table[put + (slice(None), slice(2 * CH, 3 * CH))] = odd
                table[put + (slice(None), slice(3 * CH, 4 * CH))] = after
    for frame in range(FR):
        part = None
        for tap in range(4):
            for column in range(4):
                lhs = table[frame, tap // 2 : tap // 2 + ROWS, tap % 2, :, column * CH : (column + 1) * CH]
                more = nt(lhs.reshape(ROWS * WIN, CH), weights[tap, column])
                part = more if part is None else part + more
        grad_act[frame] = part.reshape(ROWS, WIN, CH).astype(BF16)


def up_grad_kernel(core_ref, act, mine, other, out, table, flipped):
    core = core_ref[0]
    border = jnp.zeros((FR, OWN, 4 * CH), BF16)
    table[:, 0, 0] = border
    table[:, ROWS, 1] = border
    for source, which in ((mine, core), (other, 1 - core)):
        for frame in range(2):
            slot = 2 * which + frame
            for parity in range(2):
                fine = source[:, frame, :, parity].reshape(ROWS, WIN, 2 * CH).astype(F32)
                even, odd = fine[:, :, :CH], fine[:, :, CH:]
                low = 0 if parity == 0 else 1
                put = (slot, slice(low, low + ROWS), 1 - parity)
                for column, (values, shift) in enumerate(((odd, -1), (even, 0), (odd, 0), (even, 1))):
                    moved = pltpu.roll(values, WIN - (EDGE + shift), axis=1)[:, :OWN].astype(BF16)
                    table[put + (slice(None), slice(column * CH, (column + 1) * CH))] = moved
    for frame in range(FR):
        rows = ROWS * OWN
        flipped[:, frame * rows : (frame + 1) * rows] = jnp.transpose(
            own_columns(act[frame]).reshape(rows, CH)
        ).astype(BF16)
    lanes = pl.ds(pl.multiple_of(core * 2 * CH, 2 * CH), 2 * CH)
    for tap in range(4):
        rhs = table[:, tap // 2 : tap // 2 + ROWS, tap % 2, :, lanes]
        result = nn(flipped[...], rhs.reshape(FR * ROWS * OWN, 2 * CH))
        for half in range(2):
            for piece in range(8):
                out[tap * 16 + half * 8 + piece] = result[
                    piece * 32 : (piece + 1) * 32, half * CH : (half + 1) * CH
                ].astype(BF16)


def kernel_grad_kernel(by_core, core_ref, act, block, later, out, table, flipped, sums):
    clear_border(table)
    for frame in range(FR):
        fill_own_table(table, frame, block[frame])
    for frame in range(2):
        fill_own_table(table, FR + frame, later[frame])
    for frame in range(FR):
        rows = ROWS * OWN
        values = act[frame // 2, :, frame % 2] if by_core else act[frame]
        flipped[:, frame * rows : (frame + 1) * rows] = jnp.transpose(
            own_columns(values).reshape(rows, CH)
        ).astype(BF16)
    sums[TAPS * CH :] = jnp.zeros((8, CH), F32)
    for tap_t in range(3):
        for tap_h in range(3):
            rhs = table[2 - tap_t : 2 - tap_t + FR, 2 - tap_h : 2 - tap_h + ROWS]
            result = nn(flipped[...], rhs.reshape(FR * ROWS * OWN, 3 * CH))
            for tap_w in range(3):
                at = (tap_t * 9 + tap_h * 3 + tap_w) * CH
                sums[at : at + CH] = result[:, tap_w * CH : (tap_w + 1) * CH]
    for core in range(2):

        @pl.when(core_ref[0] == core)
        def _(core=core):
            for group in range(4):
                for member in range(16):
                    at = 16 * SHARE * (2 * group + core) + SHARE * member
                    out[group * 16 + member] = sums[at : at + SHARE + 2].astype(BF16)


def whole(shape):
    zeros = (0,) * len(shape)
    return pl.BlockSpec(shape, lambda *_: zeros)


SMEM = pl.BlockSpec(memory_space=pltpu.SMEM)


def tap_weights():
    return pl.BlockSpec((1, 3, 3, CH, CH), lambda step: (step, 0, 0, 0, 0))


def call(kernel, grid, args, specs, outs, scratch, flops):
    shapes = [jax.ShapeDtypeStruct(shape, dtype) for shape, dtype in outs]
    moved = sum(math.prod(a.shape) * a.dtype.itemsize for a in args)
    moved += sum(math.prod(s.shape) * s.dtype.itemsize for s in shapes)
    single = len(shapes) == 1
    return pl.pallas_call(
        kernel,
        out_shape=shapes[0] if single else shapes,
        grid=grid,
        in_specs=specs,
        out_specs=whole(shapes[0].shape) if single else [whole(s.shape) for s in shapes],
        scratch_shapes=scratch,
        compiler_params=pltpu.CompilerParams(vmem_limit_bytes=VMEM_LIMIT),
        cost_estimate=pl.CostEstimate(flops=int(flops), bytes_accessed=moved, transcendentals=0),
    )(*args)


def shift(value, axis, step):
    count = lax.axis_size(axis)
    return lax.ppermute(value, axis, [(i, i + step) for i in range(count) if 0 <= i + step < count])


def shards(features, conv_first, conv_second, up_kernel, cotangent):
    core = lax.axis_index("core")
    height = lax.axis_index("height")
    width = lax.axis_index("width")
    core_arg = core.astype(jnp.int32).reshape(1)
    window = 8 * width + height
    columns = OWN * window - EDGE + jnp.arange(WIN)
    inside = ((columns >= 0) & (columns < 128)).astype(F32)
    mask = jnp.broadcast_to(inside[:, None], (WIN, CH))
    act_shape = (FR, ROWS, WIN, CH)
    table = pltpu.VMEM((FR + 2, ROWS + 2, WIN, 3 * CH), BF16)
    own_table = pltpu.VMEM((FR + 2, ROWS + 2, OWN, 3 * CH), BF16)
    total = pltpu.VMEM((FR * ROWS * WIN, CH), F32)
    tap_flops = 2 * FR * ROWS * WIN * CH * CH

    padded = jnp.pad(features[:, 0], ((0, 0), (EDGE, EDGE), (0, 0))).reshape(2, 17, OWN, CH)
    windows = jnp.concatenate([padded[:, :-1], padded[:, 1:]], axis=2)
    windows = windows.reshape(2, 2, 8, WIN, CH).transpose(2, 1, 0, 3, 4).reshape(1, 16, 2, WIN, CH)
    windows = jnp.broadcast_to(windows, (2, 16, 2, WIN, CH)).reshape(32, 2, WIN, CH)
    block = lax.all_to_all(windows, ("core", "height", "width"), 0, 0, tiled=True)
    block = block.reshape(2, ROWS, 2, WIN, CH)
    halo = shift(block[1], "y", 1)

    paired = cotangent.reshape(2, 4, 64, 2 * CH)
    edge = jnp.where(width == 0, paired[:, :, 64 - EDGE :], paired[:, :, :EDGE])
    edge = lax.ppermute(edge, "width", [(0, 1), (1, 0)])
    nothing = jnp.zeros_like(edge)
    low, high = jnp.where(width == 0, nothing, edge), jnp.where(width == 0, edge, nothing)
    paired = jnp.concatenate([low, paired, high], axis=2).reshape(2, 4, 9, OWN, 2 * CH)
    fine = jnp.concatenate([paired[:, :, :-1], paired[:, :, 1:]], axis=3).transpose(2, 0, 1, 3, 4)
    mine = lax.all_to_all(fine, "height", 0, 0, tiled=True).reshape(8, 2, 2, 2, WIN, 2 * CH)
    other = lax.ppermute(mine, "core", [(0, 1), (1, 0)])

    first_act, first_slope = call(
        first_kernel, (3,), (halo, block, conv_first, mask),
        [whole(halo.shape), whole(block.shape), tap_weights(), whole(mask.shape)],
        [(act_shape, BF16), (act_shape, F32)], [table, total], 27 * tap_flops,
    )
    earlier = shift(first_act[2:], "y", 1)
    grad_act = call(
        cotangent_kernel, (), (core_arg, mine, other, up_kernel),
        [SMEM, whole(mine.shape), whole(mine.shape), whole(up_kernel.shape)],
        [(act_shape, BF16)], [pltpu.VMEM((FR, ROWS + 1, 2, WIN, 4 * CH), BF16)], 16 * tap_flops,
    )
    grad_sum, up_act = call(
        second_kernel, (3,), (earlier, first_act, block, grad_act, conv_second, mask),
        [whole(earlier.shape), whole(act_shape), whole(block.shape), whole(act_shape), tap_weights(), whole(mask.shape)],
        [(act_shape, BF16), (act_shape, BF16)], [table, total], 27 * tap_flops,
    )
    later = shift(grad_sum[:2], "y", -1)
    up_part = call(
        up_grad_kernel, (), (core_arg, up_act, mine, other),
        [SMEM, whole(act_shape), whole(mine.shape), whole(mine.shape)],
        [((64, 32, CH), BF16)],
        [pltpu.VMEM((FR, ROWS + 1, 2, OWN, 4 * CH), BF16), pltpu.VMEM((CH, FR * ROWS * OWN), BF16)], 4 * tap_flops,
    )
    grad_hidden = call(
        hidden_kernel, (3,), (grad_sum, later, first_slope, conv_second, mask),
        [whole(act_shape), whole(later.shape), whole(act_shape), tap_weights(), whole(mask.shape)],
        [(act_shape, BF16)], [table, total], 27 * tap_flops,
    )
    later_hidden = shift(grad_hidden[:2], "y", -1)

    def kernel_grad(act, by_core, grad, after):
        return call(
            functools.partial(kernel_grad_kernel, by_core), (), (core_arg, act, grad, after),
            [SMEM, whole(act.shape), whole(act_shape), whole(after.shape)],
            [((64, SHARE + 2, CH), BF16)],
            [own_table, pltpu.VMEM((CH, FR * ROWS * OWN), BF16), pltpu.VMEM((TAPS * CH + 8, CH), F32)], 14 * tap_flops,
        )

    second_part = kernel_grad(first_act, False, grad_sum, later)
    first_part = kernel_grad(block, True, grad_hidden, later_hidden)
    rows_out = call(
        features_kernel, (3,), (core_arg, grad_hidden, later_hidden, grad_sum, conv_first),
        [SMEM, whole(act_shape), whole(later_hidden.shape), whole(act_shape), tap_weights()],
        [((ROWS, 2, OWN, CH), BF16)], [own_table, pltpu.VMEM((2 * ROWS * OWN, CH), F32)], 7 * tap_flops,
    )

    factor = 1.0 / math.sqrt(32768)

    def share_of(part, rows):
        received = lax.all_to_all(part, ("y", "height", "width"), 0, 0, tiled=True)
        return (jnp.sum(received[:, :rows].astype(F32), axis=0) * factor).reshape(-1)

    up_share = share_of(up_part, 32)
    second_share = share_of(second_part, SHARE)
    first_share = share_of(first_part, SHARE)
    returned = lax.all_to_all(rows_out, ("height", "width"), 0, 0, tiled=True)
    returned = returned.reshape(8, 2, 2, OWN, CH).transpose(2, 1, 0, 3, 4)
    grad_features = returned.reshape(2, 1, 128, CH)
    return (grad_features, first_share, second_share, up_share)


def solution(mesh):
    names = ("y", "core", "height", "width")
    split = Mesh(mesh.devices.reshape(4, 2, 8, 2), names)
    tm = ("y", "core")
    in_specs = (
        P(tm, ("height", "width"), None, None),
        P(),
        P(),
        P(),
        P(tm, "height", "width", None),
    )
    flat = P(names)
    out_specs = (P(tm, ("height", "width"), None, None), flat, flat, flat)
    return jax.shard_map(shards, mesh=split, in_specs=in_specs, out_specs=out_specs, check_vma=False)
```

```python
import functools
import math

import jax
import jax.numpy as jnp
from jax import lax
from jax.experimental import pallas as pl
from jax.experimental.pallas import tpu as pltpu
from jax.sharding import Mesh, PartitionSpec as P

F32 = jnp.float32
BF16 = jnp.bfloat16
VMEM_LIMIT = 48 * 1024 * 1024

FR = 4
ROWS = 16
WIN = 16
OWN = 8
EDGE = 4
CH = 256
TAPS = 27
SHARE = 54


def slope_of(values, sigma):
    return sigma * (1.0 + values * (1.0 - sigma))


def nt(lhs, rhs):
    return lax.dot_general(lhs, rhs, (((1,), (1,)), ((), ())), preferred_element_type=F32)


def nn(lhs, rhs):
    return jnp.dot(lhs, rhs, preferred_element_type=F32)


def fill_table(table, slot, block, forward):
    wide = block.astype(F32)
    before = pltpu.roll(wide, 1, axis=1).astype(BF16)
    after = pltpu.roll(wide, WIN - 1, axis=1).astype(BF16)
    table[slot, 1 : ROWS + 1, :, 0:CH] = before if forward else after
    table[slot, 1 : ROWS + 1, :, CH : 2 * CH] = block
    table[slot, 1 : ROWS + 1, :, 2 * CH : 3 * CH] = after if forward else before


def fill_own_table(table, slot, block):
    wide = block.astype(F32)
    for tap in range(3):
        moved = pltpu.roll(wide, WIN - (EDGE + 1 - tap), axis=1)
        table[slot, 1 : ROWS + 1, :, tap * CH : (tap + 1) * CH] = moved[:, :OWN].astype(BF16)


def clear_border(table):
    frames, _, columns, lanes = table.shape
    border = jnp.zeros((frames, columns, lanes), BF16)
    table[:, 0] = border
    table[:, ROWS + 1] = border


def own_columns(block):
    return pltpu.roll(block.astype(F32), WIN - EDGE, axis=1)[:, :OWN]


def first_kernel(halo, block, weights, mask, act, slope, table, total):
    step = pl.program_id(0)

    @pl.when(step == 0)
    def _():
        clear_border(table)
        for frame in range(2):
            fill_table(table, frame, halo[:, frame], True)
        for frame in range(FR):
            fill_table(table, 2 + frame, block[frame // 2, :, frame % 2], True)
        total[...] = jnp.zeros_like(total)

    for tap in range(3):
        lhs = table[pl.ds(step, FR), tap : tap + ROWS].reshape(FR * ROWS * WIN, 3 * CH)
        total[...] += nn(lhs, weights[0, tap].reshape(3 * CH, CH))

    @pl.when(step == 2)
    def _():
        inside = mask[...]
        for frame in range(FR):
            rows = ROWS * WIN
            values = total[frame * rows : (frame + 1) * rows].reshape(ROWS, WIN, CH)
            sigma = jax.nn.sigmoid(values)
            act[frame] = (values * sigma * inside).astype(BF16)
            slope[frame] = slope_of(values, sigma)


def second_kernel(halo, block, features, weights, summed, up_act, table, total):
    step = pl.program_id(0)

    @pl.when(step == 0)
    def _():
        clear_border(table)
        for frame in range(2):
            fill_table(table, frame, halo[frame], True)
        for frame in range(FR):
            fill_table(table, 2 + frame, block[frame], True)
        total[...] = jnp.zeros_like(total)

    for tap in range(3):
        lhs = table[pl.ds(step, FR), tap : tap + ROWS].reshape(FR * ROWS * WIN, 3 * CH)
        total[...] += nn(lhs, weights[0, tap].reshape(3 * CH, CH))

    @pl.when(step == 2)
    def _():
        for frame in range(FR):
            rows = ROWS * WIN
            values = total[frame * rows : (frame + 1) * rows].reshape(ROWS, WIN, CH)
            values = values + features[frame // 2, :, frame % 2].astype(F32)
            summed[frame] = values
            up_act[frame] = (values * jax.nn.sigmoid(values)).astype(BF16)


def hidden_kernel(block, later, slope, weights, mask, grad_hidden, table, total):
    step = pl.program_id(0)

    @pl.when(step == 0)
    def _():
        clear_border(table)
        for frame in range(FR):
            fill_table(table, frame, block[frame], False)
        for frame in range(2):
            fill_table(table, FR + frame, later[frame], False)
        total[...] = jnp.zeros_like(total)

    for tap in range(3):
        part = None
        for column in range(3):
            lhs = table[pl.ds(2 - step, FR), 2 - tap : 2 - tap + ROWS, :, column * CH : (column + 1) * CH]
            more = nt(lhs.reshape(FR * ROWS * WIN, CH), weights[0, tap, column])
            part = more if part is None else part + more
        total[...] += part

    @pl.when(step == 2)
    def _():
        inside = mask[...]
        for frame in range(FR):
            rows = ROWS * WIN
            values = total[frame * rows : (frame + 1) * rows].reshape(ROWS, WIN, CH)
            grad_hidden[frame] = (values * slope[frame] * inside).astype(BF16)


def features_kernel(core_ref, block, later, grad_sum, weights, grad_features, table, total):
    step = pl.program_id(0)
    core = core_ref[0]

    @pl.when(step == 0)
    def _():
        clear_border(table)
        for frame in range(FR):
            fill_own_table(table, frame, block[frame])
        for frame in range(2):
            fill_own_table(table, FR + frame, later[frame])
        total[...] = jnp.zeros_like(total)

    for tap in range(3):
        part = None
        for column in range(3):
            lhs = table[
                pl.ds(2 * core + 2 - step, 2), 2 - tap : 2 - tap + ROWS, :, column * CH : (column + 1) * CH
            ]
            more = nt(lhs.reshape(2 * ROWS * OWN, CH), weights[0, tap, column])
            part = more if part is None else part + more
        total[...] += part

    @pl.when(step == 2)
    def _():
        for frame in range(2):
            rows = ROWS * OWN
            values = total[frame * rows : (frame + 1) * rows].reshape(ROWS, OWN, CH)
            values = values + own_columns(grad_sum[2 * core + frame])
            grad_features[:, frame] = values.astype(BF16)


def cotangent_kernel(core_ref, mine, other, weights, summed, mask, grad_sum, table):
    core = core_ref[0]
    border = jnp.zeros((FR, WIN, 4 * CH), BF16)
    table[:, 0, 0] = border
    table[:, ROWS, 1] = border
    for source, which in ((mine, core), (other, 1 - core)):
        for frame in range(2):
            slot = 2 * which + frame
            for parity in range(2):
                fine = source[:, frame, :, parity].reshape(ROWS, WIN, 2 * CH)
                even, odd = fine[:, :, :CH], fine[:, :, CH:]
                before = pltpu.roll(odd.astype(F32), 1, axis=1).astype(BF16)
                after = pltpu.roll(even.astype(F32), WIN - 1, axis=1).astype(BF16)
                low = 0 if parity == 0 else 1
                put = (slot, slice(low, low + ROWS), 1 - parity)
                table[put + (slice(None), slice(0, CH))] = before
                table[put + (slice(None), slice(CH, 2 * CH))] = even
                table[put + (slice(None), slice(2 * CH, 3 * CH))] = odd
                table[put + (slice(None), slice(3 * CH, 4 * CH))] = after
    for frame in range(FR):
        part = None
        for tap in range(4):
            for column in range(4):
                lhs = table[frame, tap // 2 : tap // 2 + ROWS, tap % 2, :, column * CH : (column + 1) * CH]
                more = nt(lhs.reshape(ROWS * WIN, CH), weights[tap, column])
                part = more if part is None else part + more
        grad_act = part.reshape(ROWS, WIN, CH).astype(BF16).astype(F32)
        values = summed[frame]
        grad = grad_act * slope_of(values, jax.nn.sigmoid(values)) * mask[...]
        grad_sum[frame] = grad.astype(BF16)


def up_grad_kernel(core_ref, act, mine, other, out, table, flipped):
    core = core_ref[0]
    border = jnp.zeros((FR, OWN, 4 * CH), BF16)
    table[:, 0, 0] = border
    table[:, ROWS, 1] = border
    for source, which in ((mine, core), (other, 1 - core)):
        for frame in range(2):
            slot = 2 * which + frame
            for parity in range(2):
                fine = source[:, frame, :, parity].reshape(ROWS, WIN, 2 * CH).astype(F32)
                even, odd = fine[:, :, :CH], fine[:, :, CH:]
                low = 0 if parity == 0 else 1
                put = (slot, slice(low, low + ROWS), 1 - parity)
                for column, (values, shift) in enumerate(((odd, -1), (even, 0), (odd, 0), (even, 1))):
                    moved = pltpu.roll(values, WIN - (EDGE + shift), axis=1)[:, :OWN].astype(BF16)
                    table[put + (slice(None), slice(column * CH, (column + 1) * CH))] = moved
    for frame in range(FR):
        rows = ROWS * OWN
        flipped[:, frame * rows : (frame + 1) * rows] = jnp.transpose(
            own_columns(act[frame]).reshape(rows, CH)
        ).astype(BF16)
    lanes = pl.ds(pl.multiple_of(core * 2 * CH, 2 * CH), 2 * CH)
    for tap in range(4):
        rhs = table[:, tap // 2 : tap // 2 + ROWS, tap % 2, :, lanes]
        result = nn(flipped[...], rhs.reshape(FR * ROWS * OWN, 2 * CH))
        for half in range(2):
            for piece in range(8):
                out[tap * 16 + half * 8 + piece] = result[
                    piece * 32 : (piece + 1) * 32, half * CH : (half + 1) * CH
                ].astype(BF16)


def kernel_grad_kernel(by_core, core_ref, act, block, later, out, table, flipped, sums):
    clear_border(table)
    for frame in range(FR):
        fill_own_table(table, frame, block[frame])
    for frame in range(2):
        fill_own_table(table, FR + frame, later[frame])
    for frame in range(FR):
        rows = ROWS * OWN
        values = act[frame // 2, :, frame % 2] if by_core else act[frame]
        flipped[:, frame * rows : (frame + 1) * rows] = jnp.transpose(
            own_columns(values).reshape(rows, CH)
        ).astype(BF16)
    sums[TAPS * CH :] = jnp.zeros((8, CH), F32)
    for tap_t in range(3):
        for tap_h in range(3):
            rhs = table[2 - tap_t : 2 - tap_t + FR, 2 - tap_h : 2 - tap_h + ROWS]
            result = nn(flipped[...], rhs.reshape(FR * ROWS * OWN, 3 * CH))
            for tap_w in range(3):
                at = (tap_t * 9 + tap_h * 3 + tap_w) * CH
                sums[at : at + CH] = result[:, tap_w * CH : (tap_w + 1) * CH]
    for core in range(2):

        @pl.when(core_ref[0] == core)
        def _(core=core):
            for group in range(4):
                for member in range(16):
                    at = 16 * SHARE * (2 * group + core) + SHARE * member
                    out[group * 16 + member] = sums[at : at + SHARE + 2].astype(BF16)


def whole(shape):
    zeros = (0,) * len(shape)
    return pl.BlockSpec(shape, lambda *_: zeros)


SMEM = pl.BlockSpec(memory_space=pltpu.SMEM)


def tap_weights():
    return pl.BlockSpec((1, 3, 3, CH, CH), lambda step: (step, 0, 0, 0, 0))


def call(kernel, grid, args, specs, outs, scratch, flops):
    shapes = [jax.ShapeDtypeStruct(shape, dtype) for shape, dtype in outs]
    moved = sum(math.prod(a.shape) * a.dtype.itemsize for a in args)
    moved += sum(math.prod(s.shape) * s.dtype.itemsize for s in shapes)
    single = len(shapes) == 1
    return pl.pallas_call(
        kernel,
        out_shape=shapes[0] if single else shapes,
        grid=grid,
        in_specs=specs,
        out_specs=whole(shapes[0].shape) if single else [whole(s.shape) for s in shapes],
        scratch_shapes=scratch,
        compiler_params=pltpu.CompilerParams(vmem_limit_bytes=VMEM_LIMIT),
        cost_estimate=pl.CostEstimate(flops=int(flops), bytes_accessed=moved, transcendentals=0),
    )(*args)


def shift(value, axis, step):
    count = lax.axis_size(axis)
    return lax.ppermute(value, axis, [(i, i + step) for i in range(count) if 0 <= i + step < count])


def shards(features, conv_first, conv_second, up_kernel, cotangent):
    core = lax.axis_index("core")
    height = lax.axis_index("height")
    width = lax.axis_index("width")
    core_arg = core.astype(jnp.int32).reshape(1)
    window = 8 * width + height
    columns = OWN * window - EDGE + jnp.arange(WIN)
    inside = ((columns >= 0) & (columns < 128)).astype(F32)
    mask = jnp.broadcast_to(inside[:, None], (WIN, CH))
    act_shape = (FR, ROWS, WIN, CH)
    table = pltpu.VMEM((FR + 2, ROWS + 2, WIN, 3 * CH), BF16)
    own_table = pltpu.VMEM((FR + 2, ROWS + 2, OWN, 3 * CH), BF16)
    total = pltpu.VMEM((FR * ROWS * WIN, CH), F32)
    tap_flops = 2 * FR * ROWS * WIN * CH * CH

    padded = jnp.pad(features[:, 0], ((0, 0), (EDGE, EDGE), (0, 0))).reshape(2, 17, OWN, CH)
    windows = jnp.concatenate([padded[:, :-1], padded[:, 1:]], axis=2)
    windows = windows.reshape(2, 2, 8, WIN, CH).transpose(2, 1, 0, 3, 4).reshape(1, 16, 2, WIN, CH)
    windows = jnp.broadcast_to(windows, (2, 16, 2, WIN, CH)).reshape(32, 2, WIN, CH)
    block = lax.all_to_all(windows, ("core", "height", "width"), 0, 0, tiled=True)

    paired = cotangent.reshape(2, 4, 64, 2 * CH)
    edge = jnp.where(width == 0, paired[:, :, 64 - EDGE :], paired[:, :, :EDGE])
    edge = lax.ppermute(edge, "width", [(0, 1), (1, 0)])
    nothing = jnp.zeros_like(edge)
    low, high = jnp.where(width == 0, nothing, edge), jnp.where(width == 0, edge, nothing)
    paired = jnp.concatenate([low, paired, high], axis=2).reshape(2, 4, 9, OWN, 2 * CH)
    fine = jnp.concatenate([paired[:, :, :-1], paired[:, :, 1:]], axis=3).transpose(2, 0, 1, 3, 4)
    fine, block = lax.optimization_barrier((fine, block))
    block = block.reshape(2, ROWS, 2, WIN, CH)
    halo = shift(block[1], "y", 1)
    mine = lax.all_to_all(fine, "height", 0, 0, tiled=True).reshape(8, 2, 2, 2, WIN, 2 * CH)

    first_act, first_slope = call(
        first_kernel, (3,), (halo, block, conv_first, mask),
        [whole(halo.shape), whole(block.shape), tap_weights(), whole(mask.shape)],
        [(act_shape, BF16), (act_shape, F32)], [table, total], 27 * tap_flops,
    )
    mine, first_act = lax.optimization_barrier((mine, first_act))
    earlier = shift(first_act[2:], "y", 1)
    other = lax.ppermute(mine, "core", [(0, 1), (1, 0)])
    summed, up_act = call(
        second_kernel, (3,), (earlier, first_act, block, conv_second),
        [whole(earlier.shape), whole(act_shape), whole(block.shape), tap_weights()],
        [(act_shape, F32), (act_shape, BF16)], [table, total], 27 * tap_flops,
    )
    grad_sum = call(
        cotangent_kernel, (), (core_arg, mine, other, up_kernel, summed, mask),
        [SMEM, whole(mine.shape), whole(mine.shape), whole(up_kernel.shape), whole(act_shape), whole(mask.shape)],
        [(act_shape, BF16)], [pltpu.VMEM((FR, ROWS + 1, 2, WIN, 4 * CH), BF16)], 16 * tap_flops,
    )
    up_act, grad_sum = lax.optimization_barrier((up_act, grad_sum))
    later = shift(grad_sum[:2], "y", -1)
    up_part = call(
        up_grad_kernel, (), (core_arg, up_act, mine, other),
        [SMEM, whole(act_shape), whole(mine.shape), whole(mine.shape)],
        [((64, 32, CH), BF16)],
        [pltpu.VMEM((FR, ROWS + 1, 2, OWN, 4 * CH), BF16), pltpu.VMEM((CH, FR * ROWS * OWN), BF16)], 4 * tap_flops,
    )
    everyone = ("y", "height", "width")
    up_received = lax.all_to_all(up_part, everyone, 0, 0, tiled=True)
    grad_hidden = call(
        hidden_kernel, (3,), (grad_sum, later, first_slope, conv_second, mask),
        [whole(act_shape), whole(later.shape), whole(act_shape), tap_weights(), whole(mask.shape)],
        [(act_shape, BF16)], [table, total], 27 * tap_flops,
    )
    later_hidden = shift(grad_hidden[:2], "y", -1)

    def kernel_grad(act, by_core, grad, after):
        return call(
            functools.partial(kernel_grad_kernel, by_core), (), (core_arg, act, grad, after),
            [SMEM, whole(act.shape), whole(act_shape), whole(after.shape)],
            [((64, SHARE + 2, CH), BF16)],
            [own_table, pltpu.VMEM((CH, FR * ROWS * OWN), BF16), pltpu.VMEM((TAPS * CH + 8, CH), F32)], 14 * tap_flops,
        )

    second_part = kernel_grad(first_act, False, grad_sum, later)
    second_part, up_received = lax.optimization_barrier((second_part, up_received))
    second_received = lax.all_to_all(second_part, everyone, 0, 0, tiled=True)
    rows_out = call(
        features_kernel, (3,), (core_arg, grad_hidden, later_hidden, grad_sum, conv_first),
        [SMEM, whole(act_shape), whole(later_hidden.shape), whole(act_shape), tap_weights()],
        [((ROWS, 2, OWN, CH), BF16)], [own_table, pltpu.VMEM((2 * ROWS * OWN, CH), F32)], 7 * tap_flops,
    )
    first_part = kernel_grad(block, True, grad_hidden, later_hidden)
    first_part, rows_out, second_received = lax.optimization_barrier((first_part, rows_out, second_received))
    first_received = lax.all_to_all(first_part, everyone, 0, 0, tiled=True)
    rows_out, first_received = lax.optimization_barrier((rows_out, first_received))
    returned = lax.all_to_all(rows_out, ("height", "width"), 0, 0, tiled=True)
    returned = returned.reshape(8, 2, 2, OWN, CH).transpose(2, 1, 0, 3, 4)
    grad_features = returned.reshape(2, 1, 128, CH)

    factor = 1.0 / math.sqrt(32768)

    def share_of(received, rows):
        return (jnp.sum(received[:, :rows].astype(F32), axis=0) * factor).reshape(-1)

    return (
        grad_features,
        share_of(first_received, SHARE),
        share_of(second_received, SHARE),
        share_of(up_received, 32),
    )


def solution(mesh):
    names = ("y", "core", "height", "width")
    split = Mesh(mesh.devices.reshape(4, 2, 8, 2), names)
    tm = ("y", "core")
    in_specs = (
        P(tm, ("height", "width"), None, None),
        P(),
        P(),
        P(),
        P(tm, "height", "width", None),
    )
    flat = P(names)
    out_specs = (P(tm, ("height", "width"), None, None), flat, flat, flat)
    return jax.shard_map(shards, mesh=split, in_specs=in_specs, out_specs=out_specs, check_vma=False)
```

```python
import math

import jax
import jax.numpy as jnp
from jax import lax
from jax.experimental import pallas as pl
from jax.experimental.pallas import tpu as pltpu
from jax.sharding import Mesh, PartitionSpec as P

F32 = jnp.float32
BF16 = jnp.bfloat16
VMEM_LIMIT = 48 * 1024 * 1024

FR = 4
ROWS = 16
WIN = 16
OWN = 8
EDGE = 4
CH = 256
TAPS = 27
SHARE = 54
PIECE = 56
UP_ROWS = 32
GRAD_ROWS = UP_ROWS + 2 * OWN
SENT_ROWS = GRAD_ROWS + 2 * PIECE


def slope_of(values, sigma):
    return sigma * (1.0 + values * (1.0 - sigma))


def nt(lhs, rhs):
    return lax.dot_general(lhs, rhs, (((1,), (1,)), ((), ())), preferred_element_type=F32)


def nn(lhs, rhs):
    return jnp.dot(lhs, rhs, preferred_element_type=F32)


def fill_table(table, slot, block, forward):
    wide = block.astype(F32)
    before = pltpu.roll(wide, 1, axis=1).astype(BF16)
    after = pltpu.roll(wide, WIN - 1, axis=1).astype(BF16)
    table[slot, 1 : ROWS + 1, :, 0:CH] = before if forward else after
    table[slot, 1 : ROWS + 1, :, CH : 2 * CH] = block
    table[slot, 1 : ROWS + 1, :, 2 * CH : 3 * CH] = after if forward else before


def fill_own_table(table, slot, block):
    wide = block.astype(F32)
    for tap in range(3):
        moved = pltpu.roll(wide, WIN - (EDGE + 1 - tap), axis=1)
        table[slot, 1 : ROWS + 1, :, tap * CH : (tap + 1) * CH] = moved[:, :OWN].astype(BF16)


def clear_border(table):
    frames, _, columns, lanes = table.shape
    border = jnp.zeros((frames, columns, lanes), BF16)
    table[:, 0] = border
    table[:, ROWS + 1] = border


def own_columns(block):
    return pltpu.roll(block.astype(F32), WIN - EDGE, axis=1)[:, :OWN]


def first_kernel(halo, block, weights, mask, act, slope, table, total):
    step = pl.program_id(0)

    @pl.when(step == 0)
    def _():
        clear_border(table)
        for frame in range(2):
            fill_table(table, frame, halo[:, frame], True)
        for frame in range(FR):
            fill_table(table, 2 + frame, block[frame // 2, :, frame % 2], True)
        total[...] = jnp.zeros_like(total)

    for tap in range(3):
        lhs = table[pl.ds(step, FR), tap : tap + ROWS].reshape(FR * ROWS * WIN, 3 * CH)
        total[...] += nn(lhs, weights[0, tap].reshape(3 * CH, CH))

    @pl.when(step == 2)
    def _():
        inside = mask[...]
        for frame in range(FR):
            rows = ROWS * WIN
            values = total[frame * rows : (frame + 1) * rows].reshape(ROWS, WIN, CH)
            sigma = jax.nn.sigmoid(values)
            act[frame] = (values * sigma * inside).astype(BF16)
            slope[frame] = slope_of(values, sigma)


def second_kernel(halo, block, features, weights, summed, up_act, table, total):
    step = pl.program_id(0)

    @pl.when(step == 0)
    def _():
        clear_border(table)
        for frame in range(2):
            fill_table(table, frame, halo[frame], True)
        for frame in range(FR):
            fill_table(table, 2 + frame, block[frame], True)
        total[...] = jnp.zeros_like(total)

    for tap in range(3):
        lhs = table[pl.ds(step, FR), tap : tap + ROWS].reshape(FR * ROWS * WIN, 3 * CH)
        total[...] += nn(lhs, weights[0, tap].reshape(3 * CH, CH))

    @pl.when(step == 2)
    def _():
        for frame in range(FR):
            rows = ROWS * WIN
            values = total[frame * rows : (frame + 1) * rows].reshape(ROWS, WIN, CH)
            values = values + features[frame // 2, :, frame % 2].astype(F32)
            summed[frame] = values
            up_act[frame] = (values * jax.nn.sigmoid(values)).astype(BF16)


def hidden_kernel(block, later, slope, weights, mask, grad_hidden, table, total):
    step = pl.program_id(0)

    @pl.when(step == 0)
    def _():
        clear_border(table)
        for frame in range(FR):
            fill_table(table, frame, block[frame], False)
        for frame in range(2):
            fill_table(table, FR + frame, later[frame], False)
        total[...] = jnp.zeros_like(total)

    for tap in range(3):
        part = None
        for column in range(3):
            lhs = table[pl.ds(2 - step, FR), 2 - tap : 2 - tap + ROWS, :, column * CH : (column + 1) * CH]
            more = nt(lhs.reshape(FR * ROWS * WIN, CH), weights[0, tap, column])
            part = more if part is None else part + more
        total[...] += part

    @pl.when(step == 2)
    def _():
        inside = mask[...]
        for frame in range(FR):
            rows = ROWS * WIN
            values = total[frame * rows : (frame + 1) * rows].reshape(ROWS, WIN, CH)
            grad_hidden[frame] = (values * slope[frame] * inside).astype(BF16)


def features_kernel(core_ref, block, later, grad_sum, weights, grad_features, table, total):
    step = pl.program_id(0)
    core = core_ref[0]

    @pl.when(step == 0)
    def _():
        clear_border(table)
        for frame in range(FR):
            fill_own_table(table, frame, block[frame])
        for frame in range(2):
            fill_own_table(table, FR + frame, later[frame])
        total[...] = jnp.zeros_like(total)

    for tap in range(3):
        part = None
        for column in range(3):
            lhs = table[
                pl.ds(2 * core + 2 - step, 2), 2 - tap : 2 - tap + ROWS, :, column * CH : (column + 1) * CH
            ]
            more = nt(lhs.reshape(2 * ROWS * OWN, CH), weights[0, tap, column])
            part = more if part is None else part + more
        total[...] += part

    @pl.when(step == 2)
    def _():
        for frame in range(2):
            rows = ROWS * OWN
            values = total[frame * rows : (frame + 1) * rows].reshape(ROWS, OWN, CH)
            values = values + own_columns(grad_sum[2 * core + frame])
            grad_features[:, frame] = values.astype(BF16)


def cotangent_kernel(core_ref, mine, other, weights, summed, mask, grad_sum, table):
    core = core_ref[0]
    border = jnp.zeros((FR, WIN, 4 * CH), BF16)
    table[:, 0, 0] = border
    table[:, ROWS, 1] = border
    for source, which in ((mine, core), (other, 1 - core)):
        for frame in range(2):
            slot = 2 * which + frame
            for parity in range(2):
                fine = source[:, frame, :, parity].reshape(ROWS, WIN, 2 * CH)
                even, odd = fine[:, :, :CH], fine[:, :, CH:]
                before = pltpu.roll(odd.astype(F32), 1, axis=1).astype(BF16)
                after = pltpu.roll(even.astype(F32), WIN - 1, axis=1).astype(BF16)
                low = 0 if parity == 0 else 1
                put = (slot, slice(low, low + ROWS), 1 - parity)
                table[put + (slice(None), slice(0, CH))] = before
                table[put + (slice(None), slice(CH, 2 * CH))] = even
                table[put + (slice(None), slice(2 * CH, 3 * CH))] = odd
                table[put + (slice(None), slice(3 * CH, 4 * CH))] = after
    for frame in range(FR):
        part = None
        for tap in range(4):
            for column in range(4):
                lhs = table[frame, tap // 2 : tap // 2 + ROWS, tap % 2, :, column * CH : (column + 1) * CH]
                more = nt(lhs.reshape(ROWS * WIN, CH), weights[tap, column])
                part = more if part is None else part + more
        grad_act = part.reshape(ROWS, WIN, CH).astype(BF16).astype(F32)
        values = summed[frame]
        grad = grad_act * slope_of(values, jax.nn.sigmoid(values)) * mask[...]
        grad_sum[frame] = grad.astype(BF16)


def up_grad_kernel(core_ref, act, mine, other, out, table, flipped):
    core = core_ref[0]
    border = jnp.zeros((FR, OWN, 4 * CH), BF16)
    table[:, 0, 0] = border
    table[:, ROWS, 1] = border
    for source, which in ((mine, core), (other, 1 - core)):
        for frame in range(2):
            slot = 2 * which + frame
            for parity in range(2):
                fine = source[:, frame, :, parity].reshape(ROWS, WIN, 2 * CH).astype(F32)
                even, odd = fine[:, :, :CH], fine[:, :, CH:]
                low = 0 if parity == 0 else 1
                put = (slot, slice(low, low + ROWS), 1 - parity)
                for column, (values, shift) in enumerate(((odd, -1), (even, 0), (odd, 0), (even, 1))):
                    moved = pltpu.roll(values, WIN - (EDGE + shift), axis=1)[:, :OWN].astype(BF16)
                    table[put + (slice(None), slice(column * CH, (column + 1) * CH))] = moved
    for frame in range(FR):
        rows = ROWS * OWN
        flipped[:, frame * rows : (frame + 1) * rows] = jnp.transpose(
            own_columns(act[frame]).reshape(rows, CH)
        ).astype(BF16)
    lanes = pl.ds(pl.multiple_of(core * 2 * CH, 2 * CH), 2 * CH)
    for tap in range(4):
        rhs = table[:, tap // 2 : tap // 2 + ROWS, tap % 2, :, lanes]
        result = nn(flipped[...], rhs.reshape(FR * ROWS * OWN, 2 * CH))
        for half in range(2):
            for piece in range(8):
                out[tap * 16 + half * 8 + piece] = result[
                    piece * 32 : (piece + 1) * 32, half * CH : (half + 1) * CH
                ].astype(BF16)


def tap_sums(act_of, block, later, table, flipped, sums):
    clear_border(table)
    for frame in range(FR):
        fill_own_table(table, frame, block[frame])
    for frame in range(2):
        fill_own_table(table, FR + frame, later[frame])
    for frame in range(FR):
        rows = ROWS * OWN
        flipped[:, frame * rows : (frame + 1) * rows] = jnp.transpose(
            own_columns(act_of(frame)).reshape(rows, CH)
        ).astype(BF16)
    sums[TAPS * CH :] = jnp.zeros((8, CH), F32)
    for tap_t in range(3):
        for tap_h in range(3):
            rhs = table[2 - tap_t : 2 - tap_t + FR, 2 - tap_h : 2 - tap_h + ROWS]
            result = nn(flipped[...], rhs.reshape(FR * ROWS * OWN, 3 * CH))
            for tap_w in range(3):
                at = (tap_t * 9 + tap_h * 3 + tap_w) * CH
                sums[at : at + CH] = result[:, tap_w * CH : (tap_w + 1) * CH]


def second_grad_kernel(place, act, block, later, out, table, flipped, sums):
    tap_sums(lambda frame: act[frame], block, later, table, flipped, sums)
    for core in range(2):

        @pl.when(place[0] == core)
        def _(core=core):
            for group in range(4):
                for member in range(16):
                    at = 16 * SHARE * (2 * group + core) + SHARE * member
                    out[group * 16 + member] = sums[at : at + PIECE].astype(BF16)


def first_grad_kernel(place, act, block, later, second, up, rows_out, out, table, flipped, sums):
    tap_sums(lambda frame: act[frame // 2, :, frame % 2], block, later, table, flipped, sums)
    for group in range(4):
        here = (place[1] == group).astype(F32)
        for member in range(16):
            chunk = group * 16 + member
            out[chunk, :UP_ROWS] = up[chunk]
            rows = rows_out[member].astype(F32) * here
            out[chunk, UP_ROWS:GRAD_ROWS] = rows.reshape(2 * OWN, CH).astype(BF16)
    for core in range(2):

        @pl.when(place[0] == core)
        def _(core=core):
            for group in range(4):
                for member in range(16):
                    chunk = group * 16 + member
                    at = 16 * SHARE * (2 * group + core) + SHARE * member
                    both = jnp.concatenate([second[chunk].astype(F32), sums[at : at + PIECE]], axis=0)
                    out[chunk, GRAD_ROWS:] = both.astype(BF16)


def whole(shape):
    zeros = (0,) * len(shape)
    return pl.BlockSpec(shape, lambda *_: zeros)


SMEM = pl.BlockSpec(memory_space=pltpu.SMEM)


def tap_weights():
    return pl.BlockSpec((1, 3, 3, CH, CH), lambda step: (step, 0, 0, 0, 0))


def call(kernel, grid, args, specs, outs, scratch, flops):
    shapes = [jax.ShapeDtypeStruct(shape, dtype) for shape, dtype in outs]
    moved = sum(math.prod(a.shape) * a.dtype.itemsize for a in args)
    moved += sum(math.prod(s.shape) * s.dtype.itemsize for s in shapes)
    single = len(shapes) == 1
    return pl.pallas_call(
        kernel,
        out_shape=shapes[0] if single else shapes,
        grid=grid,
        in_specs=specs,
        out_specs=whole(shapes[0].shape) if single else [whole(s.shape) for s in shapes],
        scratch_shapes=scratch,
        compiler_params=pltpu.CompilerParams(vmem_limit_bytes=VMEM_LIMIT),
        cost_estimate=pl.CostEstimate(flops=int(flops), bytes_accessed=moved, transcendentals=0),
    )(*args)


def shift(value, axis, step):
    count = lax.axis_size(axis)
    return lax.ppermute(value, axis, [(i, i + step) for i in range(count) if 0 <= i + step < count])


def shards(features, conv_first, conv_second, up_kernel, cotangent):
    core = lax.axis_index("core")
    height = lax.axis_index("height")
    width = lax.axis_index("width")
    core_arg = core.astype(jnp.int32).reshape(1)
    place = jnp.stack([core, lax.axis_index("y")]).astype(jnp.int32)
    window = 8 * width + height
    columns = OWN * window - EDGE + jnp.arange(WIN)
    inside = ((columns >= 0) & (columns < 128)).astype(F32)
    mask = jnp.broadcast_to(inside[:, None], (WIN, CH))
    act_shape = (FR, ROWS, WIN, CH)
    table = pltpu.VMEM((FR + 2, ROWS + 2, WIN, 3 * CH), BF16)
    own_table = pltpu.VMEM((FR + 2, ROWS + 2, OWN, 3 * CH), BF16)
    total = pltpu.VMEM((FR * ROWS * WIN, CH), F32)
    tap_flops = 2 * FR * ROWS * WIN * CH * CH

    padded = jnp.pad(features[:, 0], ((0, 0), (EDGE, EDGE), (0, 0))).reshape(2, 17, OWN, CH)
    windows = jnp.concatenate([padded[:, :-1], padded[:, 1:]], axis=2)
    windows = windows.reshape(2, 2, 8, WIN, CH).transpose(2, 1, 0, 3, 4).reshape(1, 16, 2, WIN, CH)
    windows = jnp.broadcast_to(windows, (2, 16, 2, WIN, CH)).reshape(32, 2, WIN, CH)
    block = lax.all_to_all(windows, ("core", "height", "width"), 0, 0, tiled=True)

    paired = cotangent.reshape(2, 4, 64, 2 * CH)
    edge = jnp.where(width == 0, paired[:, :, 64 - EDGE :], paired[:, :, :EDGE])
    edge = lax.ppermute(edge, "width", [(0, 1), (1, 0)])
    nothing = jnp.zeros_like(edge)
    low, high = jnp.where(width == 0, nothing, edge), jnp.where(width == 0, edge, nothing)
    paired = jnp.concatenate([low, paired, high], axis=2).reshape(2, 4, 9, OWN, 2 * CH)
    fine = jnp.concatenate([paired[:, :, :-1], paired[:, :, 1:]], axis=3).transpose(2, 0, 1, 3, 4)
    fine, block = lax.optimization_barrier((fine, block))
    block = block.reshape(2, ROWS, 2, WIN, CH)
    halo = shift(block[1], "y", 1)
    mine = lax.all_to_all(fine, "height", 0, 0, tiled=True).reshape(8, 2, 2, 2, WIN, 2 * CH)

    first_act, first_slope = call(
        first_kernel, (3,), (halo, block, conv_first, mask),
        [whole(halo.shape), whole(block.shape), tap_weights(), whole(mask.shape)],
        [(act_shape, BF16), (act_shape, F32)], [table, total], 27 * tap_flops,
    )
    mine, first_act = lax.optimization_barrier((mine, first_act))
    earlier = shift(first_act[2:], "y", 1)
    other = lax.ppermute(mine, "core", [(0, 1), (1, 0)])
    summed, up_act = call(
        second_kernel, (3,), (earlier, first_act, block, conv_second),
        [whole(earlier.shape), whole(act_shape), whole(block.shape), tap_weights()],
        [(act_shape, F32), (act_shape, BF16)], [table, total], 27 * tap_flops,
    )
    grad_sum = call(
        cotangent_kernel, (), (core_arg, mine, other, up_kernel, summed, mask),
        [SMEM, whole(mine.shape), whole(mine.shape), whole(up_kernel.shape), whole(act_shape), whole(mask.shape)],
        [(act_shape, BF16)], [pltpu.VMEM((FR, ROWS + 1, 2, WIN, 4 * CH), BF16)], 16 * tap_flops,
    )
    up_act, grad_sum = lax.optimization_barrier((up_act, grad_sum))
    later = shift(grad_sum[:2], "y", -1)
    up_part = call(
        up_grad_kernel, (), (core_arg, up_act, mine, other),
        [SMEM, whole(act_shape), whole(mine.shape), whole(mine.shape)],
        [((64, 32, CH), BF16)],
        [pltpu.VMEM((FR, ROWS + 1, 2, OWN, 4 * CH), BF16), pltpu.VMEM((CH, FR * ROWS * OWN), BF16)], 4 * tap_flops,
    )
    grad_hidden = call(
        hidden_kernel, (3,), (grad_sum, later, first_slope, conv_second, mask),
        [whole(act_shape), whole(later.shape), whole(act_shape), tap_weights(), whole(mask.shape)],
        [(act_shape, BF16)], [table, total], 27 * tap_flops,
    )
    later_hidden = shift(grad_hidden[:2], "y", -1)

    grad_scratch = [own_table, pltpu.VMEM((CH, FR * ROWS * OWN), BF16), pltpu.VMEM((TAPS * CH + 8, CH), F32)]
    tied_act, grad_hidden = lax.optimization_barrier((first_act, grad_hidden))
    second_part = call(
        second_grad_kernel, (), (place, tied_act, grad_sum, later),
        [SMEM, whole(act_shape), whole(act_shape), whole(later.shape)],
        [((64, PIECE, CH), BF16)], grad_scratch, 14 * tap_flops,
    )
    rows_out = call(
        features_kernel, (3,), (core_arg, grad_hidden, later_hidden, grad_sum, conv_first),
        [SMEM, whole(act_shape), whole(later_hidden.shape), whole(act_shape), tap_weights()],
        [((ROWS, 2, OWN, CH), BF16)], [own_table, pltpu.VMEM((2 * ROWS * OWN, CH), F32)], 7 * tap_flops,
    )
    parts = call(
        first_grad_kernel, (), (place, block, grad_hidden, later_hidden, second_part, up_part, rows_out),
        [SMEM, whole(block.shape), whole(act_shape), whole(later_hidden.shape), whole(second_part.shape),
         whole(up_part.shape), whole(rows_out.shape)],
        [((64, SENT_ROWS, CH), BF16)], grad_scratch, 14 * tap_flops,
    )
    received = lax.all_to_all(parts, ("y", "height", "width"), 0, 0, tiled=True)
    returned = lax.dynamic_slice_in_dim(received, 16 * lax.axis_index("y"), 16, 0)[:, UP_ROWS:GRAD_ROWS]
    returned = returned.reshape(8, 2, 2, OWN, CH).transpose(2, 1, 0, 3, 4)
    grad_features = returned.reshape(2, 1, 128, CH)
    factor = 1.0 / math.sqrt(32768)
    summed_parts = jnp.sum(received.astype(F32), axis=0) * factor
    up_share = summed_parts[:UP_ROWS].reshape(-1)
    second_share = summed_parts[GRAD_ROWS : GRAD_ROWS + SHARE].reshape(-1)
    first_share = summed_parts[GRAD_ROWS + PIECE : GRAD_ROWS + PIECE + SHARE].reshape(-1)
    return (grad_features, first_share, second_share, up_share)


def solution(mesh):
    names = ("y", "core", "height", "width")
    split = Mesh(mesh.devices.reshape(4, 2, 8, 2), names)
    tm = ("y", "core")
    in_specs = (
        P(tm, ("height", "width"), None, None),
        P(),
        P(),
        P(),
        P(tm, "height", "width", None),
    )
    flat = P(names)
    out_specs = (P(tm, ("height", "width"), None, None), flat, flat, flat)
    return jax.shard_map(shards, mesh=split, in_specs=in_specs, out_specs=out_specs, check_vma=False)
```

```python
import functools
import math

import jax
import jax.numpy as jnp
from jax import lax
from jax.experimental import pallas as pl
from jax.experimental.pallas import tpu as pltpu
from jax.sharding import Mesh, PartitionSpec as P

F32 = jnp.float32
BF16 = jnp.bfloat16
VMEM_LIMIT = 48 * 1024 * 1024

FR = 4
ROWS = 16
WIN = 16
OWN = 8
EDGE = 4
CH = 256
TAPS = 27
SHARE = 54
PIECE = 56
UP_ROWS = 32
GRAD_ROWS = UP_ROWS + 2 * OWN


def slope_of(values, sigma):
    return sigma * (1.0 + values * (1.0 - sigma))


def nt(lhs, rhs):
    return lax.dot_general(lhs, rhs, (((1,), (1,)), ((), ())), preferred_element_type=F32)


def nn(lhs, rhs):
    return jnp.dot(lhs, rhs, preferred_element_type=F32)


def fill_table(table, slot, block, forward):
    wide = block.astype(F32)
    before = pltpu.roll(wide, 1, axis=1).astype(BF16)
    after = pltpu.roll(wide, WIN - 1, axis=1).astype(BF16)
    table[slot, 1 : ROWS + 1, :, 0:CH] = before if forward else after
    table[slot, 1 : ROWS + 1, :, CH : 2 * CH] = block
    table[slot, 1 : ROWS + 1, :, 2 * CH : 3 * CH] = after if forward else before


def fill_own_table(table, slot, block):
    wide = block.astype(F32)
    for tap in range(3):
        moved = pltpu.roll(wide, WIN - (EDGE + 1 - tap), axis=1)
        table[slot, 1 : ROWS + 1, :, tap * CH : (tap + 1) * CH] = moved[:, :OWN].astype(BF16)


def clear_border(table):
    frames, _, columns, lanes = table.shape
    border = jnp.zeros((frames, columns, lanes), BF16)
    table[:, 0] = border
    table[:, ROWS + 1] = border


def own_columns(block):
    return pltpu.roll(block.astype(F32), WIN - EDGE, axis=1)[:, :OWN]


def first_kernel(halo, block, weights, mask, act, slope, table, total):
    step = pl.program_id(0)

    @pl.when(step == 0)
    def _():
        clear_border(table)
        for frame in range(2):
            fill_table(table, frame, halo[:, frame], True)
        for frame in range(FR):
            fill_table(table, 2 + frame, block[frame // 2, :, frame % 2], True)
        total[...] = jnp.zeros_like(total)

    for tap in range(3):
        lhs = table[pl.ds(step, FR), tap : tap + ROWS].reshape(FR * ROWS * WIN, 3 * CH)
        total[...] += nn(lhs, weights[0, tap].reshape(3 * CH, CH))

    @pl.when(step == 2)
    def _():
        inside = mask[...]
        for frame in range(FR):
            rows = ROWS * WIN
            values = total[frame * rows : (frame + 1) * rows].reshape(ROWS, WIN, CH)
            sigma = jax.nn.sigmoid(values)
            act[frame] = (values * sigma * inside).astype(BF16)
            slope[frame] = slope_of(values, sigma)


def second_kernel(halo, block, features, weights, summed, up_act, table, total):
    step = pl.program_id(0)

    @pl.when(step == 0)
    def _():
        clear_border(table)
        for frame in range(2):
            fill_table(table, frame, halo[frame], True)
        for frame in range(FR):
            fill_table(table, 2 + frame, block[frame], True)
        total[...] = jnp.zeros_like(total)

    for tap in range(3):
        lhs = table[pl.ds(step, FR), tap : tap + ROWS].reshape(FR * ROWS * WIN, 3 * CH)
        total[...] += nn(lhs, weights[0, tap].reshape(3 * CH, CH))

    @pl.when(step == 2)
    def _():
        for frame in range(FR):
            rows = ROWS * WIN
            values = total[frame * rows : (frame + 1) * rows].reshape(ROWS, WIN, CH)
            values = values + features[frame // 2, :, frame % 2].astype(F32)
            summed[frame] = values
            up_act[frame] = (values * jax.nn.sigmoid(values)).astype(BF16)


def hidden_kernel(block, later, slope, weights, mask, grad_hidden, table, total):
    step = pl.program_id(0)

    @pl.when(step == 0)
    def _():
        clear_border(table)
        for frame in range(FR):
            fill_table(table, frame, block[frame], False)
        for frame in range(2):
            fill_table(table, FR + frame, later[frame], False)
        total[...] = jnp.zeros_like(total)

    for tap in range(3):
        part = None
        for column in range(3):
            lhs = table[pl.ds(2 - step, FR), 2 - tap : 2 - tap + ROWS, :, column * CH : (column + 1) * CH]
            more = nt(lhs.reshape(FR * ROWS * WIN, CH), weights[0, tap, column])
            part = more if part is None else part + more
        total[...] += part

    @pl.when(step == 2)
    def _():
        inside = mask[...]
        for frame in range(FR):
            rows = ROWS * WIN
            values = total[frame * rows : (frame + 1) * rows].reshape(ROWS, WIN, CH)
            grad_hidden[frame] = (values * slope[frame] * inside).astype(BF16)


def features_kernel(core_ref, block, later, grad_sum, weights, grad_features, table, total):
    step = pl.program_id(0)
    core = core_ref[0]

    @pl.when(step == 0)
    def _():
        clear_border(table)
        for frame in range(FR):
            fill_own_table(table, frame, block[frame])
        for frame in range(2):
            fill_own_table(table, FR + frame, later[frame])
        total[...] = jnp.zeros_like(total)

    for tap in range(3):
        part = None
        for column in range(3):
            lhs = table[
                pl.ds(2 * core + 2 - step, 2), 2 - tap : 2 - tap + ROWS, :, column * CH : (column + 1) * CH
            ]
            more = nt(lhs.reshape(2 * ROWS * OWN, CH), weights[0, tap, column])
            part = more if part is None else part + more
        total[...] += part

    @pl.when(step == 2)
    def _():
        for frame in range(2):
            rows = ROWS * OWN
            values = total[frame * rows : (frame + 1) * rows].reshape(ROWS, OWN, CH)
            values = values + own_columns(grad_sum[2 * core + frame])
            grad_features[:, frame] = values.astype(BF16)


def cotangent_kernel(core_ref, mine, other, weights, summed, mask, grad_sum, table):
    core = core_ref[0]
    border = jnp.zeros((FR, WIN, 4 * CH), BF16)
    table[:, 0, 0] = border
    table[:, ROWS, 1] = border
    for source, which in ((mine, core), (other, 1 - core)):
        for frame in range(2):
            slot = 2 * which + frame
            for parity in range(2):
                fine = source[:, frame, :, parity].reshape(ROWS, WIN, 2 * CH)
                even, odd = fine[:, :, :CH], fine[:, :, CH:]
                before = pltpu.roll(odd.astype(F32), 1, axis=1).astype(BF16)
                after = pltpu.roll(even.astype(F32), WIN - 1, axis=1).astype(BF16)
                low = 0 if parity == 0 else 1
                put = (slot, slice(low, low + ROWS), 1 - parity)
                table[put + (slice(None), slice(0, CH))] = before
                table[put + (slice(None), slice(CH, 2 * CH))] = even
                table[put + (slice(None), slice(2 * CH, 3 * CH))] = odd
                table[put + (slice(None), slice(3 * CH, 4 * CH))] = after
    for frame in range(FR):
        part = None
        for tap in range(4):
            for column in range(4):
                lhs = table[frame, tap // 2 : tap // 2 + ROWS, tap % 2, :, column * CH : (column + 1) * CH]
                more = nt(lhs.reshape(ROWS * WIN, CH), weights[tap, column])
                part = more if part is None else part + more
        grad_act = part.reshape(ROWS, WIN, CH).astype(BF16).astype(F32)
        values = summed[frame]
        grad = grad_act * slope_of(values, jax.nn.sigmoid(values)) * mask[...]
        grad_sum[frame] = grad.astype(BF16)


def up_grad_kernel(core_ref, act, mine, other, out, table, flipped):
    core = core_ref[0]
    border = jnp.zeros((FR, OWN, 4 * CH), BF16)
    table[:, 0, 0] = border
    table[:, ROWS, 1] = border
    for source, which in ((mine, core), (other, 1 - core)):
        for frame in range(2):
            slot = 2 * which + frame
            for parity in range(2):
                fine = source[:, frame, :, parity].reshape(ROWS, WIN, 2 * CH).astype(F32)
                even, odd = fine[:, :, :CH], fine[:, :, CH:]
                low = 0 if parity == 0 else 1
                put = (slot, slice(low, low + ROWS), 1 - parity)
                for column, (values, shift) in enumerate(((odd, -1), (even, 0), (odd, 0), (even, 1))):
                    moved = pltpu.roll(values, WIN - (EDGE + shift), axis=1)[:, :OWN].astype(BF16)
                    table[put + (slice(None), slice(column * CH, (column + 1) * CH))] = moved
    for frame in range(FR):
        rows = ROWS * OWN
        flipped[:, frame * rows : (frame + 1) * rows] = jnp.transpose(
            own_columns(act[frame]).reshape(rows, CH)
        ).astype(BF16)
    lanes = pl.ds(pl.multiple_of(core * 2 * CH, 2 * CH), 2 * CH)
    for tap in range(4):
        rhs = table[:, tap // 2 : tap // 2 + ROWS, tap % 2, :, lanes]
        result = nn(flipped[...], rhs.reshape(FR * ROWS * OWN, 2 * CH))
        for half in range(2):
            for piece in range(8):
                out[tap * 16 + half * 8 + piece] = result[
                    piece * 32 : (piece + 1) * 32, half * CH : (half + 1) * CH
                ].astype(BF16)


def tap_sums(act_of, block, later, table, flipped, sums):
    clear_border(table)
    for frame in range(FR):
        fill_own_table(table, frame, block[frame])
    for frame in range(2):
        fill_own_table(table, FR + frame, later[frame])
    for frame in range(FR):
        rows = ROWS * OWN
        flipped[:, frame * rows : (frame + 1) * rows] = jnp.transpose(
            own_columns(act_of(frame)).reshape(rows, CH)
        ).astype(BF16)
    sums[TAPS * CH :] = jnp.zeros((8, CH), F32)
    for tap_t in range(3):
        for tap_h in range(3):
            rhs = table[2 - tap_t : 2 - tap_t + FR, 2 - tap_h : 2 - tap_h + ROWS]
            result = nn(flipped[...], rhs.reshape(FR * ROWS * OWN, 3 * CH))
            for tap_w in range(3):
                at = (tap_t * 9 + tap_h * 3 + tap_w) * CH
                sums[at : at + CH] = result[:, tap_w * CH : (tap_w + 1) * CH]


def kernel_grad_kernel(by_core, place, act, block, later, out, table, flipped, sums):
    def act_of(frame):
        return act[frame // 2, :, frame % 2] if by_core else act[frame]

    tap_sums(act_of, block, later, table, flipped, sums)
    for core in range(2):

        @pl.when(place[0] == core)
        def _(core=core):
            for group in range(4):
                for member in range(16):
                    at = 16 * SHARE * (2 * group + core) + SHARE * member
                    out[group * 16 + member] = sums[at : at + PIECE].astype(BF16)


def whole(shape):
    zeros = (0,) * len(shape)
    return pl.BlockSpec(shape, lambda *_: zeros)


SMEM = pl.BlockSpec(memory_space=pltpu.SMEM)


def tap_weights():
    return pl.BlockSpec((1, 3, 3, CH, CH), lambda step: (step, 0, 0, 0, 0))


def call(kernel, grid, args, specs, outs, scratch, flops):
    shapes = [jax.ShapeDtypeStruct(shape, dtype) for shape, dtype in outs]
    moved = sum(math.prod(a.shape) * a.dtype.itemsize for a in args)
    moved += sum(math.prod(s.shape) * s.dtype.itemsize for s in shapes)
    single = len(shapes) == 1
    return pl.pallas_call(
        kernel,
        out_shape=shapes[0] if single else shapes,
        grid=grid,
        in_specs=specs,
        out_specs=whole(shapes[0].shape) if single else [whole(s.shape) for s in shapes],
        scratch_shapes=scratch,
        compiler_params=pltpu.CompilerParams(vmem_limit_bytes=VMEM_LIMIT),
        cost_estimate=pl.CostEstimate(flops=int(flops), bytes_accessed=moved, transcendentals=0),
    )(*args)


def shift(value, axis, step):
    count = lax.axis_size(axis)
    return lax.ppermute(value, axis, [(i, i + step) for i in range(count) if 0 <= i + step < count])


def shards(features, conv_first, conv_second, up_kernel, cotangent):
    core = lax.axis_index("core")
    height = lax.axis_index("height")
    width = lax.axis_index("width")
    core_arg = core.astype(jnp.int32).reshape(1)
    window = 8 * width + height
    columns = OWN * window - EDGE + jnp.arange(WIN)
    inside = ((columns >= 0) & (columns < 128)).astype(F32)
    mask = jnp.broadcast_to(inside[:, None], (WIN, CH))
    act_shape = (FR, ROWS, WIN, CH)
    table = pltpu.VMEM((FR + 2, ROWS + 2, WIN, 3 * CH), BF16)
    own_table = pltpu.VMEM((FR + 2, ROWS + 2, OWN, 3 * CH), BF16)
    total = pltpu.VMEM((FR * ROWS * WIN, CH), F32)
    tap_flops = 2 * FR * ROWS * WIN * CH * CH

    padded = jnp.pad(features[:, 0], ((0, 0), (EDGE, EDGE), (0, 0))).reshape(2, 17, OWN, CH)
    windows = jnp.concatenate([padded[:, :-1], padded[:, 1:]], axis=2)
    windows = windows.reshape(2, 2, 8, WIN, CH).transpose(2, 1, 0, 3, 4).reshape(1, 16, 2, WIN, CH)
    windows = jnp.broadcast_to(windows, (2, 16, 2, WIN, CH)).reshape(32, 2, WIN, CH)
    block = lax.all_to_all(windows, ("core", "height", "width"), 0, 0, tiled=True)

    paired = cotangent.reshape(2, 4, 64, 2 * CH)
    edge = jnp.where(width == 0, paired[:, :, 64 - EDGE :], paired[:, :, :EDGE])
    edge = lax.ppermute(edge, "width", [(0, 1), (1, 0)])
    nothing = jnp.zeros_like(edge)
    low, high = jnp.where(width == 0, nothing, edge), jnp.where(width == 0, edge, nothing)
    paired = jnp.concatenate([low, paired, high], axis=2).reshape(2, 4, 9, OWN, 2 * CH)
    fine = jnp.concatenate([paired[:, :, :-1], paired[:, :, 1:]], axis=3).transpose(2, 0, 1, 3, 4)
    fine, block = lax.optimization_barrier((fine, block))
    block = block.reshape(2, ROWS, 2, WIN, CH)
    halo = shift(block[1], "y", 1)
    mine = lax.all_to_all(fine, "height", 0, 0, tiled=True).reshape(8, 2, 2, 2, WIN, 2 * CH)

    first_act, first_slope = call(
        first_kernel, (3,), (halo, block, conv_first, mask),
        [whole(halo.shape), whole(block.shape), tap_weights(), whole(mask.shape)],
        [(act_shape, BF16), (act_shape, F32)], [table, total], 27 * tap_flops,
    )
    mine, first_act = lax.optimization_barrier((mine, first_act))
    earlier = shift(first_act[2:], "y", 1)
    other = lax.ppermute(mine, "core", [(0, 1), (1, 0)])
    summed, up_act = call(
        second_kernel, (3,), (earlier, first_act, block, conv_second),
        [whole(earlier.shape), whole(act_shape), whole(block.shape), tap_weights()],
        [(act_shape, F32), (act_shape, BF16)], [table, total], 27 * tap_flops,
    )
    grad_sum = call(
        cotangent_kernel, (), (core_arg, mine, other, up_kernel, summed, mask),
        [SMEM, whole(mine.shape), whole(mine.shape), whole(up_kernel.shape), whole(act_shape), whole(mask.shape)],
        [(act_shape, BF16)], [pltpu.VMEM((FR, ROWS + 1, 2, WIN, 4 * CH), BF16)], 16 * tap_flops,
    )
    up_act, grad_sum = lax.optimization_barrier((up_act, grad_sum))
    later = shift(grad_sum[:2], "y", -1)
    up_part = call(
        up_grad_kernel, (), (core_arg, up_act, mine, other),
        [SMEM, whole(act_shape), whole(mine.shape), whole(mine.shape)],
        [((64, 32, CH), BF16)],
        [pltpu.VMEM((FR, ROWS + 1, 2, OWN, 4 * CH), BF16), pltpu.VMEM((CH, FR * ROWS * OWN), BF16)], 4 * tap_flops,
    )
    grad_hidden = call(
        hidden_kernel, (3,), (grad_sum, later, first_slope, conv_second, mask),
        [whole(act_shape), whole(later.shape), whole(act_shape), tap_weights(), whole(mask.shape)],
        [(act_shape, BF16)], [table, total], 27 * tap_flops,
    )
    later_hidden = shift(grad_hidden[:2], "y", -1)

    grad_scratch = [own_table, pltpu.VMEM((CH, FR * ROWS * OWN), BF16), pltpu.VMEM((TAPS * CH + 8, CH), F32)]

    def kernel_grad(act, by_core, grad, after):
        return call(
            functools.partial(kernel_grad_kernel, by_core), (), (core_arg, act, grad, after),
            [SMEM, whole(act.shape), whole(act_shape), whole(after.shape)],
            [((64, PIECE, CH), BF16)], grad_scratch, 14 * tap_flops,
        ).reshape(4, 16 * PIECE, CH)

    up_sum = lax.psum_scatter(up_part.reshape(4, 16 * UP_ROWS, CH), "y", scatter_dimension=0, tiled=True)
    tied_act, grad_hidden = lax.optimization_barrier((first_act, grad_hidden))
    second_part = kernel_grad(tied_act, False, grad_sum, later)
    second_sum = lax.psum_scatter(second_part, "y", scatter_dimension=0, tiled=True)
    first_part = kernel_grad(block, True, grad_hidden, later_hidden)
    first_sum = lax.all_to_all(first_part, "y", 0, 0, tiled=True)
    tied_hidden, first_part = lax.optimization_barrier((grad_hidden, first_part))
    rows_out = call(
        features_kernel, (3,), (core_arg, tied_hidden, later_hidden, grad_sum, conv_first),
        [SMEM, whole(act_shape), whole(later_hidden.shape), whole(act_shape), tap_weights()],
        [((ROWS, 2, OWN, CH), BF16)], [own_table, pltpu.VMEM((2 * ROWS * OWN, CH), F32)], 7 * tap_flops,
    )
    first_sum = jnp.sum(first_sum.astype(F32), axis=0).astype(BF16)
    parts = jnp.concatenate(
        [
            up_sum.reshape(16, UP_ROWS, CH),
            rows_out.reshape(16, 2 * OWN, CH),
            second_sum.reshape(16, PIECE, CH),
            first_sum.reshape(16, PIECE, CH),
        ],
        axis=1,
    )
    received = lax.all_to_all(parts, ("height", "width"), 0, 0, tiled=True)
    returned = received[:, UP_ROWS:GRAD_ROWS].reshape(8, 2, 2, OWN, CH).transpose(2, 1, 0, 3, 4)
    grad_features = returned.reshape(2, 1, 128, CH)
    factor = 1.0 / math.sqrt(32768)
    summed_parts = jnp.sum(received.astype(F32), axis=0) * factor
    up_share = summed_parts[:UP_ROWS].reshape(-1)
    second_share = summed_parts[GRAD_ROWS : GRAD_ROWS + SHARE].reshape(-1)
    first_share = summed_parts[GRAD_ROWS + PIECE : GRAD_ROWS + PIECE + SHARE].reshape(-1)
    return (grad_features, first_share, second_share, up_share)


def solution(mesh):
    names = ("y", "core", "height", "width")
    split = Mesh(mesh.devices.reshape(4, 2, 8, 2), names)
    tm = ("y", "core")
    in_specs = (
        P(tm, ("height", "width"), None, None),
        P(),
        P(),
        P(),
        P(tm, "height", "width", None),
    )
    flat = P(names)
    out_specs = (P(tm, ("height", "width"), None, None), flat, flat, flat)
    return jax.shard_map(shards, mesh=split, in_specs=in_specs, out_specs=out_specs, check_vma=False)
```

```python
import math

import jax
import jax.numpy as jnp
from jax import lax
from jax.experimental import pallas as pl
from jax.experimental.pallas import tpu as pltpu
from jax.sharding import Mesh, PartitionSpec as P

F32 = jnp.float32
BF16 = jnp.bfloat16
VMEM_LIMIT = 48 * 1024 * 1024

FR = 4
ROWS = 16
WIN = 16
OWN = 8
EDGE = 4
CH = 256
TAPS = 27
SHARE = 54
PIECE = 56
UP_ROWS = 32


def slope_of(values, sigma):
    return sigma * (1.0 + values * (1.0 - sigma))


def nt(lhs, rhs):
    return lax.dot_general(lhs, rhs, (((1,), (1,)), ((), ())), preferred_element_type=F32)


def nn(lhs, rhs):
    return jnp.dot(lhs, rhs, preferred_element_type=F32)


def fill_table(table, slot, block, forward):
    wide = block.astype(F32)
    before = pltpu.roll(wide, 1, axis=1).astype(BF16)
    after = pltpu.roll(wide, WIN - 1, axis=1).astype(BF16)
    table[slot, 1 : ROWS + 1, :, 0:CH] = before if forward else after
    table[slot, 1 : ROWS + 1, :, CH : 2 * CH] = block
    table[slot, 1 : ROWS + 1, :, 2 * CH : 3 * CH] = after if forward else before


def fill_own_table(table, slot, block):
    wide = block.astype(F32)
    for tap in range(3):
        moved = pltpu.roll(wide, WIN - (EDGE + 1 - tap), axis=1)
        table[slot, 1 : ROWS + 1, :, tap * CH : (tap + 1) * CH] = moved[:, :OWN].astype(BF16)


def clear_border(table):
    frames, _, columns, lanes = table.shape
    border = jnp.zeros((frames, columns, lanes), BF16)
    table[:, 0] = border
    table[:, ROWS + 1] = border


def own_columns(block):
    return pltpu.roll(block.astype(F32), WIN - EDGE, axis=1)[:, :OWN]


def first_kernel(halo, block, weights, mask, act, slope, table, total):
    step = pl.program_id(0)

    @pl.when(step == 0)
    def _():
        clear_border(table)
        for frame in range(2):
            fill_table(table, frame, halo[:, frame], True)
        for frame in range(FR):
            fill_table(table, 2 + frame, block[frame // 2, :, frame % 2], True)
        total[...] = jnp.zeros_like(total)

    for tap in range(3):
        lhs = table[pl.ds(step, FR), tap : tap + ROWS].reshape(FR * ROWS * WIN, 3 * CH)
        total[...] += nn(lhs, weights[0, tap].reshape(3 * CH, CH))

    @pl.when(step == 2)
    def _():
        inside = mask[...]
        for frame in range(FR):
            rows = ROWS * WIN
            values = total[frame * rows : (frame + 1) * rows].reshape(ROWS, WIN, CH)
            sigma = jax.nn.sigmoid(values)
            act[frame] = (values * sigma * inside).astype(BF16)
            slope[frame] = slope_of(values, sigma)


def second_kernel(halo, block, features, weights, summed, up_act, table, total):
    step = pl.program_id(0)

    @pl.when(step == 0)
    def _():
        clear_border(table)
        for frame in range(2):
            fill_table(table, frame, halo[frame], True)
        for frame in range(FR):
            fill_table(table, 2 + frame, block[frame], True)
        total[...] = jnp.zeros_like(total)

    for tap in range(3):
        lhs = table[pl.ds(step, FR), tap : tap + ROWS].reshape(FR * ROWS * WIN, 3 * CH)
        total[...] += nn(lhs, weights[0, tap].reshape(3 * CH, CH))

    @pl.when(step == 2)
    def _():
        for frame in range(FR):
            rows = ROWS * WIN
            values = total[frame * rows : (frame + 1) * rows].reshape(ROWS, WIN, CH)
            values = values + features[frame // 2, :, frame % 2].astype(F32)
            summed[frame] = values
            up_act[frame] = (values * jax.nn.sigmoid(values)).astype(BF16)


def hidden_kernel(block, later, slope, weights, mask, grad_hidden, table, total):
    step = pl.program_id(0)

    @pl.when(step == 0)
    def _():
        clear_border(table)
        for frame in range(FR):
            fill_table(table, frame, block[frame], False)
        for frame in range(2):
            fill_table(table, FR + frame, later[frame], False)
        total[...] = jnp.zeros_like(total)

    for tap in range(3):
        part = None
        for column in range(3):
            lhs = table[pl.ds(2 - step, FR), 2 - tap : 2 - tap + ROWS, :, column * CH : (column + 1) * CH]
            more = nt(lhs.reshape(FR * ROWS * WIN, CH), weights[0, tap, column])
            part = more if part is None else part + more
        total[...] += part

    @pl.when(step == 2)
    def _():
        inside = mask[...]
        for frame in range(FR):
            rows = ROWS * WIN
            values = total[frame * rows : (frame + 1) * rows].reshape(ROWS, WIN, CH)
            grad_hidden[frame] = (values * slope[frame] * inside).astype(BF16)


def features_kernel(core_ref, block, later, grad_sum, weights, grad_features, table, total):
    step = pl.program_id(0)
    core = core_ref[0]

    @pl.when(step == 0)
    def _():
        clear_border(table)
        for frame in range(FR):
            fill_own_table(table, frame, block[frame])
        for frame in range(2):
            fill_own_table(table, FR + frame, later[frame])
        total[...] = jnp.zeros_like(total)

    for tap in range(3):
        part = None
        for column in range(3):
            lhs = table[
                pl.ds(2 * core + 2 - step, 2), 2 - tap : 2 - tap + ROWS, :, column * CH : (column + 1) * CH
            ]
            more = nt(lhs.reshape(2 * ROWS * OWN, CH), weights[0, tap, column])
            part = more if part is None else part + more
        total[...] += part

    @pl.when(step == 2)
    def _():
        for frame in range(2):
            rows = ROWS * OWN
            values = total[frame * rows : (frame + 1) * rows].reshape(ROWS, OWN, CH)
            values = values + own_columns(grad_sum[2 * core + frame])
            grad_features[:, frame] = values.astype(BF16)


def cotangent_kernel(core_ref, mine, other, weights, summed, mask, grad_sum, table):
    core = core_ref[0]
    border = jnp.zeros((FR, WIN, 4 * CH), BF16)
    table[:, 0, 0] = border
    table[:, ROWS, 1] = border
    for source, which in ((mine, core), (other, 1 - core)):
        for frame in range(2):
            slot = 2 * which + frame
            for parity in range(2):
                fine = source[:, frame, :, parity].reshape(ROWS, WIN, 2 * CH)
                even, odd = fine[:, :, :CH], fine[:, :, CH:]
                before = pltpu.roll(odd.astype(F32), 1, axis=1).astype(BF16)
                after = pltpu.roll(even.astype(F32), WIN - 1, axis=1).astype(BF16)
                low = 0 if parity == 0 else 1
                put = (slot, slice(low, low + ROWS), 1 - parity)
                table[put + (slice(None), slice(0, CH))] = before
                table[put + (slice(None), slice(CH, 2 * CH))] = even
                table[put + (slice(None), slice(2 * CH, 3 * CH))] = odd
                table[put + (slice(None), slice(3 * CH, 4 * CH))] = after
    for frame in range(FR):
        part = None
        for tap in range(4):
            for column in range(4):
                lhs = table[frame, tap // 2 : tap // 2 + ROWS, tap % 2, :, column * CH : (column + 1) * CH]
                more = nt(lhs.reshape(ROWS * WIN, CH), weights[tap, column])
                part = more if part is None else part + more
        grad_act = part.reshape(ROWS, WIN, CH).astype(BF16).astype(F32)
        values = summed[frame]
        grad = grad_act * slope_of(values, jax.nn.sigmoid(values)) * mask[...]
        grad_sum[frame] = grad.astype(BF16)


def up_grad_kernel(core_ref, act, mine, other, out, table, flipped):
    core = core_ref[0]
    border = jnp.zeros((FR, OWN, 4 * CH), BF16)
    table[:, 0, 0] = border
    table[:, ROWS, 1] = border
    for source, which in ((mine, core), (other, 1 - core)):
        for frame in range(2):
            slot = 2 * which + frame
            for parity in range(2):
                fine = source[:, frame, :, parity].reshape(ROWS, WIN, 2 * CH).astype(F32)
                even, odd = fine[:, :, :CH], fine[:, :, CH:]
                low = 0 if parity == 0 else 1
                put = (slot, slice(low, low + ROWS), 1 - parity)
                for column, (values, shift) in enumerate(((odd, -1), (even, 0), (odd, 0), (even, 1))):
                    moved = pltpu.roll(values, WIN - (EDGE + shift), axis=1)[:, :OWN].astype(BF16)
                    table[put + (slice(None), slice(column * CH, (column + 1) * CH))] = moved
    for frame in range(FR):
        rows = ROWS * OWN
        flipped[:, frame * rows : (frame + 1) * rows] = jnp.transpose(
            own_columns(act[frame]).reshape(rows, CH)
        ).astype(BF16)
    lanes = pl.ds(pl.multiple_of(core * 2 * CH, 2 * CH), 2 * CH)
    for tap in range(4):
        rhs = table[:, tap // 2 : tap // 2 + ROWS, tap % 2, :, lanes]
        result = nn(flipped[...], rhs.reshape(FR * ROWS * OWN, 2 * CH))
        for half in range(2):
            for piece in range(8):
                out[tap * 16 + half * 8 + piece] = result[
                    piece * 32 : (piece + 1) * 32, half * CH : (half + 1) * CH
                ].astype(BF16)


def tap_sums(act_of, block, later, table, flipped, sums):
    clear_border(table)
    for frame in range(FR):
        fill_own_table(table, frame, block[frame])
    for frame in range(2):
        fill_own_table(table, FR + frame, later[frame])
    for frame in range(FR):
        rows = ROWS * OWN
        flipped[:, frame * rows : (frame + 1) * rows] = jnp.transpose(
            own_columns(act_of(frame)).reshape(rows, CH)
        ).astype(BF16)
    sums[TAPS * CH :] = jnp.zeros((8, CH), F32)
    for tap_t in range(3):
        for tap_h in range(3):
            rhs = table[2 - tap_t : 2 - tap_t + FR, 2 - tap_h : 2 - tap_h + ROWS]
            result = nn(flipped[...], rhs.reshape(FR * ROWS * OWN, 3 * CH))
            for tap_w in range(3):
                at = (tap_t * 9 + tap_h * 3 + tap_w) * CH
                sums[at : at + CH] = result[:, tap_w * CH : (tap_w + 1) * CH]


def piece_of(sums, owner, member):
    at = SHARE * member
    start = pl.multiple_of(16 * SHARE * owner + at // 8 * 8, 8)
    return sums[pl.ds(start, PIECE + 8)][at % 8 : at % 8 + PIECE]


def second_grad_kernel(place, act, block, later, up, out, table, flipped, sums):
    tap_sums(lambda frame: act[frame], block, later, table, flipped, sums)
    for group in range(4):
        for member in range(16):
            chunk = member // 4 * 16 + group * 4 + member % 4
            out[chunk, :UP_ROWS] = up[group * 16 + member]
            out[chunk, UP_ROWS:] = piece_of(sums, 2 * group + place[0], member).astype(BF16)


def first_grad_kernel(place, act, block, later, own, next_one, next_two, next_three, table, flipped, sums):
    tap_sums(lambda frame: act[frame // 2, :, frame % 2], block, later, table, flipped, sums)
    for step, out in enumerate((own, next_one, next_two, next_three)):
        group = lax.rem(place[1] + step, 4)
        for member in range(16):
            out[member] = piece_of(sums, 2 * group + place[0], member).astype(BF16)


def whole(shape):
    zeros = (0,) * len(shape)
    return pl.BlockSpec(shape, lambda *_: zeros)


SMEM = pl.BlockSpec(memory_space=pltpu.SMEM)


def tap_weights():
    return pl.BlockSpec((1, 3, 3, CH, CH), lambda step: (step, 0, 0, 0, 0))


def call(kernel, grid, args, specs, outs, scratch, flops):
    shapes = [jax.ShapeDtypeStruct(shape, dtype) for shape, dtype in outs]
    moved = sum(math.prod(a.shape) * a.dtype.itemsize for a in args)
    moved += sum(math.prod(s.shape) * s.dtype.itemsize for s in shapes)
    single = len(shapes) == 1
    return pl.pallas_call(
        kernel,
        out_shape=shapes[0] if single else shapes,
        grid=grid,
        in_specs=specs,
        out_specs=whole(shapes[0].shape) if single else [whole(s.shape) for s in shapes],
        scratch_shapes=scratch,
        compiler_params=pltpu.CompilerParams(vmem_limit_bytes=VMEM_LIMIT),
        cost_estimate=pl.CostEstimate(flops=int(flops), bytes_accessed=moved, transcendentals=0),
    )(*args)


def shift(value, axis, step):
    count = lax.axis_size(axis)
    return lax.ppermute(value, axis, [(i, i + step) for i in range(count) if 0 <= i + step < count])


def shards(features, conv_first, conv_second, up_kernel, cotangent):
    core = lax.axis_index("core")
    height = 2 * lax.axis_index("z") + lax.axis_index("x_hi")
    width = lax.axis_index("width")
    core_arg = core.astype(jnp.int32).reshape(1)
    place = jnp.stack([core, lax.axis_index("y")]).astype(jnp.int32)
    window = 8 * width + height
    columns = OWN * window - EDGE + jnp.arange(WIN)
    inside = ((columns >= 0) & (columns < 128)).astype(F32)
    mask = jnp.broadcast_to(inside[:, None], (WIN, CH))
    act_shape = (FR, ROWS, WIN, CH)
    table = pltpu.VMEM((FR + 2, ROWS + 2, WIN, 3 * CH), BF16)
    own_table = pltpu.VMEM((FR + 2, ROWS + 2, OWN, 3 * CH), BF16)
    total = pltpu.VMEM((FR * ROWS * WIN, CH), F32)
    tap_flops = 2 * FR * ROWS * WIN * CH * CH

    padded = jnp.pad(features[:, 0], ((0, 0), (EDGE, EDGE), (0, 0))).reshape(2, 17, OWN, CH)
    windows = jnp.concatenate([padded[:, :-1], padded[:, 1:]], axis=2)
    windows = windows.reshape(2, 2, 8, WIN, CH).transpose(2, 1, 0, 3, 4).reshape(1, 16, 2, WIN, CH)
    windows = jnp.broadcast_to(windows, (2, 16, 2, WIN, CH)).reshape(32, 2, WIN, CH)
    block = lax.all_to_all(windows, ("core", "z", "x_hi", "width"), 0, 0, tiled=True)

    paired = cotangent.reshape(2, 4, 64, 2 * CH)
    edge = jnp.where(width == 0, paired[:, :, 64 - EDGE :], paired[:, :, :EDGE])
    edge = lax.ppermute(edge, "width", [(0, 1), (1, 0)])
    nothing = jnp.zeros_like(edge)
    low, high = jnp.where(width == 0, nothing, edge), jnp.where(width == 0, edge, nothing)
    paired = jnp.concatenate([low, paired, high], axis=2).reshape(2, 4, 9, OWN, 2 * CH)
    fine = jnp.concatenate([paired[:, :, :-1], paired[:, :, 1:]], axis=3).transpose(2, 0, 1, 3, 4)
    fine, block = lax.optimization_barrier((fine, block))
    block = block.reshape(2, ROWS, 2, WIN, CH)
    halo = shift(block[1], "y", 1)
    mine = lax.all_to_all(fine, ("z", "x_hi"), 0, 0, tiled=True).reshape(8, 2, 2, 2, WIN, 2 * CH)

    first_act, first_slope = call(
        first_kernel, (3,), (halo, block, conv_first, mask),
        [whole(halo.shape), whole(block.shape), tap_weights(), whole(mask.shape)],
        [(act_shape, BF16), (act_shape, F32)], [table, total], 27 * tap_flops,
    )
    mine, first_act = lax.optimization_barrier((mine, first_act))
    earlier = shift(first_act[2:], "y", 1)
    other = lax.ppermute(mine, "core", [(0, 1), (1, 0)])
    summed, up_act = call(
        second_kernel, (3,), (earlier, first_act, block, conv_second),
        [whole(earlier.shape), whole(act_shape), whole(block.shape), tap_weights()],
        [(act_shape, F32), (act_shape, BF16)], [table, total], 27 * tap_flops,
    )
    grad_sum = call(
        cotangent_kernel, (), (core_arg, mine, other, up_kernel, summed, mask),
        [SMEM, whole(mine.shape), whole(mine.shape), whole(up_kernel.shape), whole(act_shape), whole(mask.shape)],
        [(act_shape, BF16)], [pltpu.VMEM((FR, ROWS + 1, 2, WIN, 4 * CH), BF16)], 16 * tap_flops,
    )
    later = shift(grad_sum[:2], "y", -1)
    up_act, later = lax.optimization_barrier((up_act, later))
    up_part = call(
        up_grad_kernel, (), (core_arg, up_act, mine, other),
        [SMEM, whole(act_shape), whole(mine.shape), whole(mine.shape)],
        [((64, 32, CH), BF16)],
        [pltpu.VMEM((FR, ROWS + 1, 2, OWN, 4 * CH), BF16), pltpu.VMEM((CH, FR * ROWS * OWN), BF16)], 4 * tap_flops,
    )
    grad_scratch = [own_table, pltpu.VMEM((CH, FR * ROWS * OWN), BF16), pltpu.VMEM((TAPS * CH + 8, CH), F32)]
    early = call(
        second_grad_kernel, (), (place, first_act, grad_sum, later, up_part),
        [SMEM, whole(act_shape), whole(act_shape), whole(later.shape), whole(up_part.shape)],
        [((64, UP_ROWS + PIECE, CH), BF16)], grad_scratch, 14 * tap_flops,
    )
    early = lax.all_to_all(early, "z", 0, 0, tiled=True)

    grad_hidden = call(
        hidden_kernel, (3,), (grad_sum, later, first_slope, conv_second, mask),
        [whole(act_shape), whole(later.shape), whole(act_shape), tap_weights(), whole(mask.shape)],
        [(act_shape, BF16)], [table, total], 27 * tap_flops,
    )
    later_hidden = shift(grad_hidden[:2], "y", -1)
    blocks = call(
        first_grad_kernel, (), (place, block, grad_hidden, later_hidden),
        [SMEM, whole(block.shape), whole(act_shape), whole(later_hidden.shape)],
        [((16, PIECE, CH), BF16)] * 4, grad_scratch, 14 * tap_flops,
    )
    arrived = [blocks[0]]
    for step in (2, 1, 3):
        arrived.append(lax.ppermute(blocks[step], "y", [(i, (i + step) % 4) for i in range(4)]))
    tied_hidden, _ = lax.optimization_barrier((grad_hidden, blocks[0]))
    rows_out = call(
        features_kernel, (3,), (core_arg, tied_hidden, later_hidden, grad_sum, conv_first),
        [SMEM, whole(act_shape), whole(later_hidden.shape), whole(act_shape), tap_weights()],
        [((ROWS, 2, OWN, CH), BF16)], [own_table, pltpu.VMEM((2 * ROWS * OWN, CH), F32)], 7 * tap_flops,
    )

    early = jnp.sum(early.reshape(4, 16, UP_ROWS + PIECE, CH).astype(F32), axis=0).astype(BF16)
    early = lax.all_to_all(early, ("y", "x_hi", "width"), 0, 0, tiled=True)
    first_sum = sum(value.astype(F32) for value in arrived).astype(BF16)
    late = jnp.concatenate([rows_out.reshape(16, 2 * OWN, CH), first_sum], axis=1)
    late, early = lax.optimization_barrier((late, early))
    late = lax.all_to_all(late, ("z", "x_hi", "width"), 0, 0, tiled=True)

    factor = 1.0 / math.sqrt(32768)
    early = jnp.sum(early.astype(F32), axis=0) * factor
    returned = late[:, : 2 * OWN].reshape(8, 2, 2, OWN, CH).transpose(2, 1, 0, 3, 4)
    first_share = jnp.sum(late[:, 2 * OWN : 2 * OWN + SHARE].astype(F32), axis=0) * factor
    return (
        returned.reshape(2, 1, 128, CH),
        first_share.reshape(-1),
        early[UP_ROWS : UP_ROWS + SHARE].reshape(-1),
        early[:UP_ROWS].reshape(-1),
    )


def solution(mesh):
    names = ("y", "core", "z", "x_hi", "width")
    split = Mesh(mesh.devices.reshape(4, 2, 4, 2, 2), names)
    tm, height = ("y", "core"), ("z", "x_hi")
    in_specs = (
        P(tm, (*height, "width"), None, None),
        P(),
        P(),
        P(),
        P(tm, height, "width", None),
    )
    flat = P(names)
    out_specs = (P(tm, (*height, "width"), None, None), flat, flat, flat)
    return jax.shard_map(shards, mesh=split, in_specs=in_specs, out_specs=out_specs, check_vma=False)
```

```python
import math

import jax
import jax.numpy as jnp
from jax import lax
from jax.experimental import pallas as pl
from jax.experimental.pallas import tpu as pltpu
from jax.sharding import Mesh, PartitionSpec as P

F32 = jnp.float32
BF16 = jnp.bfloat16
VMEM_LIMIT = 48 * 1024 * 1024

FR = 4
ROWS = 16
WIN = 16
OWN = 8
EDGE = 4
CH = 256
TAPS = 27
SHARE = 54
PIECE = 56
UP_ROWS = 32


def slope_of(values, sigma):
    return sigma * (1.0 + values * (1.0 - sigma))


def nt(lhs, rhs):
    return lax.dot_general(lhs, rhs, (((1,), (1,)), ((), ())), preferred_element_type=F32)


def nn(lhs, rhs):
    return jnp.dot(lhs, rhs, preferred_element_type=F32)


def fill_table(table, slot, block, forward):
    wide = block.astype(F32)
    before = pltpu.roll(wide, 1, axis=1).astype(BF16)
    after = pltpu.roll(wide, WIN - 1, axis=1).astype(BF16)
    table[slot, 1 : ROWS + 1, :, 0:CH] = before if forward else after
    table[slot, 1 : ROWS + 1, :, CH : 2 * CH] = block
    table[slot, 1 : ROWS + 1, :, 2 * CH : 3 * CH] = after if forward else before


def fill_own_table(table, slot, block):
    wide = block.astype(F32)
    for tap in range(3):
        moved = pltpu.roll(wide, WIN - (EDGE + 1 - tap), axis=1)
        table[slot, 1 : ROWS + 1, :, tap * CH : (tap + 1) * CH] = moved[:, :OWN].astype(BF16)


def clear_border(table):
    frames, _, columns, lanes = table.shape
    border = jnp.zeros((frames, columns, lanes), BF16)
    table[:, 0] = border
    table[:, ROWS + 1] = border


def own_columns(block):
    return pltpu.roll(block.astype(F32), WIN - EDGE, axis=1)[:, :OWN]


def fetch(weights, held, arrived):
    copies = [pltpu.make_async_copy(weights.at[tap], held.at[tap], arrived.at[tap]) for tap in range(3)]
    for copy in copies:
        copy.start()
    return copies


def forward_taps(table, held, copies, total):
    for tap_t in range(3):
        copies[tap_t].wait()
        for tap_h in range(3):
            lhs = table[tap_t : tap_t + FR, tap_h : tap_h + ROWS].reshape(FR * ROWS * WIN, 3 * CH)
            part = nn(lhs, held[tap_t, tap_h].reshape(3 * CH, CH))
            if tap_t + tap_h == 0:
                total[...] = part
            else:
                total[...] += part


def backward_taps(table, start, frames, columns, held, copies, total):
    for tap_t in range(3):
        copies[tap_t].wait()
        for tap_h in range(3):
            part = None
            for tap_w in range(3):
                lanes = slice(tap_w * CH, (tap_w + 1) * CH)
                lhs = table[pl.ds(start + 2 - tap_t, frames), 2 - tap_h : 2 - tap_h + ROWS, :, lanes]
                more = nt(lhs.reshape(frames * ROWS * columns, CH), held[tap_t, tap_h, tap_w])
                part = more if part is None else part + more
            if tap_t + tap_h == 0:
                total[...] = part
            else:
                total[...] += part


def frame_of(total, frame, columns):
    rows = ROWS * columns
    return total[frame * rows : (frame + 1) * rows].reshape(ROWS, columns, CH)


def first_kernel(halo, block, weights, mask, act, tail, slope, table, total, held, arrived):
    copies = fetch(weights, held, arrived)
    clear_border(table)
    for frame in range(2):
        fill_table(table, frame, halo[:, frame], True)
    for frame in range(FR):
        fill_table(table, 2 + frame, block[frame // 2, :, frame % 2], True)
    forward_taps(table, held, copies, total)
    for frame in range(FR):
        values = frame_of(total, frame, WIN)
        sigma = jax.nn.sigmoid(values)
        result = (values * sigma * mask[...]).astype(BF16)
        act[frame] = result
        if frame >= 2:
            tail[frame - 2] = result
        slope[frame] = slope_of(values, sigma)


def second_kernel(halo, block, features, weights, summed, up_act, table, total, held, arrived):
    copies = fetch(weights, held, arrived)
    clear_border(table)
    for frame in range(2):
        fill_table(table, frame, halo[frame], True)
    for frame in range(FR):
        fill_table(table, 2 + frame, block[frame], True)
    forward_taps(table, held, copies, total)
    for frame in range(FR):
        values = frame_of(total, frame, WIN) + features[frame // 2, :, frame % 2].astype(F32)
        summed[frame] = values
        up_act[frame] = (values * jax.nn.sigmoid(values)).astype(BF16)


def hidden_kernel(block, later, slope, weights, mask, grad_hidden, head, table, total, held, arrived):
    copies = fetch(weights, held, arrived)
    clear_border(table)
    for frame in range(FR):
        fill_table(table, frame, block[frame], False)
    for frame in range(2):
        fill_table(table, FR + frame, later[frame], False)
    backward_taps(table, 0, FR, WIN, held, copies, total)
    for frame in range(FR):
        result = (frame_of(total, frame, WIN) * slope[frame] * mask[...]).astype(BF16)
        grad_hidden[frame] = result
        if frame < 2:
            head[frame] = result


def features_kernel(core_ref, block, later, grad_sum, weights, grad_features, table, total, held, arrived):
    copies = fetch(weights, held, arrived)
    core = core_ref[0]
    clear_border(table)
    for frame in range(FR):
        fill_own_table(table, frame, block[frame])
    for frame in range(2):
        fill_own_table(table, FR + frame, later[frame])
    backward_taps(table, 2 * core, 2, OWN, held, copies, total)
    for frame in range(2):
        values = frame_of(total, frame, OWN) + own_columns(grad_sum[2 * core + frame])
        grad_features[:, frame] = values.astype(BF16)


def cotangent_kernel(core_ref, mine, other, weights, summed, mask, grad_sum, head, table):
    core = core_ref[0]
    border = jnp.zeros((FR, WIN, 4 * CH), BF16)
    table[:, 0, 0] = border
    table[:, ROWS, 1] = border
    for source, which in ((mine, core), (other, 1 - core)):
        for frame in range(2):
            slot = 2 * which + frame
            for parity in range(2):
                fine = source[:, frame, :, parity].reshape(ROWS, WIN, 2 * CH)
                even, odd = fine[:, :, :CH], fine[:, :, CH:]
                before = pltpu.roll(odd.astype(F32), 1, axis=1).astype(BF16)
                after = pltpu.roll(even.astype(F32), WIN - 1, axis=1).astype(BF16)
                low = 0 if parity == 0 else 1
                put = (slot, slice(low, low + ROWS), 1 - parity)
                table[put + (slice(None), slice(0, CH))] = before
                table[put + (slice(None), slice(CH, 2 * CH))] = even
                table[put + (slice(None), slice(2 * CH, 3 * CH))] = odd
                table[put + (slice(None), slice(3 * CH, 4 * CH))] = after
    for frame in range(FR):
        part = None
        for tap in range(4):
            for column in range(4):
                lhs = table[frame, tap // 2 : tap // 2 + ROWS, tap % 2, :, column * CH : (column + 1) * CH]
                more = nt(lhs.reshape(ROWS * WIN, CH), weights[tap, column])
                part = more if part is None else part + more
        grad_act = part.reshape(ROWS, WIN, CH).astype(BF16).astype(F32)
        values = summed[frame]
        grad = grad_act * slope_of(values, jax.nn.sigmoid(values)) * mask[...]
        grad_sum[frame] = grad.astype(BF16)
        if frame < 2:
            head[frame] = grad.astype(BF16)


def up_grad_kernel(core_ref, act, mine, other, out, table, flipped):
    core = core_ref[0]
    border = jnp.zeros((FR, OWN, 4 * CH), BF16)
    table[:, 0, 0] = border
    table[:, ROWS, 1] = border
    for source, which in ((mine, core), (other, 1 - core)):
        for frame in range(2):
            slot = 2 * which + frame
            for parity in range(2):
                fine = source[:, frame, :, parity].reshape(ROWS, WIN, 2 * CH).astype(F32)
                even, odd = fine[:, :, :CH], fine[:, :, CH:]
                low = 0 if parity == 0 else 1
                put = (slot, slice(low, low + ROWS), 1 - parity)
                for column, (values, shift) in enumerate(((odd, -1), (even, 0), (odd, 0), (even, 1))):
                    moved = pltpu.roll(values, WIN - (EDGE + shift), axis=1)[:, :OWN].astype(BF16)
                    table[put + (slice(None), slice(column * CH, (column + 1) * CH))] = moved
    for frame in range(FR):
        rows = ROWS * OWN
        flipped[:, frame * rows : (frame + 1) * rows] = jnp.transpose(
            own_columns(act[frame]).reshape(rows, CH)
        ).astype(BF16)
    lanes = pl.ds(pl.multiple_of(core * 2 * CH, 2 * CH), 2 * CH)
    for tap in range(4):
        rhs = table[:, tap // 2 : tap // 2 + ROWS, tap % 2, :, lanes]
        result = nn(flipped[...], rhs.reshape(FR * ROWS * OWN, 2 * CH))
        for half in range(2):
            for piece in range(8):
                out[tap * 16 + half * 8 + piece] = result[
                    piece * 32 : (piece + 1) * 32, half * CH : (half + 1) * CH
                ].astype(BF16)


def tap_sums(act_of, block, later, table, flipped, sums):
    clear_border(table)
    for frame in range(FR):
        fill_own_table(table, frame, block[frame])
    for frame in range(2):
        fill_own_table(table, FR + frame, later[frame])
    for frame in range(FR):
        rows = ROWS * OWN
        flipped[:, frame * rows : (frame + 1) * rows] = jnp.transpose(
            own_columns(act_of(frame)).reshape(rows, CH)
        ).astype(BF16)
    sums[TAPS * CH :] = jnp.zeros((8, CH), F32)
    for tap_t in range(3):
        for tap_h in range(3):
            rhs = table[2 - tap_t : 2 - tap_t + FR, 2 - tap_h : 2 - tap_h + ROWS]
            result = nn(flipped[...], rhs.reshape(FR * ROWS * OWN, 3 * CH))
            for tap_w in range(3):
                at = (tap_t * 9 + tap_h * 3 + tap_w) * CH
                sums[at : at + CH] = result[:, tap_w * CH : (tap_w + 1) * CH]


def piece_of(sums, owner, member):
    at = SHARE * member
    start = pl.multiple_of(16 * SHARE * owner + at // 8 * 8, 8)
    return sums[pl.ds(start, PIECE + 8)][at % 8 : at % 8 + PIECE]


def second_grad_kernel(place, act, block, later, up, out, table, flipped, sums):
    tap_sums(lambda frame: act[frame], block, later, table, flipped, sums)
    for step in range(4):
        group = lax.rem(place[1] + step, 4)
        for member in range(16):
            chunk = member * 4 + step
            out[chunk, :UP_ROWS] = up[group * 16 + member]
            out[chunk, UP_ROWS:] = piece_of(sums, 2 * group + place[0], member).astype(BF16)


def first_grad_kernel(place, act, block, later, own, next_one, next_two, next_three, table, flipped, sums):
    tap_sums(lambda frame: act[frame // 2, :, frame % 2], block, later, table, flipped, sums)
    for step, out in enumerate((own, next_one, next_two, next_three)):
        group = lax.rem(place[1] + step, 4)
        for member in range(16):
            out[member] = piece_of(sums, 2 * group + place[0], member).astype(BF16)


def whole(shape):
    zeros = (0,) * len(shape)
    return pl.BlockSpec(shape, lambda *_: zeros)


SMEM = pl.BlockSpec(memory_space=pltpu.SMEM)


HBM = pl.BlockSpec(memory_space=pltpu.HBM)
WEIGHTS = [pltpu.VMEM((3, 3, 3, CH, CH), BF16), pltpu.SemaphoreType.DMA((3,))]


def call(kernel, grid, args, specs, outs, scratch, flops):
    shapes = [jax.ShapeDtypeStruct(shape, dtype) for shape, dtype in outs]
    moved = sum(math.prod(a.shape) * a.dtype.itemsize for a in args)
    moved += sum(math.prod(s.shape) * s.dtype.itemsize for s in shapes)
    single = len(shapes) == 1
    return pl.pallas_call(
        kernel,
        out_shape=shapes[0] if single else shapes,
        grid=grid,
        in_specs=specs,
        out_specs=whole(shapes[0].shape) if single else [whole(s.shape) for s in shapes],
        scratch_shapes=scratch,
        compiler_params=pltpu.CompilerParams(vmem_limit_bytes=VMEM_LIMIT),
        cost_estimate=pl.CostEstimate(flops=int(flops), bytes_accessed=moved, transcendentals=0),
    )(*args)


def shift(value, axis, step):
    count = lax.axis_size(axis)
    return lax.ppermute(value, axis, [(i, i + step) for i in range(count) if 0 <= i + step < count])


def over_y(value, step):
    return lax.ppermute(value, "y", [(i, (i + step) % 4) for i in range(4)])


def shards(features, conv_first, conv_second, up_kernel, cotangent):
    core = lax.axis_index("core")
    height = 2 * lax.axis_index("z") + lax.axis_index("x_hi")
    width = lax.axis_index("width")
    core_arg = core.astype(jnp.int32).reshape(1)
    place = jnp.stack([core, lax.axis_index("y")]).astype(jnp.int32)
    window = 8 * width + height
    columns = OWN * window - EDGE + jnp.arange(WIN)
    inside = ((columns >= 0) & (columns < 128)).astype(F32)
    mask = jnp.broadcast_to(inside[:, None], (WIN, CH))
    act_shape = (FR, ROWS, WIN, CH)
    two_frames = (2, ROWS, WIN, CH)
    table = pltpu.VMEM((FR + 2, ROWS + 2, WIN, 3 * CH), BF16)
    own_table = pltpu.VMEM((FR + 2, ROWS + 2, OWN, 3 * CH), BF16)
    total = pltpu.VMEM((FR * ROWS * WIN, CH), F32)
    tap_flops = 2 * FR * ROWS * WIN * CH * CH

    padded = jnp.pad(features[:, 0], ((0, 0), (EDGE, EDGE), (0, 0))).reshape(2, 17, OWN, CH)
    windows = jnp.concatenate([padded[:, :-1], padded[:, 1:]], axis=2)
    windows = windows.reshape(2, 2, 8, WIN, CH).transpose(2, 1, 0, 3, 4).reshape(1, 16, 2, WIN, CH)
    windows = jnp.broadcast_to(windows, (2, 16, 2, WIN, CH)).reshape(32, 2, WIN, CH)
    block = lax.all_to_all(windows, ("core", "z", "x_hi", "width"), 0, 0, tiled=True)

    paired = cotangent.reshape(2, 4, 64, 2 * CH)
    edge = jnp.where(width == 0, paired[:, :, 64 - EDGE :], paired[:, :, :EDGE])
    edge = lax.ppermute(edge, "width", [(0, 1), (1, 0)])
    nothing = jnp.zeros_like(edge)
    low, high = jnp.where(width == 0, nothing, edge), jnp.where(width == 0, edge, nothing)
    paired = jnp.concatenate([low, paired, high], axis=2).reshape(2, 4, 9, OWN, 2 * CH)
    fine = jnp.concatenate([paired[:, :, :-1], paired[:, :, 1:]], axis=3).transpose(2, 0, 1, 3, 4)
    fine, block = lax.optimization_barrier((fine, block))
    block = block.reshape(2, ROWS, 2, WIN, CH)
    halo = shift(block[1], "y", 1)
    mine = lax.all_to_all(fine, ("z", "x_hi"), 0, 0, tiled=True).reshape(8, 2, 2, 2, WIN, 2 * CH)

    first_act, first_tail, first_slope = call(
        first_kernel, (), (halo, block, conv_first, mask),
        [whole(halo.shape), whole(block.shape), HBM, whole(mask.shape)],
        [(act_shape, BF16), (two_frames, BF16), (act_shape, F32)], [table, total, *WEIGHTS], 27 * tap_flops,
    )
    mine, first_tail = lax.optimization_barrier((mine, first_tail))
    earlier = shift(first_tail, "y", 1)
    other = lax.ppermute(mine, "core", [(0, 1), (1, 0)])
    summed, up_act = call(
        second_kernel, (), (earlier, first_act, block, conv_second),
        [whole(earlier.shape), whole(act_shape), whole(block.shape), HBM],
        [(act_shape, F32), (act_shape, BF16)], [table, total, *WEIGHTS], 27 * tap_flops,
    )
    grad_sum, sum_head = call(
        cotangent_kernel, (), (core_arg, mine, other, up_kernel, summed, mask),
        [SMEM, whole(mine.shape), whole(mine.shape), whole(up_kernel.shape), whole(act_shape), whole(mask.shape)],
        [(act_shape, BF16), (two_frames, BF16)], [pltpu.VMEM((FR, ROWS + 1, 2, WIN, 4 * CH), BF16)], 16 * tap_flops,
    )
    later = shift(sum_head, "y", -1)
    up_act, grad_sum = lax.optimization_barrier((up_act, grad_sum))
    up_part = call(
        up_grad_kernel, (), (core_arg, up_act, mine, other),
        [SMEM, whole(act_shape), whole(mine.shape), whole(mine.shape)],
        [((64, 32, CH), BF16)],
        [pltpu.VMEM((FR, ROWS + 1, 2, OWN, 4 * CH), BF16), pltpu.VMEM((CH, FR * ROWS * OWN), BF16)], 4 * tap_flops,
    )
    grad_scratch = [own_table, pltpu.VMEM((CH, FR * ROWS * OWN), BF16), pltpu.VMEM((TAPS * CH + 8, CH), F32)]
    early = call(
        second_grad_kernel, (), (place, first_act, grad_sum, later, up_part),
        [SMEM, whole(act_shape), whole(act_shape), whole(later.shape), whole(up_part.shape)],
        [((64, UP_ROWS + PIECE, CH), BF16)], grad_scratch, 14 * tap_flops,
    )
    early = lax.all_to_all(early, ("z", "x_hi", "width"), 0, 0, tiled=True)

    grad_hidden, hidden_head = call(
        hidden_kernel, (), (grad_sum, later, first_slope, conv_second, mask),
        [whole(act_shape), whole(later.shape), whole(act_shape), HBM, whole(mask.shape)],
        [(act_shape, BF16), (two_frames, BF16)], [table, total, *WEIGHTS], 27 * tap_flops,
    )
    later_hidden = shift(hidden_head, "y", -1)
    blocks = call(
        first_grad_kernel, (), (place, block, grad_hidden, later_hidden),
        [SMEM, whole(block.shape), whole(act_shape), whole(later_hidden.shape)],
        [((16, PIECE, CH), BF16)] * 4, grad_scratch, 14 * tap_flops,
    )
    arrived = [blocks[0]]
    for step in (2, 1, 3):
        arrived.append(over_y(blocks[step], step))
    tied_hidden, _ = lax.optimization_barrier((grad_hidden, blocks[0]))
    rows_out = call(
        features_kernel, (), (core_arg, tied_hidden, later_hidden, grad_sum, conv_first),
        [SMEM, whole(act_shape), whole(later_hidden.shape), whole(act_shape), HBM],
        [((ROWS, 2, OWN, CH), BF16)], [own_table, pltpu.VMEM((2 * ROWS * OWN, CH), F32), *WEIGHTS], 7 * tap_flops,
    )

    tied_rows, early = lax.optimization_barrier((rows_out, early))
    early = jnp.sum(early.reshape(16, 4, UP_ROWS + PIECE, CH).astype(F32), axis=0)
    early_total = early[0]
    for step in (2, 1, 3):
        early_total += over_y(early[step].astype(BF16), step).astype(F32)
    first_sum = sum(value.astype(F32) for value in arrived).astype(BF16)
    late = jnp.concatenate([tied_rows.reshape(16, 2 * OWN, CH), first_sum], axis=1)
    late = lax.all_to_all(late, ("z", "x_hi", "width"), 0, 0, tiled=True)

    factor = 1.0 / math.sqrt(32768)
    early = early_total * factor
    returned = late[:, : 2 * OWN].reshape(8, 2, 2, OWN, CH).transpose(2, 1, 0, 3, 4)
    first_share = jnp.sum(late[:, 2 * OWN : 2 * OWN + SHARE].astype(F32), axis=0) * factor
    return (
        returned.reshape(2, 1, 128, CH),
        first_share.reshape(-1),
        early[UP_ROWS : UP_ROWS + SHARE].reshape(-1),
        early[:UP_ROWS].reshape(-1),
    )


def solution(mesh):
    names = ("y", "core", "z", "x_hi", "width")
    split = Mesh(mesh.devices.reshape(4, 2, 4, 2, 2), names)
    tm, height = ("y", "core"), ("z", "x_hi")
    in_specs = (
        P(tm, (*height, "width"), None, None),
        P(),
        P(),
        P(),
        P(tm, height, "width", None),
    )
    flat = P(names)
    out_specs = (P(tm, (*height, "width"), None, None), flat, flat, flat)
    return jax.shard_map(shards, mesh=split, in_specs=in_specs, out_specs=out_specs, check_vma=False)
```

```python
import math

import jax
import jax.numpy as jnp
from jax import lax
from jax.experimental import pallas as pl
from jax.experimental.pallas import tpu as pltpu
from jax.sharding import Mesh, PartitionSpec as P

F32 = jnp.float32
BF16 = jnp.bfloat16
VMEM_LIMIT = 48 * 1024 * 1024

FR = 4
ROWS = 16
WIN = 16
OWN = 8
EDGE = 4
CH = 256
TAPS = 27
SHARE = 54
PIECE = 56
UP_ROWS = 32


def slope_of(values, sigma):
    return sigma * (1.0 + values * (1.0 - sigma))


def nt(lhs, rhs):
    return lax.dot_general(lhs, rhs, (((1,), (1,)), ((), ())), preferred_element_type=F32)


def nn(lhs, rhs):
    return jnp.dot(lhs, rhs, preferred_element_type=F32)


def fill_table(table, slot, block, forward):
    wide = block.astype(F32)
    before = pltpu.roll(wide, 1, axis=1).astype(BF16)
    after = pltpu.roll(wide, WIN - 1, axis=1).astype(BF16)
    table[slot, 1 : ROWS + 1, :, 0:CH] = before if forward else after
    table[slot, 1 : ROWS + 1, :, CH : 2 * CH] = block
    table[slot, 1 : ROWS + 1, :, 2 * CH : 3 * CH] = after if forward else before


def fill_own_table(table, slot, block):
    wide = block.astype(F32)
    for tap in range(3):
        moved = pltpu.roll(wide, WIN - (EDGE + 1 - tap), axis=1)
        table[slot, 1 : ROWS + 1, :, tap * CH : (tap + 1) * CH] = moved[:, :OWN].astype(BF16)


def clear_border(table):
    frames, _, columns, lanes = table.shape
    border = jnp.zeros((frames, columns, lanes), BF16)
    table[:, 0] = border
    table[:, ROWS + 1] = border


def own_columns(block):
    return pltpu.roll(block.astype(F32), WIN - EDGE, axis=1)[:, :OWN]


def forward_taps(table, frames, weights, total):
    step = pl.program_id(0)
    for tap in range(3):
        lhs = table[pl.ds(step, frames), tap : tap + ROWS].reshape(frames * ROWS * WIN, 3 * CH)
        total[...] += nn(lhs, weights[0, tap].reshape(3 * CH, CH))


def backward_taps(table, start, frames, columns, weights, total):
    step = pl.program_id(0)
    for tap_h in range(3):
        part = None
        for tap_w in range(3):
            lanes = slice(tap_w * CH, (tap_w + 1) * CH)
            lhs = table[pl.ds(start + 2 - step, frames), 2 - tap_h : 2 - tap_h + ROWS, :, lanes]
            more = nt(lhs.reshape(frames * ROWS * columns, CH), weights[0, tap_h, tap_w])
            part = more if part is None else part + more
        total[...] += part


def frame_of(total, frame, columns):
    rows = ROWS * columns
    return total[frame * rows : (frame + 1) * rows].reshape(ROWS, columns, CH)


def first_kernel(block, weights, mask, act, slope, table, total):
    @pl.when(pl.program_id(0) == 0)
    def _():
        clear_border(table)
        for core in range(2):
            for frame in range(FR):
                slot = 2 * core + frame if frame < 2 else 2 + 2 * core + frame
                fill_table(table, slot, block[core, :, frame], True)
        total[...] = jnp.zeros_like(total)

    forward_taps(table, FR + 2, weights, total)

    @pl.when(pl.program_id(0) == 2)
    def _():
        for frame in range(FR + 2):
            values = frame_of(total, frame, WIN)
            sigma = jax.nn.sigmoid(values)
            act[frame] = (values * sigma * mask[...]).astype(BF16)
            if frame >= 2:
                slope[frame - 2] = slope_of(values, sigma)


def second_kernel(act, features, weights, summed, up_act, table, total):
    @pl.when(pl.program_id(0) == 0)
    def _():
        clear_border(table)
        for frame in range(FR + 2):
            fill_table(table, frame, act[frame], True)
        total[...] = jnp.zeros_like(total)

    forward_taps(table, FR, weights, total)

    @pl.when(pl.program_id(0) == 2)
    def _():
        for frame in range(FR):
            values = frame_of(total, frame, WIN) + features[frame // 2, :, 2 + frame % 2].astype(F32)
            summed[frame] = values
            up_act[frame] = (values * jax.nn.sigmoid(values)).astype(BF16)


def hidden_kernel(block, later, slope, weights, mask, grad_hidden, head, table, total):
    @pl.when(pl.program_id(0) == 0)
    def _():
        clear_border(table)
        for frame in range(FR):
            fill_table(table, frame, block[frame], False)
        for frame in range(2):
            fill_table(table, FR + frame, later[frame], False)
        total[...] = jnp.zeros_like(total)

    backward_taps(table, 0, FR, WIN, weights, total)

    @pl.when(pl.program_id(0) == 2)
    def _():
        for frame in range(FR):
            result = (frame_of(total, frame, WIN) * slope[frame] * mask[...]).astype(BF16)
            grad_hidden[frame] = result
            if frame < 2:
                head[frame] = result


def features_kernel(core_ref, block, later, grad_sum, weights, grad_features, table, total):
    core = core_ref[0]

    @pl.when(pl.program_id(0) == 0)
    def _():
        clear_border(table)
        for frame in range(FR):
            fill_own_table(table, frame, block[frame])
        for frame in range(2):
            fill_own_table(table, FR + frame, later[frame])
        total[...] = jnp.zeros_like(total)

    backward_taps(table, 2 * core, 2, OWN, weights, total)

    @pl.when(pl.program_id(0) == 2)
    def _():
        for frame in range(2):
            values = frame_of(total, frame, OWN) + own_columns(grad_sum[2 * core + frame])
            grad_features[:, frame] = values.astype(BF16)


def cotangent_kernel(core_ref, mine, other, weights, summed, mask, grad_sum, head, table):
    core = core_ref[0]
    border = jnp.zeros((FR, WIN, 4 * CH), BF16)
    table[:, 0, 0] = border
    table[:, ROWS, 1] = border
    for source, which in ((mine, core), (other, 1 - core)):
        for frame in range(2):
            slot = 2 * which + frame
            for parity in range(2):
                fine = source[:, frame, :, parity].reshape(ROWS, WIN, 2 * CH)
                even, odd = fine[:, :, :CH], fine[:, :, CH:]
                before = pltpu.roll(odd.astype(F32), 1, axis=1).astype(BF16)
                after = pltpu.roll(even.astype(F32), WIN - 1, axis=1).astype(BF16)
                low = 0 if parity == 0 else 1
                put = (slot, slice(low, low + ROWS), 1 - parity)
                table[put + (slice(None), slice(0, CH))] = before
                table[put + (slice(None), slice(CH, 2 * CH))] = even
                table[put + (slice(None), slice(2 * CH, 3 * CH))] = odd
                table[put + (slice(None), slice(3 * CH, 4 * CH))] = after
    for frame in range(FR):
        part = None
        for tap in range(4):
            for column in range(4):
                lhs = table[frame, tap // 2 : tap // 2 + ROWS, tap % 2, :, column * CH : (column + 1) * CH]
                more = nt(lhs.reshape(ROWS * WIN, CH), weights[tap, column])
                part = more if part is None else part + more
        grad_act = part.reshape(ROWS, WIN, CH).astype(BF16).astype(F32)
        values = summed[frame]
        grad = grad_act * slope_of(values, jax.nn.sigmoid(values)) * mask[...]
        grad_sum[frame] = grad.astype(BF16)
        if frame < 2:
            head[frame] = grad.astype(BF16)


def up_grad_kernel(core_ref, act, mine, other, out, table, flipped):
    core = core_ref[0]
    border = jnp.zeros((FR, OWN, 4 * CH), BF16)
    table[:, 0, 0] = border
    table[:, ROWS, 1] = border
    for source, which in ((mine, core), (other, 1 - core)):
        for frame in range(2):
            slot = 2 * which + frame
            for parity in range(2):
                fine = source[:, frame, :, parity].reshape(ROWS, WIN, 2 * CH).astype(F32)
                even, odd = fine[:, :, :CH], fine[:, :, CH:]
                low = 0 if parity == 0 else 1
                put = (slot, slice(low, low + ROWS), 1 - parity)
                for column, (values, shift) in enumerate(((odd, -1), (even, 0), (odd, 0), (even, 1))):
                    moved = pltpu.roll(values, WIN - (EDGE + shift), axis=1)[:, :OWN].astype(BF16)
                    table[put + (slice(None), slice(column * CH, (column + 1) * CH))] = moved
    for frame in range(FR):
        rows = ROWS * OWN
        flipped[:, frame * rows : (frame + 1) * rows] = jnp.transpose(
            own_columns(act[frame]).reshape(rows, CH)
        ).astype(BF16)
    lanes = pl.ds(pl.multiple_of(core * 2 * CH, 2 * CH), 2 * CH)
    for tap in range(4):
        rhs = table[:, tap // 2 : tap // 2 + ROWS, tap % 2, :, lanes]
        result = nn(flipped[...], rhs.reshape(FR * ROWS * OWN, 2 * CH))
        for half in range(2):
            for piece in range(8):
                out[tap * 16 + half * 8 + piece] = result[
                    piece * 32 : (piece + 1) * 32, half * CH : (half + 1) * CH
                ].astype(BF16)


def tap_sums(act_of, block, later, table, flipped, sums):
    clear_border(table)
    for frame in range(FR):
        fill_own_table(table, frame, block[frame])
    for frame in range(2):
        fill_own_table(table, FR + frame, later[frame])
    for frame in range(FR):
        rows = ROWS * OWN
        flipped[:, frame * rows : (frame + 1) * rows] = jnp.transpose(
            own_columns(act_of(frame)).reshape(rows, CH)
        ).astype(BF16)
    sums[TAPS * CH :] = jnp.zeros((8, CH), F32)
    for tap_t in range(3):
        for tap_h in range(3):
            rhs = table[2 - tap_t : 2 - tap_t + FR, 2 - tap_h : 2 - tap_h + ROWS]
            result = nn(flipped[...], rhs.reshape(FR * ROWS * OWN, 3 * CH))
            for tap_w in range(3):
                at = (tap_t * 9 + tap_h * 3 + tap_w) * CH
                sums[at : at + CH] = result[:, tap_w * CH : (tap_w + 1) * CH]


def piece_of(sums, owner, member):
    at = SHARE * member
    start = pl.multiple_of(16 * SHARE * owner + at // 8 * 8, 8)
    return sums[pl.ds(start, PIECE + 8)][at % 8 : at % 8 + PIECE]


def second_grad_kernel(place, act, block, later, up, out, table, flipped, sums):
    tap_sums(lambda frame: act[2 + frame], block, later, table, flipped, sums)
    for step in range(4):
        group = lax.rem(place[1] + step, 4)
        for member in range(16):
            chunk = member * 4 + step
            out[chunk, :UP_ROWS] = up[group * 16 + member]
            out[chunk, UP_ROWS:] = piece_of(sums, 2 * group + place[0], member).astype(BF16)


def first_grad_kernel(place, act, block, later, own, next_one, next_two, next_three, table, flipped, sums):
    tap_sums(lambda frame: act[frame // 2, :, 2 + frame % 2], block, later, table, flipped, sums)
    for step, out in enumerate((own, next_one, next_two, next_three)):
        group = lax.rem(place[1] + step, 4)
        for member in range(16):
            out[member] = piece_of(sums, 2 * group + place[0], member).astype(BF16)


def whole(shape):
    zeros = (0,) * len(shape)
    return pl.BlockSpec(shape, lambda *_: zeros)


SMEM = pl.BlockSpec(memory_space=pltpu.SMEM)


def tap_weights():
    return pl.BlockSpec((1, 3, 3, CH, CH), lambda step: (step, 0, 0, 0, 0))


def call(kernel, grid, args, specs, outs, scratch, flops):
    shapes = [jax.ShapeDtypeStruct(shape, dtype) for shape, dtype in outs]
    moved = sum(math.prod(a.shape) * a.dtype.itemsize for a in args)
    moved += sum(math.prod(s.shape) * s.dtype.itemsize for s in shapes)
    single = len(shapes) == 1
    return pl.pallas_call(
        kernel,
        out_shape=shapes[0] if single else shapes,
        grid=grid,
        in_specs=specs,
        out_specs=whole(shapes[0].shape) if single else [whole(s.shape) for s in shapes],
        scratch_shapes=scratch,
        compiler_params=pltpu.CompilerParams(vmem_limit_bytes=VMEM_LIMIT),
        cost_estimate=pl.CostEstimate(flops=int(flops), bytes_accessed=moved, transcendentals=0),
    )(*args)


def shift(value, axis, step):
    count = lax.axis_size(axis)
    return lax.ppermute(value, axis, [(i, i + step) for i in range(count) if 0 <= i + step < count])


def over_y(value, step):
    return lax.ppermute(value, "y", [(i, (i + step) % 4) for i in range(4)])


def shards(features, conv_first, conv_second, up_kernel, cotangent):
    core = lax.axis_index("core")
    height = 2 * lax.axis_index("z") + lax.axis_index("x_hi")
    width = lax.axis_index("width")
    core_arg = core.astype(jnp.int32).reshape(1)
    place = jnp.stack([core, lax.axis_index("y")]).astype(jnp.int32)
    window = 8 * width + height
    columns = OWN * window - EDGE + jnp.arange(WIN)
    inside = ((columns >= 0) & (columns < 128)).astype(F32)
    mask = jnp.broadcast_to(inside[:, None], (WIN, CH))
    act_shape = (FR, ROWS, WIN, CH)
    two_frames = (2, ROWS, WIN, CH)
    six_frames = (FR + 2, ROWS, WIN, CH)
    table = pltpu.VMEM((FR + 2, ROWS + 2, WIN, 3 * CH), BF16)
    own_table = pltpu.VMEM((FR + 2, ROWS + 2, OWN, 3 * CH), BF16)
    total = pltpu.VMEM((FR * ROWS * WIN, CH), F32)
    tap_flops = 2 * FR * ROWS * WIN * CH * CH

    frames = features[:, 0]
    frames = jnp.concatenate([shift(frames, "y", 1), frames], axis=0)
    padded = jnp.pad(frames, ((0, 0), (EDGE, EDGE), (0, 0))).reshape(4, 17, OWN, CH)
    windows = jnp.concatenate([padded[:, :-1], padded[:, 1:]], axis=2)
    windows = windows.reshape(4, 2, 8, WIN, CH).transpose(2, 1, 0, 3, 4).reshape(1, 16, 4, WIN, CH)
    windows = jnp.broadcast_to(windows, (2, 16, 4, WIN, CH)).reshape(32, 4, WIN, CH)
    block = lax.all_to_all(windows, ("core", "z", "x_hi", "width"), 0, 0, tiled=True)

    paired, _ = lax.optimization_barrier((cotangent, windows))
    paired = paired.reshape(2, 4, 64, 2 * CH)
    edge = jnp.where(width == 0, paired[:, :, 64 - EDGE :], paired[:, :, :EDGE])
    edge = lax.ppermute(edge, "width", [(0, 1), (1, 0)])
    nothing = jnp.zeros_like(edge)
    low, high = jnp.where(width == 0, nothing, edge), jnp.where(width == 0, edge, nothing)
    paired = jnp.concatenate([low, paired, high], axis=2).reshape(2, 4, 9, OWN, 2 * CH)
    fine = jnp.concatenate([paired[:, :, :-1], paired[:, :, 1:]], axis=3).transpose(2, 0, 1, 3, 4)
    fine, block = lax.optimization_barrier((fine, block))
    block = block.reshape(2, ROWS, 4, WIN, CH)
    mine = lax.all_to_all(fine, ("z", "x_hi"), 0, 0, tiled=True).reshape(8, 2, 2, 2, WIN, 2 * CH)

    first_act, first_slope = call(
        first_kernel, (3,), (block, conv_first, mask),
        [whole(block.shape), tap_weights(), whole(mask.shape)],
        [(six_frames, BF16), (act_shape, F32)],
        [pltpu.VMEM((FR + 4, ROWS + 2, WIN, 3 * CH), BF16), pltpu.VMEM(((FR + 2) * ROWS * WIN, CH), F32)],
        40 * tap_flops,
    )
    mine, first_slope = lax.optimization_barrier((mine, first_slope))
    other = lax.ppermute(mine, "core", [(0, 1), (1, 0)])
    summed, up_act = call(
        second_kernel, (3,), (first_act, block, conv_second),
        [whole(six_frames), whole(block.shape), tap_weights()],
        [(act_shape, F32), (act_shape, BF16)], [table, total], 27 * tap_flops,
    )
    grad_sum, sum_head = call(
        cotangent_kernel, (), (core_arg, mine, other, up_kernel, summed, mask),
        [SMEM, whole(mine.shape), whole(mine.shape), whole(up_kernel.shape), whole(act_shape), whole(mask.shape)],
        [(act_shape, BF16), (two_frames, BF16)], [pltpu.VMEM((FR, ROWS + 1, 2, WIN, 4 * CH), BF16)], 16 * tap_flops,
    )
    later = shift(sum_head, "y", -1)
    up_act, grad_sum = lax.optimization_barrier((up_act, grad_sum))
    up_part = call(
        up_grad_kernel, (), (core_arg, up_act, mine, other),
        [SMEM, whole(act_shape), whole(mine.shape), whole(mine.shape)],
        [((64, 32, CH), BF16)],
        [pltpu.VMEM((FR, ROWS + 1, 2, OWN, 4 * CH), BF16), pltpu.VMEM((CH, FR * ROWS * OWN), BF16)], 4 * tap_flops,
    )
    grad_scratch = [own_table, pltpu.VMEM((CH, FR * ROWS * OWN), BF16), pltpu.VMEM((TAPS * CH + 8, CH), F32)]
    early = call(
        second_grad_kernel, (), (place, first_act, grad_sum, later, up_part),
        [SMEM, whole(six_frames), whole(act_shape), whole(later.shape), whole(up_part.shape)],
        [((64, UP_ROWS + PIECE, CH), BF16)], grad_scratch, 14 * tap_flops,
    )
    early = lax.all_to_all(early, ("z", "x_hi", "width"), 0, 0, tiled=True)

    grad_hidden, hidden_head = call(
        hidden_kernel, (3,), (grad_sum, later, first_slope, conv_second, mask),
        [whole(act_shape), whole(later.shape), whole(act_shape), tap_weights(), whole(mask.shape)],
        [(act_shape, BF16), (two_frames, BF16)], [table, total], 27 * tap_flops,
    )
    later_hidden = shift(hidden_head, "y", -1)
    blocks = call(
        first_grad_kernel, (), (place, block, grad_hidden, later_hidden),
        [SMEM, whole(block.shape), whole(act_shape), whole(later_hidden.shape)],
        [((16, PIECE, CH), BF16)] * 4, grad_scratch, 14 * tap_flops,
    )
    arrived = [blocks[0]]
    for step in (2, 1, 3):
        arrived.append(over_y(blocks[step], step))
    tied_hidden, _ = lax.optimization_barrier((grad_hidden, blocks[0]))
    rows_out = call(
        features_kernel, (3,), (core_arg, tied_hidden, later_hidden, grad_sum, conv_first),
        [SMEM, whole(act_shape), whole(later_hidden.shape), whole(act_shape), tap_weights()],
        [((ROWS, 2, OWN, CH), BF16)], [own_table, pltpu.VMEM((2 * ROWS * OWN, CH), F32)], 7 * tap_flops,
    )

    tied_rows, early = lax.optimization_barrier((rows_out, early))
    early = jnp.sum(early.reshape(16, 4, UP_ROWS + PIECE, CH).astype(F32), axis=0)
    early_total = early[0]
    for step in (2, 1, 3):
        early_total += over_y(early[step].astype(BF16), step).astype(F32)
    first_sum = sum(value.astype(F32) for value in arrived).astype(BF16)
    late = jnp.concatenate([tied_rows.reshape(16, 2 * OWN, CH), first_sum], axis=1)
    late = lax.all_to_all(late, ("z", "x_hi", "width"), 0, 0, tiled=True)

    factor = 1.0 / math.sqrt(32768)
    early = early_total * factor
    returned = late[:, : 2 * OWN].reshape(8, 2, 2, OWN, CH).transpose(2, 1, 0, 3, 4)
    first_share = jnp.sum(late[:, 2 * OWN : 2 * OWN + SHARE].astype(F32), axis=0) * factor
    return (
        returned.reshape(2, 1, 128, CH),
        first_share.reshape(-1),
        early[UP_ROWS : UP_ROWS + SHARE].reshape(-1),
        early[:UP_ROWS].reshape(-1),
    )


def solution(mesh):
    names = ("y", "core", "z", "x_hi", "width")
    split = Mesh(mesh.devices.reshape(4, 2, 4, 2, 2), names)
    tm, height = ("y", "core"), ("z", "x_hi")
    in_specs = (
        P(tm, (*height, "width"), None, None),
        P(),
        P(),
        P(),
        P(tm, height, "width", None),
    )
    flat = P(names)
    out_specs = (P(tm, (*height, "width"), None, None), flat, flat, flat)
    return jax.shard_map(shards, mesh=split, in_specs=in_specs, out_specs=out_specs, check_vma=False)
```

```python
import math

import jax
import jax.numpy as jnp
from jax import lax
from jax.experimental import pallas as pl
from jax.experimental.pallas import tpu as pltpu
from jax.sharding import Mesh, PartitionSpec as P

F32 = jnp.float32
BF16 = jnp.bfloat16
VMEM_LIMIT = 48 * 1024 * 1024

FR = 4
ROWS = 16
WIN = 16
OWN = 8
EDGE = 4
CH = 256
TAPS = 27
SHARE = 54
PIECE = 56
UP_ROWS = 32


def slope_of(values, sigma):
    return sigma * (1.0 + values * (1.0 - sigma))


def nt(lhs, rhs):
    return lax.dot_general(lhs, rhs, (((1,), (1,)), ((), ())), preferred_element_type=F32)


def nn(lhs, rhs):
    return jnp.dot(lhs, rhs, preferred_element_type=F32)


def fill_table(table, slot, block, forward):
    wide = block.astype(F32)
    before = pltpu.roll(wide, 1, axis=1).astype(BF16)
    after = pltpu.roll(wide, WIN - 1, axis=1).astype(BF16)
    table[slot, 1 : ROWS + 1, :, 0:CH] = before if forward else after
    table[slot, 1 : ROWS + 1, :, CH : 2 * CH] = block
    table[slot, 1 : ROWS + 1, :, 2 * CH : 3 * CH] = after if forward else before


def fill_own_table(table, slot, block):
    wide = block.astype(F32)
    for tap in range(3):
        moved = pltpu.roll(wide, WIN - (EDGE + 1 - tap), axis=1)
        table[slot, 1 : ROWS + 1, :, tap * CH : (tap + 1) * CH] = moved[:, :OWN].astype(BF16)


def clear_border(table):
    frames, _, columns, lanes = table.shape
    border = jnp.zeros((frames, columns, lanes), BF16)
    table[:, 0] = border
    table[:, ROWS + 1] = border


def own_columns(block):
    return pltpu.roll(block.astype(F32), WIN - EDGE, axis=1)[:, :OWN]


def forward_taps(table, frames, weights, total):
    step = pl.program_id(0)
    for tap in range(3):
        lhs = table[pl.ds(step, frames), tap : tap + ROWS].reshape(frames * ROWS * WIN, 3 * CH)
        total[...] += nn(lhs, weights[0, tap].reshape(3 * CH, CH))


def backward_taps(table, start, frames, columns, weights, total):
    step = pl.program_id(0)
    for tap_h in range(3):
        part = None
        for tap_w in range(3):
            lanes = slice(tap_w * CH, (tap_w + 1) * CH)
            lhs = table[pl.ds(start + 2 - step, frames), 2 - tap_h : 2 - tap_h + ROWS, :, lanes]
            more = nt(lhs.reshape(frames * ROWS * columns, CH), weights[0, tap_h, tap_w])
            part = more if part is None else part + more
        total[...] += part


def frame_of(total, frame, columns):
    rows = ROWS * columns
    return total[frame * rows : (frame + 1) * rows].reshape(ROWS, columns, CH)


def first_kernel(block, weights, mask, act, slope, table, total):
    @pl.when(pl.program_id(0) == 0)
    def _():
        clear_border(table)
        for core in range(2):
            for frame in range(FR):
                slot = 2 * core + frame if frame < 2 else 2 + 2 * core + frame
                fill_table(table, slot, block[core, :, frame], True)
        total[...] = jnp.zeros_like(total)

    forward_taps(table, FR + 2, weights, total)

    @pl.when(pl.program_id(0) == 2)
    def _():
        for frame in range(FR + 2):
            values = frame_of(total, frame, WIN)
            sigma = jax.nn.sigmoid(values)
            act[frame] = (values * sigma * mask[...]).astype(BF16)
            if frame >= 2:
                slope[frame - 2] = slope_of(values, sigma)


def second_kernel(act, features, weights, summed, up_act, table, total):
    @pl.when(pl.program_id(0) == 0)
    def _():
        clear_border(table)
        for frame in range(FR + 2):
            fill_table(table, frame, act[frame], True)
        total[...] = jnp.zeros_like(total)

    forward_taps(table, FR, weights, total)

    @pl.when(pl.program_id(0) == 2)
    def _():
        for frame in range(FR):
            values = frame_of(total, frame, WIN) + features[frame // 2, :, 2 + frame % 2].astype(F32)
            summed[frame] = values
            up_act[frame] = (values * jax.nn.sigmoid(values)).astype(BF16)


def hidden_kernel(block, later, slope, weights, mask, grad_hidden, head, table, total):
    @pl.when(pl.program_id(0) == 0)
    def _():
        clear_border(table)
        for frame in range(FR):
            fill_table(table, frame, block[frame], False)
        for frame in range(2):
            fill_table(table, FR + frame, later[frame], False)
        total[...] = jnp.zeros_like(total)

    backward_taps(table, 0, FR, WIN, weights, total)

    @pl.when(pl.program_id(0) == 2)
    def _():
        for frame in range(FR):
            result = (frame_of(total, frame, WIN) * slope[frame] * mask[...]).astype(BF16)
            grad_hidden[frame] = result
            if frame < 2:
                head[frame] = result


def features_kernel(core_ref, block, later, grad_sum, weights, grad_features, table, total):
    core = core_ref[0]

    @pl.when(pl.program_id(0) == 0)
    def _():
        clear_border(table)
        for frame in range(FR):
            fill_own_table(table, frame, block[frame])
        for frame in range(2):
            fill_own_table(table, FR + frame, later[frame])
        total[...] = jnp.zeros_like(total)

    backward_taps(table, 2 * core, 2, OWN, weights, total)

    @pl.when(pl.program_id(0) == 2)
    def _():
        for frame in range(2):
            values = frame_of(total, frame, OWN) + own_columns(grad_sum[2 * core + frame])
            grad_features[:, frame] = values.astype(BF16)


def cotangent_kernel(core_ref, mine, other, weights, summed, mask, grad_sum, head, table):
    core = core_ref[0]
    border = jnp.zeros((FR, WIN, 4 * CH), BF16)
    table[:, 0, 0] = border
    table[:, ROWS, 1] = border
    for source, which in ((mine, core), (other, 1 - core)):
        for frame in range(2):
            slot = 2 * which + frame
            for parity in range(2):
                fine = source[:, frame, :, parity].reshape(ROWS, WIN, 2 * CH)
                even, odd = fine[:, :, :CH], fine[:, :, CH:]
                before = pltpu.roll(odd.astype(F32), 1, axis=1).astype(BF16)
                after = pltpu.roll(even.astype(F32), WIN - 1, axis=1).astype(BF16)
                low = 0 if parity == 0 else 1
                put = (slot, slice(low, low + ROWS), 1 - parity)
                table[put + (slice(None), slice(0, CH))] = before
                table[put + (slice(None), slice(CH, 2 * CH))] = even
                table[put + (slice(None), slice(2 * CH, 3 * CH))] = odd
                table[put + (slice(None), slice(3 * CH, 4 * CH))] = after
    for frame in range(FR):
        part = None
        for tap in range(4):
            for column in range(4):
                lhs = table[frame, tap // 2 : tap // 2 + ROWS, tap % 2, :, column * CH : (column + 1) * CH]
                more = nt(lhs.reshape(ROWS * WIN, CH), weights[tap, column])
                part = more if part is None else part + more
        grad_act = part.reshape(ROWS, WIN, CH).astype(BF16).astype(F32)
        values = summed[frame]
        grad = grad_act * slope_of(values, jax.nn.sigmoid(values)) * mask[...]
        grad_sum[frame] = grad.astype(BF16)
        if frame < 2:
            head[frame] = grad.astype(BF16)


def up_grad_kernel(core_ref, act, mine, other, out, table, flipped):
    core = core_ref[0]
    border = jnp.zeros((FR, OWN, 4 * CH), BF16)
    table[:, 0, 0] = border
    table[:, ROWS, 1] = border
    for source, which in ((mine, core), (other, 1 - core)):
        for frame in range(2):
            slot = 2 * which + frame
            for parity in range(2):
                fine = source[:, frame, :, parity].reshape(ROWS, WIN, 2 * CH).astype(F32)
                even, odd = fine[:, :, :CH], fine[:, :, CH:]
                low = 0 if parity == 0 else 1
                put = (slot, slice(low, low + ROWS), 1 - parity)
                for column, (values, shift) in enumerate(((odd, -1), (even, 0), (odd, 0), (even, 1))):
                    moved = pltpu.roll(values, WIN - (EDGE + shift), axis=1)[:, :OWN].astype(BF16)
                    table[put + (slice(None), slice(column * CH, (column + 1) * CH))] = moved
    for frame in range(FR):
        rows = ROWS * OWN
        flipped[:, frame * rows : (frame + 1) * rows] = jnp.transpose(
            own_columns(act[frame]).reshape(rows, CH)
        ).astype(BF16)
    lanes = pl.ds(pl.multiple_of(core * 2 * CH, 2 * CH), 2 * CH)
    for tap in range(4):
        rhs = table[:, tap // 2 : tap // 2 + ROWS, tap % 2, :, lanes]
        result = nn(flipped[...], rhs.reshape(FR * ROWS * OWN, 2 * CH))
        for half in range(2):
            for piece in range(8):
                out[tap * 16 + half * 8 + piece] = result[
                    piece * 32 : (piece + 1) * 32, half * CH : (half + 1) * CH
                ].astype(BF16)


def tap_sums(act_of, block, table, flipped, sums):
    clear_border(table)
    column = lax.broadcasted_iota(jnp.int32, (ROWS, WIN, CH), 1)
    own = (column >= EDGE) & (column < EDGE + OWN)
    for frame in range(FR):
        fill_table(table, frame, jnp.where(own, block[frame].astype(F32), 0.0).astype(BF16), False)
    rows = ROWS * WIN
    for frame in range(FR + 2):
        values = act_of(frame).astype(F32).reshape(rows, CH)
        flipped[:, frame * rows : (frame + 1) * rows] = jnp.transpose(values).astype(BF16)
    sums[TAPS * CH :] = jnp.zeros((8, CH), F32)
    for tap_t in range(3):
        lhs = flipped[:, tap_t * rows : (tap_t + FR) * rows]
        for tap_h in range(3):
            rhs = table[:, 2 - tap_h : 2 - tap_h + ROWS]
            result = nn(lhs, rhs.reshape(FR * rows, 3 * CH))
            for tap_w in range(3):
                at = (tap_t * 9 + tap_h * 3 + tap_w) * CH
                sums[at : at + CH] = result[:, tap_w * CH : (tap_w + 1) * CH]


def piece_of(sums, owner, member):
    at = SHARE * member
    start = pl.multiple_of(16 * SHARE * owner + at // 8 * 8, 8)
    return sums[pl.ds(start, PIECE + 8)][at % 8 : at % 8 + PIECE]


def second_grad_kernel(place, act, block, up, out, table, flipped, sums):
    tap_sums(lambda frame: act[frame], block, table, flipped, sums)
    for step in range(4):
        group = lax.rem(place[1] + step, 4)
        for member in range(16):
            chunk = member * 4 + step
            out[chunk, :UP_ROWS] = up[group * 16 + member]
            out[chunk, UP_ROWS:] = piece_of(sums, 2 * group + place[0], member).astype(BF16)


def first_grad_kernel(place, act, block, own, next_one, next_two, next_three, table, flipped, sums):
    def frame_at(frame):
        return act[1, :, frame] if frame < 2 else act[(frame - 2) // 2, :, 2 + frame % 2]

    tap_sums(frame_at, block, table, flipped, sums)
    for step, out in enumerate((own, next_one, next_two, next_three)):
        group = lax.rem(place[1] + step, 4)
        for member in range(16):
            out[member] = piece_of(sums, 2 * group + place[0], member).astype(BF16)


def whole(shape):
    zeros = (0,) * len(shape)
    return pl.BlockSpec(shape, lambda *_: zeros)


SMEM = pl.BlockSpec(memory_space=pltpu.SMEM)


def tap_weights():
    return pl.BlockSpec((1, 3, 3, CH, CH), lambda step: (step, 0, 0, 0, 0))


def call(kernel, grid, args, specs, outs, scratch, flops):
    shapes = [jax.ShapeDtypeStruct(shape, dtype) for shape, dtype in outs]
    moved = sum(math.prod(a.shape) * a.dtype.itemsize for a in args)
    moved += sum(math.prod(s.shape) * s.dtype.itemsize for s in shapes)
    single = len(shapes) == 1
    return pl.pallas_call(
        kernel,
        out_shape=shapes[0] if single else shapes,
        grid=grid,
        in_specs=specs,
        out_specs=whole(shapes[0].shape) if single else [whole(s.shape) for s in shapes],
        scratch_shapes=scratch,
        compiler_params=pltpu.CompilerParams(vmem_limit_bytes=VMEM_LIMIT),
        cost_estimate=pl.CostEstimate(flops=int(flops), bytes_accessed=moved, transcendentals=0),
    )(*args)


def shift(value, axis, step):
    count = lax.axis_size(axis)
    return lax.ppermute(value, axis, [(i, i + step) for i in range(count) if 0 <= i + step < count])


def over_y(value, step):
    return lax.ppermute(value, "y", [(i, (i + step) % 4) for i in range(4)])


def shards(features, conv_first, conv_second, up_kernel, cotangent):
    core = lax.axis_index("core")
    height = 2 * lax.axis_index("z") + lax.axis_index("x_hi")
    width = lax.axis_index("width")
    core_arg = core.astype(jnp.int32).reshape(1)
    place = jnp.stack([core, lax.axis_index("y")]).astype(jnp.int32)
    window = 8 * width + height
    columns = OWN * window - EDGE + jnp.arange(WIN)
    inside = ((columns >= 0) & (columns < 128)).astype(F32)
    mask = jnp.broadcast_to(inside[:, None], (WIN, CH))
    act_shape = (FR, ROWS, WIN, CH)
    two_frames = (2, ROWS, WIN, CH)
    six_frames = (FR + 2, ROWS, WIN, CH)
    table = pltpu.VMEM((FR + 2, ROWS + 2, WIN, 3 * CH), BF16)
    own_table = pltpu.VMEM((FR + 2, ROWS + 2, OWN, 3 * CH), BF16)
    total = pltpu.VMEM((FR * ROWS * WIN, CH), F32)
    tap_flops = 2 * FR * ROWS * WIN * CH * CH

    paired = cotangent.reshape(2, 4, 64, 2 * CH)
    edge = jnp.where(width == 0, paired[:, :, 64 - EDGE :], paired[:, :, :EDGE])
    edge = lax.ppermute(edge, "width", [(0, 1), (1, 0)])
    frames = features[:, 0]
    before, edge = lax.optimization_barrier((shift(frames, "y", 1), edge))
    frames = jnp.concatenate([before, frames], axis=0)
    padded = jnp.pad(frames, ((0, 0), (EDGE, EDGE), (0, 0))).reshape(4, 17, OWN, CH)
    windows = jnp.concatenate([padded[:, :-1], padded[:, 1:]], axis=2)
    windows = windows.reshape(4, 2, 8, WIN, CH).transpose(2, 1, 0, 3, 4).reshape(1, 16, 4, WIN, CH)
    windows = jnp.broadcast_to(windows, (2, 16, 4, WIN, CH)).reshape(32, 4, WIN, CH)
    block = lax.all_to_all(windows, ("core", "z", "x_hi", "width"), 0, 0, tiled=True)

    nothing = jnp.zeros_like(edge)
    low, high = jnp.where(width == 0, nothing, edge), jnp.where(width == 0, edge, nothing)
    paired = jnp.concatenate([low, paired, high], axis=2).reshape(2, 4, 9, OWN, 2 * CH)
    fine = jnp.concatenate([paired[:, :, :-1], paired[:, :, 1:]], axis=3).transpose(2, 0, 1, 3, 4)
    fine, block = lax.optimization_barrier((fine, block))
    block = block.reshape(2, ROWS, 4, WIN, CH)
    mine = lax.all_to_all(fine, ("z", "x_hi"), 0, 0, tiled=True).reshape(8, 2, 2, 2, WIN, 2 * CH)

    first_act, first_slope = call(
        first_kernel, (3,), (block, conv_first, mask),
        [whole(block.shape), tap_weights(), whole(mask.shape)],
        [(six_frames, BF16), (act_shape, F32)],
        [pltpu.VMEM((FR + 4, ROWS + 2, WIN, 3 * CH), BF16), pltpu.VMEM(((FR + 2) * ROWS * WIN, CH), F32)],
        40 * tap_flops,
    )
    mine, first_slope = lax.optimization_barrier((mine, first_slope))
    other = lax.ppermute(mine, "core", [(0, 1), (1, 0)])
    summed, up_act = call(
        second_kernel, (3,), (first_act, block, conv_second),
        [whole(six_frames), whole(block.shape), tap_weights()],
        [(act_shape, F32), (act_shape, BF16)], [table, total], 27 * tap_flops,
    )
    grad_sum, sum_head = call(
        cotangent_kernel, (), (core_arg, mine, other, up_kernel, summed, mask),
        [SMEM, whole(mine.shape), whole(mine.shape), whole(up_kernel.shape), whole(act_shape), whole(mask.shape)],
        [(act_shape, BF16), (two_frames, BF16)], [pltpu.VMEM((FR, ROWS + 1, 2, WIN, 4 * CH), BF16)], 16 * tap_flops,
    )
    later = shift(sum_head, "y", -1)
    up_act, grad_sum = lax.optimization_barrier((up_act, grad_sum))
    up_part = call(
        up_grad_kernel, (), (core_arg, up_act, mine, other),
        [SMEM, whole(act_shape), whole(mine.shape), whole(mine.shape)],
        [((64, 32, CH), BF16)],
        [pltpu.VMEM((FR, ROWS + 1, 2, OWN, 4 * CH), BF16), pltpu.VMEM((CH, FR * ROWS * OWN), BF16)], 4 * tap_flops,
    )
    grad_table = pltpu.VMEM((FR, ROWS + 2, WIN, 3 * CH), BF16)
    grad_scratch = [grad_table, pltpu.VMEM((CH, (FR + 2) * ROWS * WIN), BF16), pltpu.VMEM((TAPS * CH + 8, CH), F32)]
    early = call(
        second_grad_kernel, (), (place, first_act, grad_sum, up_part),
        [SMEM, whole(six_frames), whole(act_shape), whole(up_part.shape)],
        [((64, UP_ROWS + PIECE, CH), BF16)], grad_scratch, 27 * tap_flops,
    )
    early, later = lax.optimization_barrier((early, later))
    early = lax.all_to_all(early, ("z", "x_hi", "width"), 0, 0, tiled=True)

    grad_hidden, hidden_head = call(
        hidden_kernel, (3,), (grad_sum, later, first_slope, conv_second, mask),
        [whole(act_shape), whole(later.shape), whole(act_shape), tap_weights(), whole(mask.shape)],
        [(act_shape, BF16), (two_frames, BF16)], [table, total], 27 * tap_flops,
    )
    later_hidden = shift(hidden_head, "y", -1)
    blocks = call(
        first_grad_kernel, (), (place, block, grad_hidden),
        [SMEM, whole(block.shape), whole(act_shape)],
        [((16, PIECE, CH), BF16)] * 4, grad_scratch, 27 * tap_flops,
    )
    arrived = [blocks[0]]
    for step in (2, 1, 3):
        arrived.append(over_y(blocks[step], step))
    tied_hidden, _ = lax.optimization_barrier((grad_hidden, blocks[0]))
    rows_out = call(
        features_kernel, (3,), (core_arg, tied_hidden, later_hidden, grad_sum, conv_first),
        [SMEM, whole(act_shape), whole(later_hidden.shape), whole(act_shape), tap_weights()],
        [((ROWS, 2, OWN, CH), BF16)], [own_table, pltpu.VMEM((2 * ROWS * OWN, CH), F32)], 7 * tap_flops,
    )

    tied_rows, early = lax.optimization_barrier((rows_out, early))
    early = jnp.sum(early.reshape(16, 4, UP_ROWS + PIECE, CH).astype(F32), axis=0)
    early_total = early[0]
    for step in (2, 1, 3):
        early_total += over_y(early[step].astype(BF16), step).astype(F32)
    first_sum = sum(value.astype(F32) for value in arrived).astype(BF16)
    late = jnp.concatenate([tied_rows.reshape(16, 2 * OWN, CH), first_sum], axis=1)
    late = lax.all_to_all(late, ("z", "x_hi", "width"), 0, 0, tiled=True)

    factor = 1.0 / math.sqrt(32768)
    early = early_total * factor
    returned = late[:, : 2 * OWN].reshape(8, 2, 2, OWN, CH).transpose(2, 1, 0, 3, 4)
    first_share = jnp.sum(late[:, 2 * OWN : 2 * OWN + SHARE].astype(F32), axis=0) * factor
    return (
        returned.reshape(2, 1, 128, CH),
        first_share.reshape(-1),
        early[UP_ROWS : UP_ROWS + SHARE].reshape(-1),
        early[:UP_ROWS].reshape(-1),
    )


def solution(mesh):
    names = ("y", "core", "z", "x_hi", "width")
    split = Mesh(mesh.devices.reshape(4, 2, 4, 2, 2), names)
    tm, height = ("y", "core"), ("z", "x_hi")
    in_specs = (
        P(tm, (*height, "width"), None, None),
        P(),
        P(),
        P(),
        P(tm, height, "width", None),
    )
    flat = P(names)
    out_specs = (P(tm, (*height, "width"), None, None), flat, flat, flat)
    return jax.shard_map(shards, mesh=split, in_specs=in_specs, out_specs=out_specs, check_vma=False)
```

```python
import math

import jax
import jax.numpy as jnp
from jax import lax
from jax.experimental import pallas as pl
from jax.experimental.pallas import tpu as pltpu
from jax.sharding import Mesh, PartitionSpec as P

F32 = jnp.float32
BF16 = jnp.bfloat16
VMEM_LIMIT = 48 * 1024 * 1024

FR = 4
ROWS = 16
WIN = 16
OWN = 8
EDGE = 4
CH = 256
TAPS = 27
SHARE = 54
PIECE = 56
UP_ROWS = 32


def slope_of(values, sigma):
    return sigma * (1.0 + values * (1.0 - sigma))


def nt(lhs, rhs):
    return lax.dot_general(lhs, rhs, (((1,), (1,)), ((), ())), preferred_element_type=F32)


def nn(lhs, rhs):
    return jnp.dot(lhs, rhs, preferred_element_type=F32)


def fill_table(table, slot, block, forward):
    wide = block.astype(F32)
    before = pltpu.roll(wide, 1, axis=1).astype(BF16)
    after = pltpu.roll(wide, WIN - 1, axis=1).astype(BF16)
    table[slot, 1 : ROWS + 1, :, 0:CH] = before if forward else after
    table[slot, 1 : ROWS + 1, :, CH : 2 * CH] = block
    table[slot, 1 : ROWS + 1, :, 2 * CH : 3 * CH] = after if forward else before


def fill_own_table(table, slot, block):
    wide = block.astype(F32)
    for tap in range(3):
        moved = pltpu.roll(wide, WIN - (EDGE + 1 - tap), axis=1)
        table[slot, 1 : ROWS + 1, :, tap * CH : (tap + 1) * CH] = moved[:, :OWN].astype(BF16)


def clear_border(table):
    frames, _, columns, lanes = table.shape
    border = jnp.zeros((frames, columns, lanes), BF16)
    table[:, 0] = border
    table[:, ROWS + 1] = border


def own_columns(block):
    return pltpu.roll(block.astype(F32), WIN - EDGE, axis=1)[:, :OWN]


def forward_taps(table, step, frames, weights, total):
    rows = frames * ROWS * WIN
    for tap in range(3):
        lhs = table[pl.ds(step, frames), tap : tap + ROWS].reshape(rows, 3 * CH)
        total[:rows] += nn(lhs, weights[0, tap].reshape(3 * CH, CH))


def backward_taps(table, start, frames, columns, weights, total):
    step = pl.program_id(0)
    for tap_h in range(3):
        part = None
        for tap_w in range(3):
            lanes = slice(tap_w * CH, (tap_w + 1) * CH)
            lhs = table[pl.ds(start + 2 - step, frames), 2 - tap_h : 2 - tap_h + ROWS, :, lanes]
            more = nt(lhs.reshape(frames * ROWS * columns, CH), weights[0, tap_h, tap_w])
            part = more if part is None else part + more
        total[...] += part


def frame_of(total, frame, columns):
    rows = ROWS * columns
    return total[frame * rows : (frame + 1) * rows].reshape(ROWS, columns, CH)


def forward_kernel(core_ref, mine, other, first, second, mask, act, slope, summed, up_act, table, total):
    step = pl.program_id(0)
    core = core_ref[0]
    sources = ((mine, core), (other, 1 - core))

    @pl.when(step == 0)
    def _():
        clear_border(table)
        for source, which in sources:
            for frame in range(FR):
                slot = 2 * which + (frame if frame < 2 else frame + 2)
                fill_table(table, slot, source[:, frame], True)
        total[...] = jnp.zeros_like(total)

    @pl.when(step < 3)
    def _():
        forward_taps(table, step, FR + 2, first, total)

    @pl.when(step == 2)
    def _():
        for frame in range(FR + 2):
            values = frame_of(total, frame, WIN)
            sigma = jax.nn.sigmoid(values)
            result = (values * sigma * mask[...]).astype(BF16)
            act[frame] = result
            fill_table(table, frame, result, True)
            if frame >= 2:
                slope[frame - 2] = slope_of(values, sigma)
        total[...] = jnp.zeros_like(total)

    @pl.when(step >= 3)
    def _():
        forward_taps(table, step - 3, FR, second, total)

    @pl.when(step == 5)
    def _():
        rows = ROWS * WIN
        for source, which in sources:
            for frame in range(2):
                place = 2 * which + frame
                values = total[pl.ds(pl.multiple_of(place * rows, rows), rows)].reshape(ROWS, WIN, CH)
                values = values + source[:, 2 + frame].astype(F32)
                summed[place] = values
                up_act[place] = (values * jax.nn.sigmoid(values)).astype(BF16)


def hidden_kernel(block, later, slope, weights, mask, grad_hidden, head, table, total):
    @pl.when(pl.program_id(0) == 0)
    def _():
        clear_border(table)
        for frame in range(FR):
            fill_table(table, frame, block[frame], False)
        for frame in range(2):
            fill_table(table, FR + frame, later[frame], False)
        total[...] = jnp.zeros_like(total)

    backward_taps(table, 0, FR, WIN, weights, total)

    @pl.when(pl.program_id(0) == 2)
    def _():
        for frame in range(FR):
            result = (frame_of(total, frame, WIN) * slope[frame] * mask[...]).astype(BF16)
            grad_hidden[frame] = result
            if frame < 2:
                head[frame] = result


def features_kernel(core_ref, block, later, grad_sum, weights, grad_features, table, total):
    core = core_ref[0]

    @pl.when(pl.program_id(0) == 0)
    def _():
        clear_border(table)
        for frame in range(FR):
            fill_own_table(table, frame, block[frame])
        for frame in range(2):
            fill_own_table(table, FR + frame, later[frame])
        total[...] = jnp.zeros_like(total)

    backward_taps(table, 2 * core, 2, OWN, weights, total)

    @pl.when(pl.program_id(0) == 2)
    def _():
        for frame in range(2):
            values = frame_of(total, frame, OWN) + own_columns(grad_sum[2 * core + frame])
            grad_features[:, frame] = values.astype(BF16)


def cotangent_kernel(core_ref, mine, other, weights, summed, mask, grad_sum, head, table):
    core = core_ref[0]
    border = jnp.zeros((FR, WIN, 4 * CH), BF16)
    table[:, 0, 0] = border
    table[:, ROWS, 1] = border
    for source, which in ((mine, core), (other, 1 - core)):
        for frame in range(2):
            slot = 2 * which + frame
            for parity in range(2):
                fine = source[:, frame, :, parity].reshape(ROWS, WIN, 2 * CH)
                even, odd = fine[:, :, :CH], fine[:, :, CH:]
                before = pltpu.roll(odd.astype(F32), 1, axis=1).astype(BF16)
                after = pltpu.roll(even.astype(F32), WIN - 1, axis=1).astype(BF16)
                low = 0 if parity == 0 else 1
                put = (slot, slice(low, low + ROWS), 1 - parity)
                table[put + (slice(None), slice(0, CH))] = before
                table[put + (slice(None), slice(CH, 2 * CH))] = even
                table[put + (slice(None), slice(2 * CH, 3 * CH))] = odd
                table[put + (slice(None), slice(3 * CH, 4 * CH))] = after
    for frame in range(FR):
        part = None
        for tap in range(4):
            for column in range(4):
                lhs = table[frame, tap // 2 : tap // 2 + ROWS, tap % 2, :, column * CH : (column + 1) * CH]
                more = nt(lhs.reshape(ROWS * WIN, CH), weights[tap, column])
                part = more if part is None else part + more
        grad_act = part.reshape(ROWS, WIN, CH).astype(BF16).astype(F32)
        values = summed[frame]
        grad = grad_act * slope_of(values, jax.nn.sigmoid(values)) * mask[...]
        grad_sum[frame] = grad.astype(BF16)
        if frame < 2:
            head[frame] = grad.astype(BF16)


def up_grad_kernel(core_ref, act, mine, other, out, table, flipped):
    core = core_ref[0]
    border = jnp.zeros((FR, OWN, 4 * CH), BF16)
    table[:, 0, 0] = border
    table[:, ROWS, 1] = border
    for source, which in ((mine, core), (other, 1 - core)):
        for frame in range(2):
            slot = 2 * which + frame
            for parity in range(2):
                fine = source[:, frame, :, parity].reshape(ROWS, WIN, 2 * CH).astype(F32)
                even, odd = fine[:, :, :CH], fine[:, :, CH:]
                low = 0 if parity == 0 else 1
                put = (slot, slice(low, low + ROWS), 1 - parity)
                for column, (values, shift) in enumerate(((odd, -1), (even, 0), (odd, 0), (even, 1))):
                    moved = pltpu.roll(values, WIN - (EDGE + shift), axis=1)[:, :OWN].astype(BF16)
                    table[put + (slice(None), slice(column * CH, (column + 1) * CH))] = moved
    for frame in range(FR):
        rows = ROWS * OWN
        flipped[:, frame * rows : (frame + 1) * rows] = jnp.transpose(
            own_columns(act[frame]).reshape(rows, CH)
        ).astype(BF16)
    lanes = pl.ds(pl.multiple_of(core * 2 * CH, 2 * CH), 2 * CH)
    for tap in range(4):
        rhs = table[:, tap // 2 : tap // 2 + ROWS, tap % 2, :, lanes]
        result = nn(flipped[...], rhs.reshape(FR * ROWS * OWN, 2 * CH))
        for half in range(2):
            for piece in range(8):
                out[tap * 16 + half * 8 + piece] = result[
                    piece * 32 : (piece + 1) * 32, half * CH : (half + 1) * CH
                ].astype(BF16)


def tap_sums(frames, block, table, flipped, sums):
    clear_border(table)
    column = lax.broadcasted_iota(jnp.int32, (ROWS, WIN, CH), 1)
    own = (column >= EDGE) & (column < EDGE + OWN)
    for frame in range(FR):
        fill_table(table, frame, jnp.where(own, block[frame].astype(F32), 0.0).astype(BF16), False)
    rows = ROWS * WIN
    for slot, values in frames:
        lanes = pl.ds(pl.multiple_of(slot * rows, rows), rows)
        flipped[:, lanes] = jnp.transpose(values.astype(F32).reshape(rows, CH)).astype(BF16)
    sums[TAPS * CH :] = jnp.zeros((8, CH), F32)
    for tap_t in range(3):
        lhs = flipped[:, tap_t * rows : (tap_t + FR) * rows]
        for tap_h in range(3):
            rhs = table[:, 2 - tap_h : 2 - tap_h + ROWS]
            result = nn(lhs, rhs.reshape(FR * rows, 3 * CH))
            for tap_w in range(3):
                at = (tap_t * 9 + tap_h * 3 + tap_w) * CH
                sums[at : at + CH] = result[:, tap_w * CH : (tap_w + 1) * CH]


def piece_of(sums, owner, member):
    at = SHARE * member
    start = pl.multiple_of(16 * SHARE * owner + at // 8 * 8, 8)
    return sums[pl.ds(start, PIECE + 8)][at % 8 : at % 8 + PIECE]


def second_grad_kernel(place, act, block, up, out, table, flipped, sums):
    tap_sums([(frame, act[frame]) for frame in range(FR + 2)], block, table, flipped, sums)
    for step in range(4):
        group = lax.rem(place[1] + step, 4)
        for member in range(16):
            chunk = member * 4 + step
            out[chunk, :UP_ROWS] = up[group * 16 + member]
            out[chunk, UP_ROWS:] = piece_of(sums, 2 * group + place[0], member).astype(BF16)


def first_grad_kernel(place, mine, other, block, own, next_one, next_two, next_three, table, flipped, sums):
    core = place[0]
    frames = []
    for frame in range(2):
        before = jnp.where(core == 1, mine[:, frame].astype(F32), other[:, frame].astype(F32))
        frames.append((frame, before))
        frames.append((2 + 2 * core + frame, mine[:, 2 + frame]))
        frames.append((4 - 2 * core + frame, other[:, 2 + frame]))
    tap_sums(frames, block, table, flipped, sums)
    for step, out in enumerate((own, next_one, next_two, next_three)):
        group = lax.rem(place[1] + step, 4)
        for member in range(16):
            out[member] = piece_of(sums, 2 * group + place[0], member).astype(BF16)


def whole(shape):
    zeros = (0,) * len(shape)
    return pl.BlockSpec(shape, lambda *_: zeros)


SMEM = pl.BlockSpec(memory_space=pltpu.SMEM)


def tap_weights(begin=0):
    return pl.BlockSpec((1, 3, 3, CH, CH), lambda step: (jnp.clip(step - begin, 0, 2), 0, 0, 0, 0))


def call(kernel, grid, args, specs, outs, scratch, flops):
    shapes = [jax.ShapeDtypeStruct(shape, dtype) for shape, dtype in outs]
    moved = sum(math.prod(a.shape) * a.dtype.itemsize for a in args)
    moved += sum(math.prod(s.shape) * s.dtype.itemsize for s in shapes)
    single = len(shapes) == 1
    return pl.pallas_call(
        kernel,
        out_shape=shapes[0] if single else shapes,
        grid=grid,
        in_specs=specs,
        out_specs=whole(shapes[0].shape) if single else [whole(s.shape) for s in shapes],
        scratch_shapes=scratch,
        compiler_params=pltpu.CompilerParams(vmem_limit_bytes=VMEM_LIMIT),
        cost_estimate=pl.CostEstimate(flops=int(flops), bytes_accessed=moved, transcendentals=0),
    )(*args)


def shift(value, axis, step):
    count = lax.axis_size(axis)
    return lax.ppermute(value, axis, [(i, i + step) for i in range(count) if 0 <= i + step < count])


def over_y(value, step):
    return lax.ppermute(value, "y", [(i, (i + step) % 4) for i in range(4)])


def shards(features, conv_first, conv_second, up_kernel, cotangent):
    core = lax.axis_index("core")
    height = 2 * lax.axis_index("z") + lax.axis_index("x_hi")
    width = lax.axis_index("width")
    core_arg = core.astype(jnp.int32).reshape(1)
    place = jnp.stack([core, lax.axis_index("y")]).astype(jnp.int32)
    window = 8 * width + height
    columns = OWN * window - EDGE + jnp.arange(WIN)
    inside = ((columns >= 0) & (columns < 128)).astype(F32)
    mask = jnp.broadcast_to(inside[:, None], (WIN, CH))
    act_shape = (FR, ROWS, WIN, CH)
    two_frames = (2, ROWS, WIN, CH)
    six_frames = (FR + 2, ROWS, WIN, CH)
    table = pltpu.VMEM((FR + 2, ROWS + 2, WIN, 3 * CH), BF16)
    own_table = pltpu.VMEM((FR + 2, ROWS + 2, OWN, 3 * CH), BF16)
    total = pltpu.VMEM((FR * ROWS * WIN, CH), F32)
    tap_flops = 2 * FR * ROWS * WIN * CH * CH

    paired = cotangent.reshape(2, 4, 64, 2 * CH)
    edge = jnp.where(width == 0, paired[:, :, 64 - EDGE :], paired[:, :, :EDGE])
    edge = lax.ppermute(edge, "width", [(0, 1), (1, 0)])
    frames = features[:, 0]
    before, edge = lax.optimization_barrier((shift(frames, "y", 1), edge))
    frames = jnp.concatenate([before, frames], axis=0)
    padded = jnp.pad(frames, ((0, 0), (EDGE, EDGE), (0, 0))).reshape(4, 17, OWN, CH)
    windows = jnp.concatenate([padded[:, :-1], padded[:, 1:]], axis=2)
    windows = windows.reshape(4, 2, 8, WIN, CH).transpose(2, 1, 0, 3, 4).reshape(16, 4, WIN, CH)
    block = lax.all_to_all(windows, ("z", "x_hi", "width"), 0, 0, tiled=True)

    nothing = jnp.zeros_like(edge)
    low, high = jnp.where(width == 0, nothing, edge), jnp.where(width == 0, edge, nothing)
    paired = jnp.concatenate([low, paired, high], axis=2).reshape(2, 4, 9, OWN, 2 * CH)
    fine = jnp.concatenate([paired[:, :, :-1], paired[:, :, 1:]], axis=3).transpose(2, 0, 1, 3, 4)
    fine, block = lax.optimization_barrier((fine, block))
    swap = [(0, 1), (1, 0)]
    other_block = lax.ppermute(block, "core", swap)
    mine = lax.all_to_all(fine, ("z", "x_hi"), 0, 0, tiled=True).reshape(8, 2, 2, 2, WIN, 2 * CH)

    first_act, first_slope, summed, up_act = call(
        forward_kernel, (6,), (core_arg, block, other_block, conv_first, conv_second, mask),
        [SMEM, whole(block.shape), whole(block.shape), tap_weights(0), tap_weights(3), whole(mask.shape)],
        [(six_frames, BF16), (act_shape, F32), (act_shape, F32), (act_shape, BF16)],
        [pltpu.VMEM((FR + 4, ROWS + 2, WIN, 3 * CH), BF16), pltpu.VMEM(((FR + 2) * ROWS * WIN, CH), F32)],
        67 * tap_flops,
    )
    mine, up_act = lax.optimization_barrier((mine, up_act))
    other = lax.ppermute(mine, "core", swap)
    grad_sum, sum_head = call(
        cotangent_kernel, (), (core_arg, mine, other, up_kernel, summed, mask),
        [SMEM, whole(mine.shape), whole(mine.shape), whole(up_kernel.shape), whole(act_shape), whole(mask.shape)],
        [(act_shape, BF16), (two_frames, BF16)], [pltpu.VMEM((FR, ROWS + 1, 2, WIN, 4 * CH), BF16)], 16 * tap_flops,
    )
    later = shift(sum_head, "y", -1)
    up_act, grad_sum = lax.optimization_barrier((up_act, grad_sum))
    up_part = call(
        up_grad_kernel, (), (core_arg, up_act, mine, other),
        [SMEM, whole(act_shape), whole(mine.shape), whole(mine.shape)],
        [((64, 32, CH), BF16)],
        [pltpu.VMEM((FR, ROWS + 1, 2, OWN, 4 * CH), BF16), pltpu.VMEM((CH, FR * ROWS * OWN), BF16)], 4 * tap_flops,
    )
    grad_table = pltpu.VMEM((FR, ROWS + 2, WIN, 3 * CH), BF16)
    grad_scratch = [grad_table, pltpu.VMEM((CH, (FR + 2) * ROWS * WIN), BF16), pltpu.VMEM((TAPS * CH + 8, CH), F32)]
    early = call(
        second_grad_kernel, (), (place, first_act, grad_sum, up_part),
        [SMEM, whole(six_frames), whole(act_shape), whole(up_part.shape)],
        [((64, UP_ROWS + PIECE, CH), BF16)], grad_scratch, 27 * tap_flops,
    )
    early, later = lax.optimization_barrier((early, later))
    early = lax.all_to_all(early, ("z", "x_hi", "width"), 0, 0, tiled=True)

    grad_hidden, hidden_head = call(
        hidden_kernel, (3,), (grad_sum, later, first_slope, conv_second, mask),
        [whole(act_shape), whole(later.shape), whole(act_shape), tap_weights(), whole(mask.shape)],
        [(act_shape, BF16), (two_frames, BF16)], [table, total], 27 * tap_flops,
    )
    later_hidden = shift(hidden_head, "y", -1)
    blocks = call(
        first_grad_kernel, (), (place, block, other_block, grad_hidden),
        [SMEM, whole(block.shape), whole(block.shape), whole(act_shape)],
        [((16, PIECE, CH), BF16)] * 4, grad_scratch, 27 * tap_flops,
    )
    arrived = [blocks[0]]
    for step in (2, 1, 3):
        arrived.append(over_y(blocks[step], step))
    tied_hidden, _ = lax.optimization_barrier((grad_hidden, blocks[0]))
    rows_out = call(
        features_kernel, (3,), (core_arg, tied_hidden, later_hidden, grad_sum, conv_first),
        [SMEM, whole(act_shape), whole(later_hidden.shape), whole(act_shape), tap_weights()],
        [((ROWS, 2, OWN, CH), BF16)], [own_table, pltpu.VMEM((2 * ROWS * OWN, CH), F32)], 7 * tap_flops,
    )

    tied_rows, early = lax.optimization_barrier((rows_out, early))
    early = jnp.sum(early.reshape(16, 4, UP_ROWS + PIECE, CH).astype(F32), axis=0)
    early_total = early[0]
    for step in (2, 1, 3):
        early_total += over_y(early[step].astype(BF16), step).astype(F32)
    first_sum = sum(value.astype(F32) for value in arrived).astype(BF16)
    late = jnp.concatenate([tied_rows.reshape(16, 2 * OWN, CH), first_sum], axis=1)
    late = lax.all_to_all(late, ("z", "x_hi", "width"), 0, 0, tiled=True)

    factor = 1.0 / math.sqrt(32768)
    early = early_total * factor
    returned = late[:, : 2 * OWN].reshape(8, 2, 2, OWN, CH).transpose(2, 1, 0, 3, 4)
    first_share = jnp.sum(late[:, 2 * OWN : 2 * OWN + SHARE].astype(F32), axis=0) * factor
    return (
        returned.reshape(2, 1, 128, CH),
        first_share.reshape(-1),
        early[UP_ROWS : UP_ROWS + SHARE].reshape(-1),
        early[:UP_ROWS].reshape(-1),
    )


def solution(mesh):
    names = ("y", "core", "z", "x_hi", "width")
    split = Mesh(mesh.devices.reshape(4, 2, 4, 2, 2), names)
    tm, height = ("y", "core"), ("z", "x_hi")
    in_specs = (
        P(tm, (*height, "width"), None, None),
        P(),
        P(),
        P(),
        P(tm, height, "width", None),
    )
    flat = P(names)
    out_specs = (P(tm, (*height, "width"), None, None), flat, flat, flat)
    return jax.shard_map(shards, mesh=split, in_specs=in_specs, out_specs=out_specs, check_vma=False)
```

```python
import math

import jax
import jax.numpy as jnp
from jax import lax
from jax.experimental import pallas as pl
from jax.experimental.pallas import tpu as pltpu
from jax.sharding import Mesh, PartitionSpec as P

F32 = jnp.float32
BF16 = jnp.bfloat16
VMEM_LIMIT = 48 * 1024 * 1024

FR = 4
ROWS = 16
WIN = 16
OWN = 8
EDGE = 4
CH = 256
TAPS = 27
SHARE = 54
PIECE = 56
UP_ROWS = 32


def slope_of(values, sigma):
    return sigma * (1.0 + values * (1.0 - sigma))


def nt(lhs, rhs):
    return lax.dot_general(lhs, rhs, (((1,), (1,)), ((), ())), preferred_element_type=F32)


def nn(lhs, rhs):
    return jnp.dot(lhs, rhs, preferred_element_type=F32)


def fill_table(table, slot, block, forward):
    wide = block.astype(F32)
    before = pltpu.roll(wide, 1, axis=1).astype(BF16)
    after = pltpu.roll(wide, WIN - 1, axis=1).astype(BF16)
    table[slot, 1 : ROWS + 1, :, 0:CH] = before if forward else after
    table[slot, 1 : ROWS + 1, :, CH : 2 * CH] = block
    table[slot, 1 : ROWS + 1, :, 2 * CH : 3 * CH] = after if forward else before


def fill_own_table(table, slot, block):
    wide = block.astype(F32)
    for tap in range(3):
        moved = pltpu.roll(wide, WIN - (EDGE + 1 - tap), axis=1)
        table[slot, 1 : ROWS + 1, :, tap * CH : (tap + 1) * CH] = moved[:, :OWN].astype(BF16)


def clear_border(table):
    frames, _, columns, lanes = table.shape
    border = jnp.zeros((frames, columns, lanes), BF16)
    table[:, 0] = border
    table[:, ROWS + 1] = border


def own_columns(block):
    return pltpu.roll(block.astype(F32), WIN - EDGE, axis=1)[:, :OWN]


def forward_taps(table, step, frames, weights, total):
    rows = frames * ROWS * WIN
    for tap in range(3):
        lhs = table[pl.ds(step, frames), tap : tap + ROWS].reshape(rows, 3 * CH)
        total[:rows] += nn(lhs, weights[0, tap].reshape(3 * CH, CH))


def backward_taps(table, start, frames, columns, weights, total):
    step = pl.program_id(0)
    for tap_h in range(3):
        part = None
        for tap_w in range(3):
            lanes = slice(tap_w * CH, (tap_w + 1) * CH)
            lhs = table[pl.ds(start + 2 - step, frames), 2 - tap_h : 2 - tap_h + ROWS, :, lanes]
            more = nt(lhs.reshape(frames * ROWS * columns, CH), weights[0, tap_h, tap_w])
            part = more if part is None else part + more
        total[...] += part


def frame_of(total, frame, columns):
    rows = ROWS * columns
    return total[frame * rows : (frame + 1) * rows].reshape(ROWS, columns, CH)


def forward_kernel(core_ref, mine, other, first, second, mask, act, slope, late_slope, up_act, table, total):
    step = pl.program_id(0)
    core = core_ref[0]
    sources = ((mine, core), (other, 1 - core))

    @pl.when(step == 0)
    def _():
        clear_border(table)
        for source, which in sources:
            for frame in range(FR):
                slot = 2 * which + (frame if frame < 2 else frame + 2)
                fill_table(table, slot, source[:, frame], True)
        total[...] = jnp.zeros_like(total)

    @pl.when(step < 3)
    def _():
        forward_taps(table, step, FR + 2, first, total)

    @pl.when(step == 2)
    def _():
        for frame in range(FR + 2):
            values = frame_of(total, frame, WIN)
            sigma = jax.nn.sigmoid(values)
            result = (values * sigma * mask[...]).astype(BF16)
            act[frame] = result
            fill_table(table, frame, result, True)
            if frame >= 2:
                slope[frame - 2] = slope_of(values, sigma).astype(BF16)
        total[...] = jnp.zeros_like(total)

    @pl.when(step >= 3)
    def _():
        forward_taps(table, step - 3, FR, second, total)

    @pl.when(step == 5)
    def _():
        rows = ROWS * WIN
        for source, which in sources:
            for frame in range(2):
                place = 2 * which + frame
                values = total[pl.ds(pl.multiple_of(place * rows, rows), rows)].reshape(ROWS, WIN, CH)
                values = values + source[:, 2 + frame].astype(F32)
                sigma = jax.nn.sigmoid(values)
                late_slope[place] = slope_of(values, sigma).astype(BF16)
                up_act[place] = (values * sigma).astype(BF16)


def hidden_kernel(block, later, slope, weights, mask, grad_hidden, head, table, total):
    @pl.when(pl.program_id(0) == 0)
    def _():
        clear_border(table)
        for frame in range(FR):
            fill_table(table, frame, block[frame], False)
        for frame in range(2):
            fill_table(table, FR + frame, later[frame], False)
        total[...] = jnp.zeros_like(total)

    backward_taps(table, 0, FR, WIN, weights, total)

    @pl.when(pl.program_id(0) == 2)
    def _():
        for frame in range(FR):
            result = (frame_of(total, frame, WIN) * slope[frame].astype(F32) * mask[...]).astype(BF16)
            grad_hidden[frame] = result
            if frame < 2:
                head[frame] = result


def features_kernel(core_ref, block, later, grad_sum, weights, grad_features, table, total):
    core = core_ref[0]

    @pl.when(pl.program_id(0) == 0)
    def _():
        clear_border(table)
        for frame in range(FR):
            fill_own_table(table, frame, block[frame])
        for frame in range(2):
            fill_own_table(table, FR + frame, later[frame])
        total[...] = jnp.zeros_like(total)

    backward_taps(table, 2 * core, 2, OWN, weights, total)

    @pl.when(pl.program_id(0) == 2)
    def _():
        for frame in range(2):
            values = frame_of(total, frame, OWN) + own_columns(grad_sum[2 * core + frame])
            grad_features[:, frame] = values.astype(BF16)


def cotangent_kernel(core_ref, mine, other, weights, slope, mask, grad_sum, head, table):
    core = core_ref[0]
    border = jnp.zeros((FR, WIN, 4 * CH), BF16)
    table[:, 0, 0] = border
    table[:, ROWS, 1] = border
    for source, which in ((mine, core), (other, 1 - core)):
        for frame in range(2):
            slot = 2 * which + frame
            for parity in range(2):
                fine = source[:, frame, :, parity].reshape(ROWS, WIN, 2 * CH)
                even, odd = fine[:, :, :CH], fine[:, :, CH:]
                before = pltpu.roll(odd.astype(F32), 1, axis=1).astype(BF16)
                after = pltpu.roll(even.astype(F32), WIN - 1, axis=1).astype(BF16)
                low = 0 if parity == 0 else 1
                put = (slot, slice(low, low + ROWS), 1 - parity)
                table[put + (slice(None), slice(0, CH))] = before
                table[put + (slice(None), slice(CH, 2 * CH))] = even
                table[put + (slice(None), slice(2 * CH, 3 * CH))] = odd
                table[put + (slice(None), slice(3 * CH, 4 * CH))] = after
    for frame in range(FR):
        part = None
        for tap in range(4):
            for column in range(4):
                lhs = table[frame, tap // 2 : tap // 2 + ROWS, tap % 2, :, column * CH : (column + 1) * CH]
                more = nt(lhs.reshape(ROWS * WIN, CH), weights[tap, column])
                part = more if part is None else part + more
        grad_act = part.reshape(ROWS, WIN, CH).astype(BF16).astype(F32)
        grad = grad_act * slope[frame].astype(F32) * mask[...]
        grad_sum[frame] = grad.astype(BF16)
        if frame < 2:
            head[frame] = grad.astype(BF16)


def up_grad_kernel(core_ref, act, mine, other, out, table, flipped):
    core = core_ref[0]
    border = jnp.zeros((FR, OWN, 4 * CH), BF16)
    table[:, 0, 0] = border
    table[:, ROWS, 1] = border
    for source, which in ((mine, core), (other, 1 - core)):
        for frame in range(2):
            slot = 2 * which + frame
            for parity in range(2):
                fine = source[:, frame, :, parity].reshape(ROWS, WIN, 2 * CH).astype(F32)
                even, odd = fine[:, :, :CH], fine[:, :, CH:]
                low = 0 if parity == 0 else 1
                put = (slot, slice(low, low + ROWS), 1 - parity)
                for column, (values, shift) in enumerate(((odd, -1), (even, 0), (odd, 0), (even, 1))):
                    moved = pltpu.roll(values, WIN - (EDGE + shift), axis=1)[:, :OWN].astype(BF16)
                    table[put + (slice(None), slice(column * CH, (column + 1) * CH))] = moved
    for frame in range(FR):
        rows = ROWS * OWN
        flipped[:, frame * rows : (frame + 1) * rows] = jnp.transpose(
            own_columns(act[frame]).reshape(rows, CH)
        ).astype(BF16)
    lanes = pl.ds(pl.multiple_of(core * 2 * CH, 2 * CH), 2 * CH)
    for tap in range(4):
        rhs = table[:, tap // 2 : tap // 2 + ROWS, tap % 2, :, lanes]
        result = nn(flipped[...], rhs.reshape(FR * ROWS * OWN, 2 * CH))
        for half in range(2):
            for piece in range(8):
                out[tap * 16 + half * 8 + piece] = result[
                    piece * 32 : (piece + 1) * 32, half * CH : (half + 1) * CH
                ].astype(BF16)


def owners_of(tap):
    first, last = tap * CH // (16 * SHARE), ((tap + 1) * CH - 1) // (16 * SHARE)
    return sorted({k % 2 for k in range(first, last + 1)})


def tap_sums(core, frames, block, table, flipped, sums):
    clear_border(table)
    column = lax.broadcasted_iota(jnp.int32, (ROWS, WIN, CH), 1)
    own = (column >= EDGE) & (column < EDGE + OWN)
    for frame in range(FR):
        fill_table(table, frame, jnp.where(own, block[frame].astype(F32), 0.0).astype(BF16), False)
    rows = ROWS * WIN
    for slot, values in frames:
        lanes = pl.ds(pl.multiple_of(slot * rows, rows), rows)
        flipped[:, lanes] = jnp.transpose(values.astype(F32).reshape(rows, CH)).astype(BF16)
    sums[TAPS * CH :] = jnp.zeros((8, CH), F32)
    for tap_t in range(3):
        lhs = flipped[:, tap_t * rows : (tap_t + FR) * rows]
        for tap_h in range(3):
            for tap_w in range(3):

                def fill(tap_h=tap_h, tap_w=tap_w, at=(tap_t * 9 + tap_h * 3 + tap_w) * CH, lhs=lhs):
                    rhs = table[:, 2 - tap_h : 2 - tap_h + ROWS, :, tap_w * CH : (tap_w + 1) * CH]
                    sums[at : at + CH] = nn(lhs, rhs.reshape(FR * rows, CH))

                owners = owners_of(tap_t * 9 + tap_h * 3 + tap_w)
                if len(owners) == 2:
                    fill()
                else:
                    pl.when(core == owners[0])(fill)


def piece_of(sums, owner, member):
    at = SHARE * member
    start = pl.multiple_of(16 * SHARE * owner + at // 8 * 8, 8)
    return sums[pl.ds(start, PIECE + 8)][at % 8 : at % 8 + PIECE]


def second_grad_kernel(place, act, block, up, out, table, flipped, sums):
    tap_sums(place[0], [(frame, act[frame]) for frame in range(FR + 2)], block, table, flipped, sums)
    for step in range(4):
        group = lax.rem(place[1] + step, 4)
        for member in range(16):
            chunk = member * 4 + step
            out[chunk, :UP_ROWS] = up[group * 16 + member]
            out[chunk, UP_ROWS:] = piece_of(sums, 2 * group + place[0], member).astype(BF16)


def first_grad_kernel(place, mine, other, block, own, next_one, next_two, next_three, table, flipped, sums):
    core = place[0]
    frames = []
    for frame in range(2):
        before = jnp.where(core == 1, mine[:, frame].astype(F32), other[:, frame].astype(F32))
        frames.append((frame, before))
        frames.append((2 + 2 * core + frame, mine[:, 2 + frame]))
        frames.append((4 - 2 * core + frame, other[:, 2 + frame]))
    tap_sums(core, frames, block, table, flipped, sums)
    for step, out in enumerate((own, next_one, next_two, next_three)):
        group = lax.rem(place[1] + step, 4)
        for member in range(16):
            out[member] = piece_of(sums, 2 * group + place[0], member).astype(BF16)


def whole(shape):
    zeros = (0,) * len(shape)
    return pl.BlockSpec(shape, lambda *_: zeros)


SMEM = pl.BlockSpec(memory_space=pltpu.SMEM)


def tap_weights(begin=0):
    return pl.BlockSpec((1, 3, 3, CH, CH), lambda step: (jnp.clip(step - begin, 0, 2), 0, 0, 0, 0))


def call(kernel, grid, args, specs, outs, scratch, flops):
    shapes = [jax.ShapeDtypeStruct(shape, dtype) for shape, dtype in outs]
    moved = sum(math.prod(a.shape) * a.dtype.itemsize for a in args)
    moved += sum(math.prod(s.shape) * s.dtype.itemsize for s in shapes)
    single = len(shapes) == 1
    return pl.pallas_call(
        kernel,
        out_shape=shapes[0] if single else shapes,
        grid=grid,
        in_specs=specs,
        out_specs=whole(shapes[0].shape) if single else [whole(s.shape) for s in shapes],
        scratch_shapes=scratch,
        compiler_params=pltpu.CompilerParams(vmem_limit_bytes=VMEM_LIMIT),
        cost_estimate=pl.CostEstimate(flops=int(flops), bytes_accessed=moved, transcendentals=0),
    )(*args)


def shift(value, axis, step):
    count = lax.axis_size(axis)
    return lax.ppermute(value, axis, [(i, i + step) for i in range(count) if 0 <= i + step < count])


def over_y(value, step):
    return lax.ppermute(value, "y", [(i, (i + step) % 4) for i in range(4)])


def shards(features, conv_first, conv_second, up_kernel, cotangent):
    core = lax.axis_index("core")
    height = 2 * lax.axis_index("z") + lax.axis_index("x_hi")
    width = lax.axis_index("width")
    core_arg = core.astype(jnp.int32).reshape(1)
    place = jnp.stack([core, lax.axis_index("y")]).astype(jnp.int32)
    window = 8 * width + height
    columns = OWN * window - EDGE + jnp.arange(WIN)
    inside = ((columns >= 0) & (columns < 128)).astype(F32)
    mask = jnp.broadcast_to(inside[:, None], (WIN, CH))
    act_shape = (FR, ROWS, WIN, CH)
    two_frames = (2, ROWS, WIN, CH)
    six_frames = (FR + 2, ROWS, WIN, CH)
    table = pltpu.VMEM((FR + 2, ROWS + 2, WIN, 3 * CH), BF16)
    own_table = pltpu.VMEM((FR + 2, ROWS + 2, OWN, 3 * CH), BF16)
    total = pltpu.VMEM((FR * ROWS * WIN, CH), F32)
    tap_flops = 2 * FR * ROWS * WIN * CH * CH

    paired = cotangent.reshape(2, 4, 64, 2 * CH)
    edge = jnp.where(width == 0, paired[:, :, 64 - EDGE :], paired[:, :, :EDGE])
    edge = lax.ppermute(edge, "width", [(0, 1), (1, 0)])
    frames = features[:, 0]
    before, edge = lax.optimization_barrier((shift(frames, "y", 1), edge))
    frames = jnp.concatenate([before, frames], axis=0)
    padded = jnp.pad(frames, ((0, 0), (EDGE, EDGE), (0, 0))).reshape(4, 17, OWN, CH)
    windows = jnp.concatenate([padded[:, :-1], padded[:, 1:]], axis=2)
    windows = windows.reshape(4, 2, 8, WIN, CH).transpose(2, 1, 0, 3, 4).reshape(16, 4, WIN, CH)
    block = lax.all_to_all(windows, ("z", "x_hi", "width"), 0, 0, tiled=True)

    nothing = jnp.zeros_like(edge)
    low, high = jnp.where(width == 0, nothing, edge), jnp.where(width == 0, edge, nothing)
    paired = jnp.concatenate([low, paired, high], axis=2).reshape(2, 4, 9, OWN, 2 * CH)
    fine = jnp.concatenate([paired[:, :, :-1], paired[:, :, 1:]], axis=3).transpose(2, 0, 1, 3, 4)
    fine, block = lax.optimization_barrier((fine, block))
    swap = [(0, 1), (1, 0)]
    other_block = lax.ppermute(block, "core", swap)
    mine = lax.all_to_all(fine, ("z", "x_hi"), 0, 0, tiled=True).reshape(8, 2, 2, 2, WIN, 2 * CH)

    first_act, first_slope, late_slope, up_act = call(
        forward_kernel, (6,), (core_arg, block, other_block, conv_first, conv_second, mask),
        [SMEM, whole(block.shape), whole(block.shape), tap_weights(0), tap_weights(3), whole(mask.shape)],
        [(six_frames, BF16), (act_shape, BF16), (act_shape, BF16), (act_shape, BF16)],
        [pltpu.VMEM((FR + 4, ROWS + 2, WIN, 3 * CH), BF16), pltpu.VMEM(((FR + 2) * ROWS * WIN, CH), F32)],
        67 * tap_flops,
    )
    mine, up_act = lax.optimization_barrier((mine, up_act))
    other = lax.ppermute(mine, "core", swap)
    grad_sum, sum_head = call(
        cotangent_kernel, (), (core_arg, mine, other, up_kernel, late_slope, mask),
        [SMEM, whole(mine.shape), whole(mine.shape), whole(up_kernel.shape), whole(act_shape), whole(mask.shape)],
        [(act_shape, BF16), (two_frames, BF16)], [pltpu.VMEM((FR, ROWS + 1, 2, WIN, 4 * CH), BF16)], 16 * tap_flops,
    )
    later = shift(sum_head, "y", -1)
    up_act, grad_sum = lax.optimization_barrier((up_act, grad_sum))
    up_part = call(
        up_grad_kernel, (), (core_arg, up_act, mine, other),
        [SMEM, whole(act_shape), whole(mine.shape), whole(mine.shape)],
        [((64, 32, CH), BF16)],
        [pltpu.VMEM((FR, ROWS + 1, 2, OWN, 4 * CH), BF16), pltpu.VMEM((CH, FR * ROWS * OWN), BF16)], 4 * tap_flops,
    )
    grad_table = pltpu.VMEM((FR, ROWS + 2, WIN, 3 * CH), BF16)
    grad_scratch = [grad_table, pltpu.VMEM((CH, (FR + 2) * ROWS * WIN), BF16), pltpu.VMEM((TAPS * CH + 8, CH), F32)]
    early = call(
        second_grad_kernel, (), (place, first_act, grad_sum, up_part),
        [SMEM, whole(six_frames), whole(act_shape), whole(up_part.shape)],
        [((64, UP_ROWS + PIECE, CH), BF16)], grad_scratch, 27 * tap_flops,
    )
    early, later = lax.optimization_barrier((early, later))
    early = lax.all_to_all(early, ("z", "x_hi", "width"), 0, 0, tiled=True)

    grad_hidden, hidden_head = call(
        hidden_kernel, (3,), (grad_sum, later, first_slope, conv_second, mask),
        [whole(act_shape), whole(later.shape), whole(act_shape), tap_weights(), whole(mask.shape)],
        [(act_shape, BF16), (two_frames, BF16)], [table, total], 27 * tap_flops,
    )
    later_hidden = lax.ppermute(hidden_head, ("y", "core"), [(2 * i + 1, 2 * i - 1) for i in range(1, 4)])
    blocks = call(
        first_grad_kernel, (), (place, block, other_block, grad_hidden),
        [SMEM, whole(block.shape), whole(block.shape), whole(act_shape)],
        [((16, PIECE, CH), BF16)] * 4, grad_scratch, 27 * tap_flops,
    )
    arrived = [blocks[0]]
    for step in (2, 1, 3):
        arrived.append(over_y(blocks[step], step))
    tied_hidden, _ = lax.optimization_barrier((grad_hidden, blocks[0]))
    rows_out = call(
        features_kernel, (3,), (core_arg, tied_hidden, later_hidden, grad_sum, conv_first),
        [SMEM, whole(act_shape), whole(later_hidden.shape), whole(act_shape), tap_weights()],
        [((ROWS, 2, OWN, CH), BF16)], [own_table, pltpu.VMEM((2 * ROWS * OWN, CH), F32)], 7 * tap_flops,
    )

    tied_rows, early = lax.optimization_barrier((rows_out, early))
    early = jnp.sum(early.reshape(16, 4, UP_ROWS + PIECE, CH).astype(F32), axis=0)
    early_total = early[0]
    for step in (2, 1, 3):
        early_total += over_y(early[step].astype(BF16), step).astype(F32)
    first_sum = sum(value.astype(F32) for value in arrived).astype(BF16)
    late = jnp.concatenate([tied_rows.reshape(16, 2 * OWN, CH), first_sum], axis=1)
    late = lax.all_to_all(late, ("z", "x_hi", "width"), 0, 0, tiled=True)

    factor = 1.0 / math.sqrt(32768)
    early = early_total * factor
    returned = late[:, : 2 * OWN].reshape(8, 2, 2, OWN, CH).transpose(2, 1, 0, 3, 4)
    first_share = jnp.sum(late[:, 2 * OWN : 2 * OWN + SHARE].astype(F32), axis=0) * factor
    return (
        returned.reshape(2, 1, 128, CH),
        first_share.reshape(-1),
        early[UP_ROWS : UP_ROWS + SHARE].reshape(-1),
        early[:UP_ROWS].reshape(-1),
    )


def solution(mesh):
    names = ("y", "core", "z", "x_hi", "width")
    split = Mesh(mesh.devices.reshape(4, 2, 4, 2, 2), names)
    tm, height = ("y", "core"), ("z", "x_hi")
    in_specs = (
        P(tm, (*height, "width"), None, None),
        P(),
        P(),
        P(),
        P(tm, height, "width", None),
    )
    flat = P(names)
    out_specs = (P(tm, (*height, "width"), None, None), flat, flat, flat)
    return jax.shard_map(shards, mesh=split, in_specs=in_specs, out_specs=out_specs, check_vma=False)
```

```python
import math

import jax
import jax.numpy as jnp
from jax import lax
from jax.experimental import pallas as pl
from jax.experimental.pallas import tpu as pltpu
from jax.sharding import Mesh, PartitionSpec as P

F32 = jnp.float32
BF16 = jnp.bfloat16
VMEM_LIMIT = 48 * 1024 * 1024

FR = 4
ROWS = 16
WIN = 16
OWN = 8
EDGE = 4
CH = 256
TAPS = 27
SHARE = 54
PIECE = 56
UP_ROWS = 32


def slope_of(values, sigma):
    return sigma * (1.0 + values * (1.0 - sigma))


def nt(lhs, rhs):
    return lax.dot_general(lhs, rhs, (((1,), (1,)), ((), ())), preferred_element_type=F32)


def nn(lhs, rhs):
    return jnp.dot(lhs, rhs, preferred_element_type=F32)


def fill_table(table, slot, block, forward):
    wide = block.astype(F32)
    before = pltpu.roll(wide, 1, axis=1).astype(BF16)
    after = pltpu.roll(wide, WIN - 1, axis=1).astype(BF16)
    table[slot, 1 : ROWS + 1, :, 0:CH] = before if forward else after
    table[slot, 1 : ROWS + 1, :, CH : 2 * CH] = block
    table[slot, 1 : ROWS + 1, :, 2 * CH : 3 * CH] = after if forward else before


def fill_own_table(table, slot, block):
    wide = block.astype(F32)
    for tap in range(3):
        moved = pltpu.roll(wide, WIN - (EDGE + 1 - tap), axis=1)
        table[slot, 1 : ROWS + 1, :, tap * CH : (tap + 1) * CH] = moved[:, :OWN].astype(BF16)


def clear_border(table):
    frames, _, columns, lanes = table.shape
    border = jnp.zeros((frames, columns, lanes), BF16)
    table[:, 0] = border
    table[:, ROWS + 1] = border


def own_columns(block):
    return pltpu.roll(block.astype(F32), WIN - EDGE, axis=1)[:, :OWN]


def forward_taps(table, step, frames, weights, total):
    rows = frames * ROWS * WIN
    for tap in range(3):
        lhs = table[pl.ds(step, frames), tap : tap + ROWS].reshape(rows, 3 * CH)
        total[:rows] += nn(lhs, weights[0, tap].reshape(3 * CH, CH))


def backward_taps(table, start, frames, columns, weights, total):
    step = pl.program_id(0)
    for tap_h in range(3):
        part = None
        for tap_w in range(3):
            lanes = slice(tap_w * CH, (tap_w + 1) * CH)
            lhs = table[pl.ds(start + 2 - step, frames), 2 - tap_h : 2 - tap_h + ROWS, :, lanes]
            more = nt(lhs.reshape(frames * ROWS * columns, CH), weights[0, tap_h, tap_w])
            part = more if part is None else part + more
        total[...] += part


def frame_of(total, frame, columns):
    rows = ROWS * columns
    return total[frame * rows : (frame + 1) * rows].reshape(ROWS, columns, CH)


def forward_kernel(core_ref, mine, other, mine_before, other_before, first, second, mask, act, slope, summed, up_act, table, total):
    step = pl.program_id(0)
    core = core_ref[0]
    sources = ((mine, core), (other, 1 - core))

    @pl.when(step == 0)
    def _():
        clear_border(table)
        for source, which in sources:
            for frame in range(2):
                fill_table(table, 4 + 2 * which + frame, source[:, frame], True)
        for source, which in ((mine_before, core), (other_before, 1 - core)):
            for frame in range(2):
                fill_table(table, 2 * which + frame, source[:, frame], True)
        total[...] = jnp.zeros_like(total)

    @pl.when(step < 3)
    def _():
        forward_taps(table, step, FR + 2, first, total)

    @pl.when(step == 2)
    def _():
        for frame in range(FR + 2):
            values = frame_of(total, frame, WIN)
            sigma = jax.nn.sigmoid(values)
            result = (values * sigma * mask[...]).astype(BF16)
            act[frame] = result
            fill_table(table, frame, result, True)
            if frame >= 2:
                slope[frame - 2] = slope_of(values, sigma)
        total[...] = jnp.zeros_like(total)

    @pl.when(step >= 3)
    def _():
        forward_taps(table, step - 3, FR, second, total)

    @pl.when(step == 5)
    def _():
        rows = ROWS * WIN
        for source, which in sources:
            for frame in range(2):
                place = 2 * which + frame
                values = total[pl.ds(pl.multiple_of(place * rows, rows), rows)].reshape(ROWS, WIN, CH)
                values = values + source[:, frame].astype(F32)
                summed[place] = values
                up_act[place] = (values * jax.nn.sigmoid(values)).astype(BF16)


def hidden_kernel(block, later, slope, weights, mask, grad_hidden, head, table, total):
    @pl.when(pl.program_id(0) == 0)
    def _():
        clear_border(table)
        for frame in range(FR):
            fill_table(table, frame, block[frame], False)
        for frame in range(2):
            fill_table(table, FR + frame, later[frame], False)
        total[...] = jnp.zeros_like(total)

    backward_taps(table, 0, FR, WIN, weights, total)

    @pl.when(pl.program_id(0) == 2)
    def _():
        for frame in range(FR):
            result = (frame_of(total, frame, WIN) * slope[frame] * mask[...]).astype(BF16)
            grad_hidden[frame] = result
            if frame < 2:
                head[frame] = result


def features_kernel(core_ref, block, later, grad_sum, weights, grad_features, table, total):
    core = core_ref[0]

    @pl.when(pl.program_id(0) == 0)
    def _():
        clear_border(table)
        for frame in range(FR):
            fill_own_table(table, frame, block[frame])
        for frame in range(2):
            fill_own_table(table, FR + frame, later[frame])
        total[...] = jnp.zeros_like(total)

    backward_taps(table, 2 * core, 2, OWN, weights, total)

    @pl.when(pl.program_id(0) == 2)
    def _():
        for frame in range(2):
            values = frame_of(total, frame, OWN) + own_columns(grad_sum[2 * core + frame])
            grad_features[:, frame] = values.astype(BF16)


def cotangent_kernel(core_ref, mine, other, weights, summed, mask, grad_sum, head, table):
    core = core_ref[0]
    border = jnp.zeros((FR, WIN, 4 * CH), BF16)
    table[:, 0, 0] = border
    table[:, ROWS, 1] = border
    for source, which in ((mine, core), (other, 1 - core)):
        for frame in range(2):
            slot = 2 * which + frame
            for parity in range(2):
                fine = source[:, frame, :, parity].reshape(ROWS, WIN, 2 * CH)
                even, odd = fine[:, :, :CH], fine[:, :, CH:]
                before = pltpu.roll(odd.astype(F32), 1, axis=1).astype(BF16)
                after = pltpu.roll(even.astype(F32), WIN - 1, axis=1).astype(BF16)
                low = 0 if parity == 0 else 1
                put = (slot, slice(low, low + ROWS), 1 - parity)
                table[put + (slice(None), slice(0, CH))] = before
                table[put + (slice(None), slice(CH, 2 * CH))] = even
                table[put + (slice(None), slice(2 * CH, 3 * CH))] = odd
                table[put + (slice(None), slice(3 * CH, 4 * CH))] = after
    for frame in range(FR):
        part = None
        for tap in range(4):
            for column in range(4):
                lhs = table[frame, tap // 2 : tap // 2 + ROWS, tap % 2, :, column * CH : (column + 1) * CH]
                more = nt(lhs.reshape(ROWS * WIN, CH), weights[tap, column])
                part = more if part is None else part + more
        grad_act = part.reshape(ROWS, WIN, CH).astype(BF16).astype(F32)
        values = summed[frame]
        grad = grad_act * slope_of(values, jax.nn.sigmoid(values)) * mask[...]
        grad_sum[frame] = grad.astype(BF16)
        if frame < 2:
            head[frame] = grad.astype(BF16)


def up_grad_kernel(core_ref, act, mine, other, out, table, flipped):
    core = core_ref[0]
    border = jnp.zeros((FR, OWN, 4 * CH), BF16)
    table[:, 0, 0] = border
    table[:, ROWS, 1] = border
    for source, which in ((mine, core), (other, 1 - core)):
        for frame in range(2):
            slot = 2 * which + frame
            for parity in range(2):
                fine = source[:, frame, :, parity].reshape(ROWS, WIN, 2 * CH).astype(F32)
                even, odd = fine[:, :, :CH], fine[:, :, CH:]
                low = 0 if parity == 0 else 1
                put = (slot, slice(low, low + ROWS), 1 - parity)
                for column, (values, shift) in enumerate(((odd, -1), (even, 0), (odd, 0), (even, 1))):
                    moved = pltpu.roll(values, WIN - (EDGE + shift), axis=1)[:, :OWN].astype(BF16)
                    table[put + (slice(None), slice(column * CH, (column + 1) * CH))] = moved
    for frame in range(FR):
        rows = ROWS * OWN
        flipped[:, frame * rows : (frame + 1) * rows] = jnp.transpose(
            own_columns(act[frame]).reshape(rows, CH)
        ).astype(BF16)
    lanes = pl.ds(pl.multiple_of(core * 2 * CH, 2 * CH), 2 * CH)
    for tap in range(4):
        rhs = table[:, tap // 2 : tap // 2 + ROWS, tap % 2, :, lanes]
        result = nn(flipped[...], rhs.reshape(FR * ROWS * OWN, 2 * CH))
        for half in range(2):
            for piece in range(8):
                out[tap * 16 + half * 8 + piece] = result[
                    piece * 32 : (piece + 1) * 32, half * CH : (half + 1) * CH
                ].astype(BF16)


def tap_sums(frames, block, table, flipped, sums):
    clear_border(table)
    column = lax.broadcasted_iota(jnp.int32, (ROWS, WIN, CH), 1)
    own = (column >= EDGE) & (column < EDGE + OWN)
    for frame in range(FR):
        fill_table(table, frame, jnp.where(own, block[frame].astype(F32), 0.0).astype(BF16), False)
    rows = ROWS * WIN
    for slot, values in frames:
        lanes = pl.ds(pl.multiple_of(slot * rows, rows), rows)
        flipped[:, lanes] = jnp.transpose(values.astype(F32).reshape(rows, CH)).astype(BF16)
    sums[TAPS * CH :] = jnp.zeros((8, CH), F32)
    for tap_t in range(3):
        lhs = flipped[:, tap_t * rows : (tap_t + FR) * rows]
        for tap_h in range(3):
            rhs = table[:, 2 - tap_h : 2 - tap_h + ROWS]
            result = nn(lhs, rhs.reshape(FR * rows, 3 * CH))
            for tap_w in range(3):
                at = (tap_t * 9 + tap_h * 3 + tap_w) * CH
                sums[at : at + CH] = result[:, tap_w * CH : (tap_w + 1) * CH]


def piece_of(sums, owner, member):
    at = SHARE * member
    start = pl.multiple_of(16 * SHARE * owner + at // 8 * 8, 8)
    return sums[pl.ds(start, PIECE + 8)][at % 8 : at % 8 + PIECE]


def second_grad_kernel(place, act, block, up, out, table, flipped, sums):
    tap_sums([(frame, act[frame]) for frame in range(FR + 2)], block, table, flipped, sums)
    for step in range(4):
        group = lax.rem(place[1] + step, 4)
        for member in range(16):
            chunk = member * 4 + step
            out[chunk, :UP_ROWS] = up[group * 16 + member]
            out[chunk, UP_ROWS:] = piece_of(sums, 2 * group + place[0], member).astype(BF16)


def first_grad_kernel(place, mine, other, mine_before, other_before, block, own, next_one, next_two, next_three, table, flipped, sums):
    core = place[0]
    frames = []
    for frame in range(2):
        before = jnp.where(core == 1, mine_before[:, frame].astype(F32), other_before[:, frame].astype(F32))
        frames.append((frame, before))
        frames.append((2 + 2 * core + frame, mine[:, frame]))
        frames.append((4 - 2 * core + frame, other[:, frame]))
    tap_sums(frames, block, table, flipped, sums)
    for step, out in enumerate((own, next_one, next_two, next_three)):
        group = lax.rem(place[1] + step, 4)
        for member in range(16):
            out[member] = piece_of(sums, 2 * group + place[0], member).astype(BF16)


def whole(shape):
    zeros = (0,) * len(shape)
    return pl.BlockSpec(shape, lambda *_: zeros)


SMEM = pl.BlockSpec(memory_space=pltpu.SMEM)


def tap_weights(begin=0):
    return pl.BlockSpec((1, 3, 3, CH, CH), lambda step: (jnp.clip(step - begin, 0, 2), 0, 0, 0, 0))


def call(kernel, grid, args, specs, outs, scratch, flops):
    shapes = [jax.ShapeDtypeStruct(shape, dtype) for shape, dtype in outs]
    moved = sum(math.prod(a.shape) * a.dtype.itemsize for a in args)
    moved += sum(math.prod(s.shape) * s.dtype.itemsize for s in shapes)
    single = len(shapes) == 1
    return pl.pallas_call(
        kernel,
        out_shape=shapes[0] if single else shapes,
        grid=grid,
        in_specs=specs,
        out_specs=whole(shapes[0].shape) if single else [whole(s.shape) for s in shapes],
        scratch_shapes=scratch,
        compiler_params=pltpu.CompilerParams(vmem_limit_bytes=VMEM_LIMIT),
        cost_estimate=pl.CostEstimate(flops=int(flops), bytes_accessed=moved, transcendentals=0),
    )(*args)


def shift(value, axis, step):
    count = lax.axis_size(axis)
    return lax.ppermute(value, axis, [(i, i + step) for i in range(count) if 0 <= i + step < count])


def over_y(value, step):
    return lax.ppermute(value, "y", [(i, (i + step) % 4) for i in range(4)])


def shards(features, conv_first, conv_second, up_kernel, cotangent):
    core = lax.axis_index("core")
    height = 2 * lax.axis_index("z") + lax.axis_index("x_hi")
    width = lax.axis_index("width")
    core_arg = core.astype(jnp.int32).reshape(1)
    place = jnp.stack([core, lax.axis_index("y")]).astype(jnp.int32)
    window = 8 * width + height
    columns = OWN * window - EDGE + jnp.arange(WIN)
    inside = ((columns >= 0) & (columns < 128)).astype(F32)
    mask = jnp.broadcast_to(inside[:, None], (WIN, CH))
    act_shape = (FR, ROWS, WIN, CH)
    two_frames = (2, ROWS, WIN, CH)
    six_frames = (FR + 2, ROWS, WIN, CH)
    table = pltpu.VMEM((FR + 2, ROWS + 2, WIN, 3 * CH), BF16)
    own_table = pltpu.VMEM((FR + 2, ROWS + 2, OWN, 3 * CH), BF16)
    total = pltpu.VMEM((FR * ROWS * WIN, CH), F32)
    tap_flops = 2 * FR * ROWS * WIN * CH * CH

    paired = cotangent.reshape(2, 4, 64, 2 * CH)
    edge = jnp.where(width == 0, paired[:, :, 64 - EDGE :], paired[:, :, :EDGE])
    edge = lax.ppermute(edge, "width", [(0, 1), (1, 0)])
    frames = features[:, 0]
    padded = jnp.pad(frames, ((0, 0), (EDGE, EDGE), (0, 0))).reshape(2, 17, OWN, CH)
    windows = jnp.concatenate([padded[:, :-1], padded[:, 1:]], axis=2)
    windows = windows.reshape(2, 2, 8, WIN, CH).transpose(2, 1, 0, 3, 4).reshape(16, 2, WIN, CH)
    windows, edge = lax.optimization_barrier((windows, edge))
    block = lax.all_to_all(windows, ("z", "x_hi", "width"), 0, 0, tiled=True)

    nothing = jnp.zeros_like(edge)
    low, high = jnp.where(width == 0, nothing, edge), jnp.where(width == 0, edge, nothing)
    paired = jnp.concatenate([low, paired, high], axis=2).reshape(2, 4, 9, OWN, 2 * CH)
    fine = jnp.concatenate([paired[:, :, :-1], paired[:, :, 1:]], axis=3).transpose(2, 0, 1, 3, 4)
    fine, block = lax.optimization_barrier((fine, block))
    swap = [(0, 1), (1, 0)]
    before = shift(block, "y", 1)
    other_block = lax.ppermute(block, "core", swap)
    crossed = [(2 * i + j, 2 * i + 3 - j) for i in range(3) for j in range(2)]
    other_before = lax.ppermute(block, ("y", "core"), crossed)
    blocks_in = (block, other_block, before, other_before)
    mine = lax.all_to_all(fine, ("z", "x_hi"), 0, 0, tiled=True).reshape(8, 2, 2, 2, WIN, 2 * CH)

    first_act, first_slope, summed, up_act = call(
        forward_kernel, (6,), (core_arg, *blocks_in, conv_first, conv_second, mask),
        [SMEM, *[whole(block.shape)] * 4, tap_weights(0), tap_weights(3), whole(mask.shape)],
        [(six_frames, BF16), (act_shape, F32), (act_shape, F32), (act_shape, BF16)],
        [pltpu.VMEM((FR + 4, ROWS + 2, WIN, 3 * CH), BF16), pltpu.VMEM(((FR + 2) * ROWS * WIN, CH), F32)],
        67 * tap_flops,
    )
    mine, up_act = lax.optimization_barrier((mine, up_act))
    other = lax.ppermute(mine, "core", swap)
    grad_sum, sum_head = call(
        cotangent_kernel, (), (core_arg, mine, other, up_kernel, summed, mask),
        [SMEM, whole(mine.shape), whole(mine.shape), whole(up_kernel.shape), whole(act_shape), whole(mask.shape)],
        [(act_shape, BF16), (two_frames, BF16)], [pltpu.VMEM((FR, ROWS + 1, 2, WIN, 4 * CH), BF16)], 16 * tap_flops,
    )
    later = shift(sum_head, "y", -1)
    up_act, grad_sum = lax.optimization_barrier((up_act, grad_sum))
    up_part = call(
        up_grad_kernel, (), (core_arg, up_act, mine, other),
        [SMEM, whole(act_shape), whole(mine.shape), whole(mine.shape)],
        [((64, 32, CH), BF16)],
        [pltpu.VMEM((FR, ROWS + 1, 2, OWN, 4 * CH), BF16), pltpu.VMEM((CH, FR * ROWS * OWN), BF16)], 4 * tap_flops,
    )
    grad_table = pltpu.VMEM((FR, ROWS + 2, WIN, 3 * CH), BF16)
    grad_scratch = [grad_table, pltpu.VMEM((CH, (FR + 2) * ROWS * WIN), BF16), pltpu.VMEM((TAPS * CH + 8, CH), F32)]
    early = call(
        second_grad_kernel, (), (place, first_act, grad_sum, up_part),
        [SMEM, whole(six_frames), whole(act_shape), whole(up_part.shape)],
        [((64, UP_ROWS + PIECE, CH), BF16)], grad_scratch, 27 * tap_flops,
    )
    early, later = lax.optimization_barrier((early, later))
    early = lax.all_to_all(early, ("z", "x_hi", "width"), 0, 0, tiled=True)

    grad_hidden, hidden_head = call(
        hidden_kernel, (3,), (grad_sum, later, first_slope, conv_second, mask),
        [whole(act_shape), whole(later.shape), whole(act_shape), tap_weights(), whole(mask.shape)],
        [(act_shape, BF16), (two_frames, BF16)], [table, total], 27 * tap_flops,
    )
    later_hidden = lax.ppermute(hidden_head, ("y", "core"), [(2 * i + 1, 2 * i - 1) for i in range(1, 4)])
    blocks = call(
        first_grad_kernel, (), (place, *blocks_in, grad_hidden),
        [SMEM, *[whole(block.shape)] * 4, whole(act_shape)],
        [((16, PIECE, CH), BF16)] * 4, grad_scratch, 27 * tap_flops,
    )
    arrived = [blocks[0]]
    for step in (2, 1, 3):
        arrived.append(over_y(blocks[step], step))
    tied_hidden, _ = lax.optimization_barrier((grad_hidden, blocks[0]))
    rows_out = call(
        features_kernel, (3,), (core_arg, tied_hidden, later_hidden, grad_sum, conv_first),
        [SMEM, whole(act_shape), whole(later_hidden.shape), whole(act_shape), tap_weights()],
        [((ROWS, 2, OWN, CH), BF16)], [own_table, pltpu.VMEM((2 * ROWS * OWN, CH), F32)], 7 * tap_flops,
    )

    tied_rows, early = lax.optimization_barrier((rows_out, early))
    early = jnp.sum(early.reshape(16, 4, UP_ROWS + PIECE, CH).astype(F32), axis=0)
    early_total = early[0]
    for step in (2, 1, 3):
        early_total += over_y(early[step].astype(BF16), step).astype(F32)
    first_sum = sum(value.astype(F32) for value in arrived).astype(BF16)
    late = jnp.concatenate([tied_rows.reshape(16, 2 * OWN, CH), first_sum], axis=1)
    late = lax.all_to_all(late, ("z", "x_hi", "width"), 0, 0, tiled=True)

    factor = 1.0 / math.sqrt(32768)
    early = early_total * factor
    returned = late[:, : 2 * OWN].reshape(8, 2, 2, OWN, CH).transpose(2, 1, 0, 3, 4)
    first_share = jnp.sum(late[:, 2 * OWN : 2 * OWN + SHARE].astype(F32), axis=0) * factor
    return (
        returned.reshape(2, 1, 128, CH),
        first_share.reshape(-1),
        early[UP_ROWS : UP_ROWS + SHARE].reshape(-1),
        early[:UP_ROWS].reshape(-1),
    )


def solution(mesh):
    names = ("y", "core", "z", "x_hi", "width")
    split = Mesh(mesh.devices.reshape(4, 2, 4, 2, 2), names)
    tm, height = ("y", "core"), ("z", "x_hi")
    in_specs = (
        P(tm, (*height, "width"), None, None),
        P(),
        P(),
        P(),
        P(tm, height, "width", None),
    )
    flat = P(names)
    out_specs = (P(tm, (*height, "width"), None, None), flat, flat, flat)
    return jax.shard_map(shards, mesh=split, in_specs=in_specs, out_specs=out_specs, check_vma=False)
```

```python
import math

import jax
import jax.numpy as jnp
from jax import lax
from jax.experimental import pallas as pl
from jax.experimental.pallas import tpu as pltpu
from jax.sharding import Mesh, PartitionSpec as P

F32 = jnp.float32
BF16 = jnp.bfloat16
VMEM_LIMIT = 48 * 1024 * 1024

FR = 4
ROWS = 16
WIN = 16
OWN = 8
EDGE = 4
CH = 256
TAPS = 27
SHARE = 54
PIECE = 56
UP_ROWS = 32


def slope_of(values, sigma):
    return sigma * (1.0 + values * (1.0 - sigma))


def nt(lhs, rhs):
    return lax.dot_general(lhs, rhs, (((1,), (1,)), ((), ())), preferred_element_type=F32)


def nn(lhs, rhs):
    return jnp.dot(lhs, rhs, preferred_element_type=F32)


def fill_table(table, slot, block, forward):
    wide = block.astype(F32)
    before = pltpu.roll(wide, 1, axis=1).astype(BF16)
    after = pltpu.roll(wide, WIN - 1, axis=1).astype(BF16)
    table[slot, 1 : ROWS + 1, :, 0:CH] = before if forward else after
    table[slot, 1 : ROWS + 1, :, CH : 2 * CH] = block
    table[slot, 1 : ROWS + 1, :, 2 * CH : 3 * CH] = after if forward else before


def fill_own_table(table, slot, block):
    wide = block.astype(F32)
    for tap in range(3):
        moved = pltpu.roll(wide, WIN - (EDGE + 1 - tap), axis=1)
        table[slot, 1 : ROWS + 1, :, tap * CH : (tap + 1) * CH] = moved[:, :OWN].astype(BF16)


def clear_border(table):
    frames, _, columns, lanes = table.shape
    border = jnp.zeros((frames, columns, lanes), BF16)
    table[:, 0] = border
    table[:, ROWS + 1] = border


def own_columns(block):
    return pltpu.roll(block.astype(F32), WIN - EDGE, axis=1)[:, :OWN]


def forward_taps(table, step, frames, weights, total):
    rows = frames * ROWS * WIN
    for tap in range(3):
        lhs = table[pl.ds(step, frames), tap : tap + ROWS].reshape(rows, 3 * CH)
        total[:rows] += nn(lhs, weights[0, tap].reshape(3 * CH, CH))


def backward_taps(table, start, frames, columns, weights, total):
    step = pl.program_id(0)
    for tap_h in range(3):
        part = None
        for tap_w in range(3):
            lanes = slice(tap_w * CH, (tap_w + 1) * CH)
            lhs = table[pl.ds(start + 2 - step, frames), 2 - tap_h : 2 - tap_h + ROWS, :, lanes]
            more = nt(lhs.reshape(frames * ROWS * columns, CH), weights[0, tap_h, tap_w])
            part = more if part is None else part + more
        total[...] += part


def frame_of(total, frame, columns):
    rows = ROWS * columns
    return total[frame * rows : (frame + 1) * rows].reshape(ROWS, columns, CH)


def forward_kernel(core_ref, mine, other, first, second, mask, act, slope, summed, up_act, table, total):
    step = pl.program_id(0)
    core = core_ref[0]
    sources = ((mine, core), (other, 1 - core))

    @pl.when(step == 0)
    def _():
        clear_border(table)
        for source, which in sources:
            for frame in range(FR):
                slot = 2 * which + (frame if frame < 2 else frame + 2)
                fill_table(table, slot, source[:, frame], True)
        total[...] = jnp.zeros_like(total)

    @pl.when(step < 3)
    def _():
        forward_taps(table, step, FR + 2, first, total)

    @pl.when(step == 2)
    def _():
        for frame in range(FR + 2):
            values = frame_of(total, frame, WIN)
            sigma = jax.nn.sigmoid(values)
            result = (values * sigma * mask[...]).astype(BF16)
            act[frame] = result
            fill_table(table, frame, result, True)
            if frame >= 2:
                slope[frame - 2] = slope_of(values, sigma)
        total[...] = jnp.zeros_like(total)

    @pl.when(step >= 3)
    def _():
        forward_taps(table, step - 3, FR, second, total)

    @pl.when(step == 5)
    def _():
        rows = ROWS * WIN
        for source, which in sources:
            for frame in range(2):
                place = 2 * which + frame
                values = total[pl.ds(pl.multiple_of(place * rows, rows), rows)].reshape(ROWS, WIN, CH)
                values = values + source[:, 2 + frame].astype(F32)
                summed[place] = values
                up_act[place] = (values * jax.nn.sigmoid(values)).astype(BF16)


def hidden_kernel(block, later, slope, weights, mask, grad_hidden, head, table, total):
    @pl.when(pl.program_id(0) == 0)
    def _():
        clear_border(table)
        for frame in range(FR):
            fill_table(table, frame, block[frame], False)
        for frame in range(2):
            fill_table(table, FR + frame, later[frame], False)
        total[...] = jnp.zeros_like(total)

    backward_taps(table, 0, FR, WIN, weights, total)

    @pl.when(pl.program_id(0) == 2)
    def _():
        for frame in range(FR):
            result = (frame_of(total, frame, WIN) * slope[frame] * mask[...]).astype(BF16)
            grad_hidden[frame] = result
            if frame < 2:
                head[frame] = result


def features_kernel(core_ref, block, later, grad_sum, weights, grad_features, table, total):
    core = core_ref[0]

    @pl.when(pl.program_id(0) == 0)
    def _():
        clear_border(table)
        for frame in range(FR):
            fill_own_table(table, frame, block[frame])
        for frame in range(2):
            fill_own_table(table, FR + frame, later[frame])
        total[...] = jnp.zeros_like(total)

    backward_taps(table, 2 * core, 2, OWN, weights, total)

    @pl.when(pl.program_id(0) == 2)
    def _():
        for frame in range(2):
            values = frame_of(total, frame, OWN) + own_columns(grad_sum[2 * core + frame])
            grad_features[:, frame] = values.astype(BF16)


def cotangent_kernel(core_ref, mine, other, weights, summed, mask, grad_sum, head, table):
    core = core_ref[0]
    border = jnp.zeros((FR, WIN, 4 * CH), BF16)
    table[:, 0, 0] = border
    table[:, ROWS, 1] = border
    for source, which in ((mine, core), (other, 1 - core)):
        for frame in range(2):
            slot = 2 * which + frame
            for parity in range(2):
                fine = source[:, frame, :, parity].reshape(ROWS, WIN, 2 * CH)
                even, odd = fine[:, :, :CH], fine[:, :, CH:]
                before = pltpu.roll(odd.astype(F32), 1, axis=1).astype(BF16)
                after = pltpu.roll(even.astype(F32), WIN - 1, axis=1).astype(BF16)
                low = 0 if parity == 0 else 1
                put = (slot, slice(low, low + ROWS), 1 - parity)
                table[put + (slice(None), slice(0, CH))] = before
                table[put + (slice(None), slice(CH, 2 * CH))] = even
                table[put + (slice(None), slice(2 * CH, 3 * CH))] = odd
                table[put + (slice(None), slice(3 * CH, 4 * CH))] = after
    for frame in range(FR):
        part = None
        for tap in range(4):
            for column in range(4):
                lhs = table[frame, tap // 2 : tap // 2 + ROWS, tap % 2, :, column * CH : (column + 1) * CH]
                more = nt(lhs.reshape(ROWS * WIN, CH), weights[tap, column])
                part = more if part is None else part + more
        grad_act = part.reshape(ROWS, WIN, CH).astype(BF16).astype(F32)
        values = summed[frame]
        grad = grad_act * slope_of(values, jax.nn.sigmoid(values)) * mask[...]
        grad_sum[frame] = grad.astype(BF16)
        if frame < 2:
            head[frame] = grad.astype(BF16)


def up_grad_kernel(core_ref, act, mine, other, out, table, flipped):
    core = core_ref[0]
    border = jnp.zeros((FR, OWN, 4 * CH), BF16)
    table[:, 0, 0] = border
    table[:, ROWS, 1] = border
    for source, which in ((mine, core), (other, 1 - core)):
        for frame in range(2):
            slot = 2 * which + frame
            for parity in range(2):
                fine = source[:, frame, :, parity].reshape(ROWS, WIN, 2 * CH).astype(F32)
                even, odd = fine[:, :, :CH], fine[:, :, CH:]
                low = 0 if parity == 0 else 1
                put = (slot, slice(low, low + ROWS), 1 - parity)
                for column, (values, shift) in enumerate(((odd, -1), (even, 0), (odd, 0), (even, 1))):
                    moved = pltpu.roll(values, WIN - (EDGE + shift), axis=1)[:, :OWN].astype(BF16)
                    table[put + (slice(None), slice(column * CH, (column + 1) * CH))] = moved
    for frame in range(FR):
        rows = ROWS * OWN
        flipped[:, frame * rows : (frame + 1) * rows] = jnp.transpose(
            own_columns(act[frame]).reshape(rows, CH)
        ).astype(BF16)
    lanes = pl.ds(pl.multiple_of(core * 2 * CH, 2 * CH), 2 * CH)
    for tap in range(4):
        rhs = table[:, tap // 2 : tap // 2 + ROWS, tap % 2, :, lanes]
        result = nn(flipped[...], rhs.reshape(FR * ROWS * OWN, 2 * CH))
        for half in range(2):
            for piece in range(8):
                out[tap * 16 + half * 8 + piece] = result[
                    piece * 32 : (piece + 1) * 32, half * CH : (half + 1) * CH
                ].astype(BF16)


def tap_sums(frames, block, table, flipped, sums):
    clear_border(table)
    column = lax.broadcasted_iota(jnp.int32, (ROWS, WIN, CH), 1)
    own = (column >= EDGE) & (column < EDGE + OWN)
    for frame in range(FR):
        fill_table(table, frame, jnp.where(own, block[frame].astype(F32), 0.0).astype(BF16), False)
    rows = ROWS * WIN
    for slot, values in frames:
        lanes = pl.ds(pl.multiple_of(slot * rows, rows), rows)
        flipped[:, lanes] = jnp.transpose(values.astype(F32).reshape(rows, CH)).astype(BF16)
    sums[TAPS * CH :] = jnp.zeros((8, CH), F32)
    for tap_t in range(3):
        lhs = flipped[:, tap_t * rows : (tap_t + FR) * rows]
        for tap_h in range(3):
            rhs = table[:, 2 - tap_h : 2 - tap_h + ROWS]
            result = nn(lhs, rhs.reshape(FR * rows, 3 * CH))
            for tap_w in range(3):
                at = (tap_t * 9 + tap_h * 3 + tap_w) * CH
                sums[at : at + CH] = result[:, tap_w * CH : (tap_w + 1) * CH]


def piece_of(sums, owner, member):
    at = SHARE * member
    start = pl.multiple_of(16 * SHARE * owner + at // 8 * 8, 8)
    return sums[pl.ds(start, PIECE + 8)][at % 8 : at % 8 + PIECE]


def second_grad_kernel(place, act, block, up, out, table, flipped, sums):
    tap_sums([(frame, act[frame]) for frame in range(FR + 2)], block, table, flipped, sums)
    for step in range(4):
        group = lax.rem(place[1] + step, 4)
        for member in range(16):
            chunk = member * 4 + step
            out[chunk, :UP_ROWS] = up[group * 16 + member]
            out[chunk, UP_ROWS:] = piece_of(sums, 2 * group + place[0], member).astype(BF16)


def first_grad_kernel(place, mine, other, block, own, next_one, next_two, next_three, table, flipped, sums):
    core = place[0]
    frames = []
    for frame in range(2):
        before = jnp.where(core == 1, mine[:, frame].astype(F32), other[:, frame].astype(F32))
        frames.append((frame, before))
        frames.append((2 + 2 * core + frame, mine[:, 2 + frame]))
        frames.append((4 - 2 * core + frame, other[:, 2 + frame]))
    tap_sums(frames, block, table, flipped, sums)
    for step, out in enumerate((own, next_one, next_two, next_three)):
        group = lax.rem(place[1] + step, 4)
        for member in range(16):
            out[member] = piece_of(sums, 2 * group + place[0], member).astype(BF16)


def whole(shape):
    zeros = (0,) * len(shape)
    return pl.BlockSpec(shape, lambda *_: zeros)


SMEM = pl.BlockSpec(memory_space=pltpu.SMEM)


def tap_weights(begin=0):
    return pl.BlockSpec((1, 3, 3, CH, CH), lambda step: (jnp.clip(step - begin, 0, 2), 0, 0, 0, 0))


def call(kernel, grid, args, specs, outs, scratch, flops):
    shapes = [jax.ShapeDtypeStruct(shape, dtype) for shape, dtype in outs]
    moved = sum(math.prod(a.shape) * a.dtype.itemsize for a in args)
    moved += sum(math.prod(s.shape) * s.dtype.itemsize for s in shapes)
    single = len(shapes) == 1
    return pl.pallas_call(
        kernel,
        out_shape=shapes[0] if single else shapes,
        grid=grid,
        in_specs=specs,
        out_specs=whole(shapes[0].shape) if single else [whole(s.shape) for s in shapes],
        scratch_shapes=scratch,
        compiler_params=pltpu.CompilerParams(vmem_limit_bytes=VMEM_LIMIT),
        cost_estimate=pl.CostEstimate(flops=int(flops), bytes_accessed=moved, transcendentals=0),
    )(*args)


def shift(value, axis, step):
    count = lax.axis_size(axis)
    return lax.ppermute(value, axis, [(i, i + step) for i in range(count) if 0 <= i + step < count])


def over_y(value, step):
    return lax.ppermute(value, "y", [(i, (i + step) % 4) for i in range(4)])


def shards(features, conv_first, conv_second, up_kernel, cotangent):
    core = lax.axis_index("core")
    height = 2 * lax.axis_index("z") + lax.axis_index("x_hi")
    width = lax.axis_index("width")
    core_arg = core.astype(jnp.int32).reshape(1)
    place = jnp.stack([core, lax.axis_index("y")]).astype(jnp.int32)
    window = 8 * width + height
    columns = OWN * window - EDGE + jnp.arange(WIN)
    inside = ((columns >= 0) & (columns < 128)).astype(F32)
    mask = jnp.broadcast_to(inside[:, None], (WIN, CH))
    act_shape = (FR, ROWS, WIN, CH)
    two_frames = (2, ROWS, WIN, CH)
    six_frames = (FR + 2, ROWS, WIN, CH)
    table = pltpu.VMEM((FR + 2, ROWS + 2, WIN, 3 * CH), BF16)
    own_table = pltpu.VMEM((FR + 2, ROWS + 2, OWN, 3 * CH), BF16)
    total = pltpu.VMEM((FR * ROWS * WIN, CH), F32)
    tap_flops = 2 * FR * ROWS * WIN * CH * CH

    paired = cotangent.reshape(2, 4, 64, 2 * CH)
    edge = jnp.where(width == 0, paired[:, :, 64 - EDGE :], paired[:, :, :EDGE])
    edge = lax.ppermute(edge, "width", [(0, 1), (1, 0)])
    frames = features[:, 0]
    before, edge = lax.optimization_barrier((shift(frames, "y", 1), edge))
    frames = jnp.concatenate([before, frames], axis=0)
    padded = jnp.pad(frames, ((0, 0), (EDGE, EDGE), (0, 0))).reshape(4, 17, OWN, CH)
    windows = jnp.concatenate([padded[:, :-1], padded[:, 1:]], axis=2)
    windows = windows.reshape(4, 2, 8, WIN, CH).transpose(2, 1, 0, 3, 4).reshape(16, 4, WIN, CH)
    block = lax.all_to_all(windows, ("z", "x_hi", "width"), 0, 0, tiled=True)

    nothing = jnp.zeros_like(edge)
    low, high = jnp.where(width == 0, nothing, edge), jnp.where(width == 0, edge, nothing)
    paired = jnp.concatenate([low, paired, high], axis=2).reshape(2, 4, 9, OWN, 2 * CH)
    fine = jnp.concatenate([paired[:, :, :-1], paired[:, :, 1:]], axis=3).transpose(2, 0, 1, 3, 4)
    fine, block = lax.optimization_barrier((fine, block))
    swap = [(0, 1), (1, 0)]
    other_block = lax.ppermute(block, "core", swap)
    mine = lax.all_to_all(fine, ("z", "x_hi"), 0, 0, tiled=True).reshape(8, 2, 2, 2, WIN, 2 * CH)

    first_act, first_slope, summed, up_act = call(
        forward_kernel, (6,), (core_arg, block, other_block, conv_first, conv_second, mask),
        [SMEM, whole(block.shape), whole(block.shape), tap_weights(0), tap_weights(3), whole(mask.shape)],
        [(six_frames, BF16), (act_shape, F32), (act_shape, F32), (act_shape, BF16)],
        [pltpu.VMEM((FR + 4, ROWS + 2, WIN, 3 * CH), BF16), pltpu.VMEM(((FR + 2) * ROWS * WIN, CH), F32)],
        67 * tap_flops,
    )
    mine, up_act = lax.optimization_barrier((mine, up_act))
    other = lax.ppermute(mine, "core", swap)
    grad_sum, sum_head = call(
        cotangent_kernel, (), (core_arg, mine, other, up_kernel, summed, mask),
        [SMEM, whole(mine.shape), whole(mine.shape), whole(up_kernel.shape), whole(act_shape), whole(mask.shape)],
        [(act_shape, BF16), (two_frames, BF16)], [pltpu.VMEM((FR, ROWS + 1, 2, WIN, 4 * CH), BF16)], 16 * tap_flops,
    )
    later = shift(sum_head, "y", -1)
    up_act, grad_sum = lax.optimization_barrier((up_act, grad_sum))
    up_part = call(
        up_grad_kernel, (), (core_arg, up_act, mine, other),
        [SMEM, whole(act_shape), whole(mine.shape), whole(mine.shape)],
        [((64, 32, CH), BF16)],
        [pltpu.VMEM((FR, ROWS + 1, 2, OWN, 4 * CH), BF16), pltpu.VMEM((CH, FR * ROWS * OWN), BF16)], 4 * tap_flops,
    )
    grad_table = pltpu.VMEM((FR, ROWS + 2, WIN, 3 * CH), BF16)
    grad_scratch = [grad_table, pltpu.VMEM((CH, (FR + 2) * ROWS * WIN), BF16), pltpu.VMEM((TAPS * CH + 8, CH), F32)]
    early = call(
        second_grad_kernel, (), (place, first_act, grad_sum, up_part),
        [SMEM, whole(six_frames), whole(act_shape), whole(up_part.shape)],
        [((64, UP_ROWS + PIECE, CH), BF16)], grad_scratch, 27 * tap_flops,
    )
    early, later = lax.optimization_barrier((early, later))
    early = lax.all_to_all(early, ("z", "x_hi", "width"), 0, 0, tiled=True)

    grad_hidden, hidden_head = call(
        hidden_kernel, (3,), (grad_sum, later, first_slope, conv_second, mask),
        [whole(act_shape), whole(later.shape), whole(act_shape), tap_weights(), whole(mask.shape)],
        [(act_shape, BF16), (two_frames, BF16)], [table, total], 27 * tap_flops,
    )
    later_hidden = lax.ppermute(hidden_head, ("y", "core"), [(2 * i + 1, 2 * i - 1) for i in range(1, 4)])
    blocks = call(
        first_grad_kernel, (), (place, block, other_block, grad_hidden),
        [SMEM, whole(block.shape), whole(block.shape), whole(act_shape)],
        [((16, PIECE, CH), BF16)] * 4, grad_scratch, 27 * tap_flops,
    )
    arrived = [blocks[0]]
    for step in (2, 1, 3):
        arrived.append(over_y(blocks[step], step))
    tied_hidden, _ = lax.optimization_barrier((grad_hidden, blocks[0]))
    rows_out = call(
        features_kernel, (3,), (core_arg, tied_hidden, later_hidden, grad_sum, conv_first),
        [SMEM, whole(act_shape), whole(later_hidden.shape), whole(act_shape), tap_weights()],
        [((ROWS, 2, OWN, CH), BF16)], [own_table, pltpu.VMEM((2 * ROWS * OWN, CH), F32)], 7 * tap_flops,
    )

    first_sum = sum(value.astype(F32) for value in arrived).astype(BF16)
    late = jnp.concatenate([rows_out.reshape(16, 2 * OWN, CH), first_sum], axis=1)
    late, early = lax.optimization_barrier((late, early))
    early = jnp.sum(early.reshape(16, 4, UP_ROWS + PIECE, CH).astype(F32), axis=0)
    early_total = early[0]
    for step in (2, 1, 3):
        early_total += over_y(early[step].astype(BF16), step).astype(F32)
    late = lax.all_to_all(late, ("z", "x_hi", "width"), 0, 0, tiled=True)

    factor = 1.0 / math.sqrt(32768)
    early = early_total * factor
    returned = late[:, : 2 * OWN].reshape(8, 2, 2, OWN, CH).transpose(2, 1, 0, 3, 4)
    first_share = jnp.sum(late[:, 2 * OWN : 2 * OWN + SHARE].astype(F32), axis=0) * factor
    return (
        returned.reshape(2, 1, 128, CH),
        first_share.reshape(-1),
        early[UP_ROWS : UP_ROWS + SHARE].reshape(-1),
        early[:UP_ROWS].reshape(-1),
    )


def solution(mesh):
    names = ("y", "core", "z", "x_hi", "width")
    split = Mesh(mesh.devices.reshape(4, 2, 4, 2, 2), names)
    tm, height = ("y", "core"), ("z", "x_hi")
    in_specs = (
        P(tm, (*height, "width"), None, None),
        P(),
        P(),
        P(),
        P(tm, height, "width", None),
    )
    flat = P(names)
    out_specs = (P(tm, (*height, "width"), None, None), flat, flat, flat)
    return jax.shard_map(shards, mesh=split, in_specs=in_specs, out_specs=out_specs, check_vma=False)
```

```python
import math

import jax
import jax.numpy as jnp
from jax import lax
from jax.experimental import pallas as pl
from jax.experimental.pallas import tpu as pltpu
from jax.sharding import Mesh, PartitionSpec as P

F32 = jnp.float32
BF16 = jnp.bfloat16
VMEM_LIMIT = 48 * 1024 * 1024

FR = 4
ROWS = 16
WIN = 16
OWN = 8
EDGE = 4
CH = 256
TAPS = 27
SHARE = 54
PIECE = 56
UP_ROWS = 32


def slope_of(values, sigma):
    return sigma * (1.0 + values * (1.0 - sigma))


def nt(lhs, rhs):
    return lax.dot_general(lhs, rhs, (((1,), (1,)), ((), ())), preferred_element_type=F32)


def nn(lhs, rhs):
    return jnp.dot(lhs, rhs, preferred_element_type=F32)


def fill_table(table, slot, block, forward):
    wide = block.astype(F32)
    before = pltpu.roll(wide, 1, axis=1).astype(BF16)
    after = pltpu.roll(wide, WIN - 1, axis=1).astype(BF16)
    table[slot, 1 : ROWS + 1, :, 0:CH] = before if forward else after
    table[slot, 1 : ROWS + 1, :, CH : 2 * CH] = block
    table[slot, 1 : ROWS + 1, :, 2 * CH : 3 * CH] = after if forward else before


def fill_own_table(table, slot, block):
    wide = block.astype(F32)
    for tap in range(3):
        moved = pltpu.roll(wide, WIN - (EDGE + 1 - tap), axis=1)
        table[slot, 1 : ROWS + 1, :, tap * CH : (tap + 1) * CH] = moved[:, :OWN].astype(BF16)


def clear_border(table):
    frames, _, columns, lanes = table.shape
    border = jnp.zeros((frames, columns, lanes), BF16)
    table[:, 0] = border
    table[:, ROWS + 1] = border


def own_columns(block):
    return pltpu.roll(block.astype(F32), WIN - EDGE, axis=1)[:, :OWN]


def forward_taps(table, step, frames, weights, total):
    rows = frames * ROWS * WIN
    for tap in range(3):
        lhs = table[pl.ds(step, frames), tap : tap + ROWS].reshape(rows, 3 * CH)
        total[:rows] += nn(lhs, weights[0, tap].reshape(3 * CH, CH))


def backward_taps(table, start, frames, columns, weights, total):
    step = pl.program_id(0)
    for tap_h in range(3):
        part = None
        for tap_w in range(3):
            lanes = slice(tap_w * CH, (tap_w + 1) * CH)
            lhs = table[pl.ds(start + 2 - step, frames), 2 - tap_h : 2 - tap_h + ROWS, :, lanes]
            more = nt(lhs.reshape(frames * ROWS * columns, CH), weights[0, tap_h, tap_w])
            part = more if part is None else part + more
        total[...] += part


def frame_of(total, frame, columns):
    rows = ROWS * columns
    return total[frame * rows : (frame + 1) * rows].reshape(ROWS, columns, CH)


def forward_kernel(core_ref, mine, other, first, second, mask, act, slope, summed, up_act, table, total):
    step = pl.program_id(0)
    core = core_ref[0]
    sources = ((mine, core), (other, 1 - core))

    @pl.when(step == 0)
    def _():
        clear_border(table)
        for source, which in sources:
            for frame in range(FR):
                slot = 2 * which + (frame if frame < 2 else frame + 2)
                fill_table(table, slot, source[:, frame], True)
        total[...] = jnp.zeros_like(total)

    @pl.when(step < 3)
    def _():
        forward_taps(table, step, FR + 2, first, total)

    @pl.when(step == 2)
    def _():
        for frame in range(FR + 2):
            values = frame_of(total, frame, WIN)
            sigma = jax.nn.sigmoid(values)
            result = (values * sigma * mask[...]).astype(BF16)
            act[frame] = result
            fill_table(table, frame, result, True)
            if frame >= 2:
                slope[frame - 2] = slope_of(values, sigma)
        total[...] = jnp.zeros_like(total)

    @pl.when(step >= 3)
    def _():
        forward_taps(table, step - 3, FR, second, total)

    @pl.when(step == 5)
    def _():
        rows = ROWS * WIN
        for source, which in sources:
            for frame in range(2):
                place = 2 * which + frame
                values = total[pl.ds(pl.multiple_of(place * rows, rows), rows)].reshape(ROWS, WIN, CH)
                values = values + source[:, 2 + frame].astype(F32)
                summed[place] = values
                up_act[place] = (values * jax.nn.sigmoid(values)).astype(BF16)


def hidden_kernel(block, later, slope, weights, mask, grad_hidden, head, table, total):
    @pl.when(pl.program_id(0) == 0)
    def _():
        clear_border(table)
        for frame in range(FR):
            fill_table(table, frame, block[frame], False)
        for frame in range(2):
            fill_table(table, FR + frame, later[frame], False)
        total[...] = jnp.zeros_like(total)

    backward_taps(table, 0, FR, WIN, weights, total)

    @pl.when(pl.program_id(0) == 2)
    def _():
        for frame in range(FR):
            result = (frame_of(total, frame, WIN) * slope[frame] * mask[...]).astype(BF16)
            grad_hidden[frame] = result
            if frame < 2:
                head[frame] = result


def features_kernel(core_ref, block, later, grad_sum, weights, grad_features, table, total):
    core = core_ref[0]

    @pl.when(pl.program_id(0) == 0)
    def _():
        clear_border(table)
        for frame in range(FR):
            fill_own_table(table, frame, block[frame])
        for frame in range(2):
            fill_own_table(table, FR + frame, later[frame])
        total[...] = jnp.zeros_like(total)

    backward_taps(table, 2 * core, 2, OWN, weights, total)

    @pl.when(pl.program_id(0) == 2)
    def _():
        for frame in range(2):
            values = frame_of(total, frame, OWN) + own_columns(grad_sum[2 * core + frame])
            grad_features[:, frame] = values.astype(BF16)


def cotangent_kernel(core_ref, mine, other, weights, summed, mask, grad_sum, head, table):
    core = core_ref[0]
    border = jnp.zeros((FR, WIN, 4 * CH), BF16)
    table[:, 0, 0] = border
    table[:, ROWS, 1] = border
    for source, which in ((mine, core), (other, 1 - core)):
        for frame in range(2):
            slot = 2 * which + frame
            for parity in range(2):
                fine = source[:, frame, :, parity].reshape(ROWS, WIN, 2 * CH)
                even, odd = fine[:, :, :CH], fine[:, :, CH:]
                before = pltpu.roll(odd.astype(F32), 1, axis=1).astype(BF16)
                after = pltpu.roll(even.astype(F32), WIN - 1, axis=1).astype(BF16)
                low = 0 if parity == 0 else 1
                put = (slot, slice(low, low + ROWS), 1 - parity)
                table[put + (slice(None), slice(0, CH))] = before
                table[put + (slice(None), slice(CH, 2 * CH))] = even
                table[put + (slice(None), slice(2 * CH, 3 * CH))] = odd
                table[put + (slice(None), slice(3 * CH, 4 * CH))] = after
    for frame in range(FR):
        part = None
        for tap in range(4):
            for column in range(4):
                lhs = table[frame, tap // 2 : tap // 2 + ROWS, tap % 2, :, column * CH : (column + 1) * CH]
                more = nt(lhs.reshape(ROWS * WIN, CH), weights[tap, column])
                part = more if part is None else part + more
        grad_act = part.reshape(ROWS, WIN, CH).astype(BF16).astype(F32)
        values = summed[frame]
        grad = grad_act * slope_of(values, jax.nn.sigmoid(values)) * mask[...]
        grad_sum[frame] = grad.astype(BF16)
        if frame < 2:
            head[frame] = grad.astype(BF16)


def up_grad_kernel(core_ref, act, mine, other, out, table, flipped):
    core = core_ref[0]
    border = jnp.zeros((FR, OWN, 4 * CH), BF16)
    table[:, 0, 0] = border
    table[:, ROWS, 1] = border
    for source, which in ((mine, core), (other, 1 - core)):
        for frame in range(2):
            slot = 2 * which + frame
            for parity in range(2):
                fine = source[:, frame, :, parity].reshape(ROWS, WIN, 2 * CH).astype(F32)
                even, odd = fine[:, :, :CH], fine[:, :, CH:]
                low = 0 if parity == 0 else 1
                put = (slot, slice(low, low + ROWS), 1 - parity)
                for column, (values, shift) in enumerate(((odd, -1), (even, 0), (odd, 0), (even, 1))):
                    moved = pltpu.roll(values, WIN - (EDGE + shift), axis=1)[:, :OWN].astype(BF16)
                    table[put + (slice(None), slice(column * CH, (column + 1) * CH))] = moved
    for frame in range(FR):
        rows = ROWS * OWN
        flipped[:, frame * rows : (frame + 1) * rows] = jnp.transpose(
            own_columns(act[frame]).reshape(rows, CH)
        ).astype(BF16)
    lanes = pl.ds(pl.multiple_of(core * 2 * CH, 2 * CH), 2 * CH)
    for tap in range(4):
        rhs = table[:, tap // 2 : tap // 2 + ROWS, tap % 2, :, lanes]
        result = nn(flipped[...], rhs.reshape(FR * ROWS * OWN, 2 * CH))
        for half in range(2):
            for piece in range(8):
                out[tap * 16 + half * 8 + piece] = result[
                    piece * 32 : (piece + 1) * 32, half * CH : (half + 1) * CH
                ].astype(BF16)


def tap_sums(frames, block, table, flipped, sums):
    clear_border(table)
    column = lax.broadcasted_iota(jnp.int32, (ROWS, WIN, CH), 1)
    own = (column >= EDGE) & (column < EDGE + OWN)
    for frame in range(FR):
        fill_table(table, frame, jnp.where(own, block[frame].astype(F32), 0.0).astype(BF16), False)
    rows = ROWS * WIN
    for slot, values in frames:
        lanes = pl.ds(pl.multiple_of(slot * rows, rows), rows)
        flipped[:, lanes] = jnp.transpose(values.astype(F32).reshape(rows, CH)).astype(BF16)
    sums[TAPS * CH :] = jnp.zeros((8, CH), F32)
    for tap_t in range(3):
        lhs = flipped[:, tap_t * rows : (tap_t + FR) * rows]
        for tap_h in range(3):
            rhs = table[:, 2 - tap_h : 2 - tap_h + ROWS]
            result = nn(lhs, rhs.reshape(FR * rows, 3 * CH))
            for tap_w in range(3):
                at = (tap_t * 9 + tap_h * 3 + tap_w) * CH
                sums[at : at + CH] = result[:, tap_w * CH : (tap_w + 1) * CH]


def piece_of(sums, owner, member):
    at = SHARE * member
    start = pl.multiple_of(16 * SHARE * owner + at // 8 * 8, 8)
    return sums[pl.ds(start, PIECE + 8)][at % 8 : at % 8 + PIECE]


def second_grad_kernel(place, act, block, up, out, table, flipped, sums):
    tap_sums([(frame, act[frame]) for frame in range(FR + 2)], block, table, flipped, sums)
    for step in range(4):
        group = lax.rem(place[1] + step, 4)
        for member in range(16):
            chunk = member * 4 + step
            out[chunk, :UP_ROWS] = up[group * 16 + member]
            out[chunk, UP_ROWS:] = piece_of(sums, 2 * group + place[0], member).astype(BF16)


def first_grad_kernel(place, mine, other, block, own, next_one, next_two, next_three, table, flipped, sums):
    core = place[0]
    frames = []
    for frame in range(2):
        before = jnp.where(core == 1, mine[:, frame].astype(F32), other[:, frame].astype(F32))
        frames.append((frame, before))
        frames.append((2 + 2 * core + frame, mine[:, 2 + frame]))
        frames.append((4 - 2 * core + frame, other[:, 2 + frame]))
    tap_sums(frames, block, table, flipped, sums)
    for step, out in enumerate((own, next_one, next_two, next_three)):
        group = lax.rem(place[1] + step, 4)
        for member in range(16):
            out[member] = piece_of(sums, 2 * group + place[0], member).astype(BF16)


def whole(shape):
    zeros = (0,) * len(shape)
    return pl.BlockSpec(shape, lambda *_: zeros)


SMEM = pl.BlockSpec(memory_space=pltpu.SMEM)


def tap_weights(begin=0):
    return pl.BlockSpec((1, 3, 3, CH, CH), lambda step: (jnp.clip(step - begin, 0, 2), 0, 0, 0, 0))


def call(kernel, grid, args, specs, outs, scratch, flops):
    shapes = [jax.ShapeDtypeStruct(shape, dtype) for shape, dtype in outs]
    moved = sum(math.prod(a.shape) * a.dtype.itemsize for a in args)
    moved += sum(math.prod(s.shape) * s.dtype.itemsize for s in shapes)
    single = len(shapes) == 1
    return pl.pallas_call(
        kernel,
        out_shape=shapes[0] if single else shapes,
        grid=grid,
        in_specs=specs,
        out_specs=whole(shapes[0].shape) if single else [whole(s.shape) for s in shapes],
        scratch_shapes=scratch,
        compiler_params=pltpu.CompilerParams(vmem_limit_bytes=VMEM_LIMIT),
        cost_estimate=pl.CostEstimate(flops=int(flops), bytes_accessed=moved, transcendentals=0),
    )(*args)


def shift(value, axis, step):
    count = lax.axis_size(axis)
    return lax.ppermute(value, axis, [(i, i + step) for i in range(count) if 0 <= i + step < count])


def over_y(value, step):
    return lax.ppermute(value, "y", [(i, (i + step) % 4) for i in range(4)])


def shards(features, conv_first, conv_second, up_kernel, cotangent):
    core = lax.axis_index("core")
    height = 2 * lax.axis_index("z") + lax.axis_index("x_hi")
    width = lax.axis_index("width")
    core_arg = core.astype(jnp.int32).reshape(1)
    place = jnp.stack([core, lax.axis_index("y")]).astype(jnp.int32)
    window = 8 * width + height
    columns = OWN * window - EDGE + jnp.arange(WIN)
    inside = ((columns >= 0) & (columns < 128)).astype(F32)
    mask = jnp.broadcast_to(inside[:, None], (WIN, CH))
    act_shape = (FR, ROWS, WIN, CH)
    two_frames = (2, ROWS, WIN, CH)
    six_frames = (FR + 2, ROWS, WIN, CH)
    table = pltpu.VMEM((FR + 2, ROWS + 2, WIN, 3 * CH), BF16)
    own_table = pltpu.VMEM((FR + 2, ROWS + 2, OWN, 3 * CH), BF16)
    total = pltpu.VMEM((FR * ROWS * WIN, CH), F32)
    tap_flops = 2 * FR * ROWS * WIN * CH * CH

    paired = cotangent.reshape(2, 4, 64, 2 * CH)
    edge = jnp.where(width == 0, paired[:, :, 64 - EDGE :], paired[:, :, :EDGE])
    edge = lax.ppermute(edge, "width", [(0, 1), (1, 0)])
    frames = features[:, 0]
    before, edge = lax.optimization_barrier((shift(frames, "y", 1), edge))
    frames = jnp.concatenate([before, frames], axis=0)
    padded = jnp.pad(frames, ((0, 0), (EDGE, EDGE), (0, 0))).reshape(4, 17, OWN, CH)
    windows = jnp.concatenate([padded[:, :-1], padded[:, 1:]], axis=2)
    windows = windows.reshape(4, 2, 8, WIN, CH).transpose(2, 1, 0, 3, 4).reshape(16, 4, WIN, CH)
    block = lax.all_to_all(windows, ("z", "x_hi", "width"), 0, 0, tiled=True)

    nothing = jnp.zeros_like(edge)
    low, high = jnp.where(width == 0, nothing, edge), jnp.where(width == 0, edge, nothing)
    paired = jnp.concatenate([low, paired, high], axis=2).reshape(2, 4, 9, OWN, 2 * CH)
    fine = jnp.concatenate([paired[:, :, :-1], paired[:, :, 1:]], axis=3).transpose(2, 0, 1, 3, 4)
    fine, block = lax.optimization_barrier((fine.reshape(64, WIN, 2 * CH), block))
    swap = [(0, 1), (1, 0)]
    other_block = lax.ppermute(block, "core", swap)
    mine = lax.all_to_all(fine.reshape(8, 8, WIN, 2 * CH), ("z", "x_hi"), 0, 0, tiled=True).reshape(8, 2, 2, 2, WIN, 2 * CH)

    first_act, first_slope, summed, up_act = call(
        forward_kernel, (6,), (core_arg, block, other_block, conv_first, conv_second, mask),
        [SMEM, whole(block.shape), whole(block.shape), tap_weights(0), tap_weights(3), whole(mask.shape)],
        [(six_frames, BF16), (act_shape, F32), (act_shape, F32), (act_shape, BF16)],
        [pltpu.VMEM((FR + 4, ROWS + 2, WIN, 3 * CH), BF16), pltpu.VMEM(((FR + 2) * ROWS * WIN, CH), F32)],
        67 * tap_flops,
    )
    mine, up_act = lax.optimization_barrier((mine, up_act))
    other = lax.ppermute(mine, "core", swap)
    grad_sum, sum_head = call(
        cotangent_kernel, (), (core_arg, mine, other, up_kernel, summed, mask),
        [SMEM, whole(mine.shape), whole(mine.shape), whole(up_kernel.shape), whole(act_shape), whole(mask.shape)],
        [(act_shape, BF16), (two_frames, BF16)], [pltpu.VMEM((FR, ROWS + 1, 2, WIN, 4 * CH), BF16)], 16 * tap_flops,
    )
    later = shift(sum_head, "y", -1)
    up_act, grad_sum = lax.optimization_barrier((up_act, grad_sum))
    up_part = call(
        up_grad_kernel, (), (core_arg, up_act, mine, other),
        [SMEM, whole(act_shape), whole(mine.shape), whole(mine.shape)],
        [((64, 32, CH), BF16)],
        [pltpu.VMEM((FR, ROWS + 1, 2, OWN, 4 * CH), BF16), pltpu.VMEM((CH, FR * ROWS * OWN), BF16)], 4 * tap_flops,
    )
    grad_table = pltpu.VMEM((FR, ROWS + 2, WIN, 3 * CH), BF16)
    grad_scratch = [grad_table, pltpu.VMEM((CH, (FR + 2) * ROWS * WIN), BF16), pltpu.VMEM((TAPS * CH + 8, CH), F32)]
    early = call(
        second_grad_kernel, (), (place, first_act, grad_sum, up_part),
        [SMEM, whole(six_frames), whole(act_shape), whole(up_part.shape)],
        [((64, UP_ROWS + PIECE, CH), BF16)], grad_scratch, 27 * tap_flops,
    )
    early, later = lax.optimization_barrier((early, later))
    early = lax.all_to_all(early, ("z", "x_hi", "width"), 0, 0, tiled=True)

    grad_hidden, hidden_head = call(
        hidden_kernel, (3,), (grad_sum, later, first_slope, conv_second, mask),
        [whole(act_shape), whole(later.shape), whole(act_shape), tap_weights(), whole(mask.shape)],
        [(act_shape, BF16), (two_frames, BF16)], [table, total], 27 * tap_flops,
    )
    later_hidden = lax.ppermute(hidden_head, ("y", "core"), [(2 * i + 1, 2 * i - 1) for i in range(1, 4)])
    blocks = call(
        first_grad_kernel, (), (place, block, other_block, grad_hidden),
        [SMEM, whole(block.shape), whole(block.shape), whole(act_shape)],
        [((16, PIECE, CH), BF16)] * 4, grad_scratch, 27 * tap_flops,
    )
    arrived = [blocks[0]]
    for step in (2, 1, 3):
        arrived.append(over_y(blocks[step], step))
    tied_hidden, _ = lax.optimization_barrier((grad_hidden, blocks[0]))
    rows_out = call(
        features_kernel, (3,), (core_arg, tied_hidden, later_hidden, grad_sum, conv_first),
        [SMEM, whole(act_shape), whole(later_hidden.shape), whole(act_shape), tap_weights()],
        [((ROWS, 2, OWN, CH), BF16)], [own_table, pltpu.VMEM((2 * ROWS * OWN, CH), F32)], 7 * tap_flops,
    )

    first_sum = sum(value.astype(F32) for value in arrived).astype(BF16)
    late = jnp.concatenate([rows_out.reshape(16, 2 * OWN, CH), first_sum], axis=1)
    late, early = lax.optimization_barrier((late, early))
    early = jnp.sum(early.reshape(16, 4, UP_ROWS + PIECE, CH).astype(F32), axis=0)
    early_total = early[0]
    for step in (2, 1, 3):
        early_total += over_y(early[step].astype(BF16), step).astype(F32)
    late = lax.all_to_all(late, ("z", "x_hi", "width"), 0, 0, tiled=True)

    factor = 1.0 / math.sqrt(32768)
    early = early_total * factor
    returned = late[:, : 2 * OWN].reshape(8, 2, 2, OWN, CH).transpose(2, 1, 0, 3, 4)
    first_share = jnp.sum(late[:, 2 * OWN : 2 * OWN + SHARE].astype(F32), axis=0) * factor
    return (
        returned.reshape(2, 1, 128, CH),
        first_share.reshape(-1),
        early[UP_ROWS : UP_ROWS + SHARE].reshape(-1),
        early[:UP_ROWS].reshape(-1),
    )


def solution(mesh):
    names = ("y", "core", "z", "x_hi", "width")
    split = Mesh(mesh.devices.reshape(4, 2, 4, 2, 2), names)
    tm, height = ("y", "core"), ("z", "x_hi")
    in_specs = (
        P(tm, (*height, "width"), None, None),
        P(),
        P(),
        P(),
        P(tm, height, "width", None),
    )
    flat = P(names)
    out_specs = (P(tm, (*height, "width"), None, None), flat, flat, flat)
    return jax.shard_map(shards, mesh=split, in_specs=in_specs, out_specs=out_specs, check_vma=False)
```

```python
import math

import jax
import jax.numpy as jnp
from jax import lax
from jax.experimental import pallas as pl
from jax.experimental.pallas import tpu as pltpu
from jax.sharding import Mesh, PartitionSpec as P

F32 = jnp.float32
BF16 = jnp.bfloat16
VMEM_LIMIT = 48 * 1024 * 1024

FR = 4
ROWS = 16
WIN = 16
OWN = 8
EDGE = 4
CH = 256
TAPS = 27
SHARE = 54
PIECE = 56
UP_ROWS = 32


def slope_of(values, sigma):
    return sigma * (1.0 + values * (1.0 - sigma))


def nt(lhs, rhs):
    return lax.dot_general(lhs, rhs, (((1,), (1,)), ((), ())), preferred_element_type=F32)


def nn(lhs, rhs):
    return jnp.dot(lhs, rhs, preferred_element_type=F32)


def fill_table(table, slot, block, forward):
    wide = block.astype(F32)
    before = pltpu.roll(wide, 1, axis=1).astype(BF16)
    after = pltpu.roll(wide, WIN - 1, axis=1).astype(BF16)
    table[slot, 1 : ROWS + 1, :, 0:CH] = before if forward else after
    table[slot, 1 : ROWS + 1, :, CH : 2 * CH] = block
    table[slot, 1 : ROWS + 1, :, 2 * CH : 3 * CH] = after if forward else before


def fill_own_table(table, slot, block):
    wide = block.astype(F32)
    for tap in range(3):
        moved = pltpu.roll(wide, WIN - (EDGE + 1 - tap), axis=1)
        table[slot, 1 : ROWS + 1, :, tap * CH : (tap + 1) * CH] = moved[:, :OWN].astype(BF16)


def clear_border(table):
    frames, _, columns, lanes = table.shape
    border = jnp.zeros((frames, columns, lanes), BF16)
    table[:, 0] = border
    table[:, ROWS + 1] = border


def own_columns(block):
    return pltpu.roll(block.astype(F32), WIN - EDGE, axis=1)[:, :OWN]


def forward_taps(table, step, frames, weights, total):
    rows = frames * ROWS * WIN
    for tap in range(3):
        lhs = table[pl.ds(step, frames), tap : tap + ROWS].reshape(rows, 3 * CH)
        total[:rows] += nn(lhs, weights[0, tap].reshape(3 * CH, CH))


def backward_taps(table, start, frames, columns, weights, total):
    step = pl.program_id(0)
    for tap_h in range(3):
        part = None
        for tap_w in range(3):
            lanes = slice(tap_w * CH, (tap_w + 1) * CH)
            lhs = table[pl.ds(start + 2 - step, frames), 2 - tap_h : 2 - tap_h + ROWS, :, lanes]
            more = nt(lhs.reshape(frames * ROWS * columns, CH), weights[0, tap_h, tap_w])
            part = more if part is None else part + more
        total[...] += part


def frame_of(total, frame, columns):
    rows = ROWS * columns
    return total[frame * rows : (frame + 1) * rows].reshape(ROWS, columns, CH)


def forward_kernel(core_ref, mine, other, first, second, mask, act, slope, summed, up_act, table, total):
    step = pl.program_id(0)
    core = core_ref[0]
    sources = ((mine, core), (other, 1 - core))

    @pl.when(step == 0)
    def _():
        clear_border(table)
        for source, which in sources:
            for frame in range(FR):
                slot = 2 * which + (frame if frame < 2 else frame + 2)
                fill_table(table, slot, source[:, frame], True)
        total[...] = jnp.zeros_like(total)

    @pl.when(step < 3)
    def _():
        forward_taps(table, step, FR + 2, first, total)

    @pl.when(step == 2)
    def _():
        for frame in range(FR + 2):
            values = frame_of(total, frame, WIN)
            sigma = jax.nn.sigmoid(values)
            result = (values * sigma * mask[...]).astype(BF16)
            act[frame] = result
            fill_table(table, frame, result, True)
            if frame >= 2:
                slope[frame - 2] = slope_of(values, sigma)
        total[...] = jnp.zeros_like(total)

    @pl.when(step >= 3)
    def _():
        forward_taps(table, step - 3, FR, second, total)

    @pl.when(step == 5)
    def _():
        rows = ROWS * WIN
        for source, which in sources:
            for frame in range(2):
                place = 2 * which + frame
                values = total[pl.ds(pl.multiple_of(place * rows, rows), rows)].reshape(ROWS, WIN, CH)
                values = values + source[:, 2 + frame].astype(F32)
                summed[place] = values
                up_act[place] = (values * jax.nn.sigmoid(values)).astype(BF16)


def hidden_kernel(block, later, slope, weights, mask, grad_hidden, head, table, total):
    @pl.when(pl.program_id(0) == 0)
    def _():
        clear_border(table)
        for frame in range(FR):
            fill_table(table, frame, block[frame], False)
        for frame in range(2):
            fill_table(table, FR + frame, later[frame], False)
        total[...] = jnp.zeros_like(total)

    backward_taps(table, 0, FR, WIN, weights, total)

    @pl.when(pl.program_id(0) == 2)
    def _():
        for frame in range(FR):
            result = (frame_of(total, frame, WIN) * slope[frame] * mask[...]).astype(BF16)
            grad_hidden[frame] = result
            if frame < 2:
                head[frame] = result


def features_kernel(core_ref, block, later, grad_sum, weights, grad_features, table, total):
    core = core_ref[0]

    @pl.when(pl.program_id(0) == 0)
    def _():
        clear_border(table)
        for frame in range(FR):
            fill_own_table(table, frame, block[frame])
        for frame in range(2):
            fill_own_table(table, FR + frame, later[frame])
        total[...] = jnp.zeros_like(total)

    backward_taps(table, 2 * core, 2, OWN, weights, total)

    @pl.when(pl.program_id(0) == 2)
    def _():
        for frame in range(2):
            values = frame_of(total, frame, OWN) + own_columns(grad_sum[2 * core + frame])
            grad_features[:, frame] = values.astype(BF16)


def cotangent_kernel(core_ref, mine, other, weights, summed, mask, grad_sum, head, table):
    core = core_ref[0]
    border = jnp.zeros((FR, WIN, 4 * CH), BF16)
    table[:, 0, 0] = border
    table[:, ROWS, 1] = border
    for source, which in ((mine, core), (other, 1 - core)):
        for frame in range(2):
            slot = 2 * which + frame
            for parity in range(2):
                fine = source[:, frame, :, parity].reshape(ROWS, WIN, 2 * CH)
                even, odd = fine[:, :, :CH], fine[:, :, CH:]
                before = pltpu.roll(odd.astype(F32), 1, axis=1).astype(BF16)
                after = pltpu.roll(even.astype(F32), WIN - 1, axis=1).astype(BF16)
                low = 0 if parity == 0 else 1
                put = (slot, slice(low, low + ROWS), 1 - parity)
                table[put + (slice(None), slice(0, CH))] = before
                table[put + (slice(None), slice(CH, 2 * CH))] = even
                table[put + (slice(None), slice(2 * CH, 3 * CH))] = odd
                table[put + (slice(None), slice(3 * CH, 4 * CH))] = after
    for frame in range(FR):
        part = None
        for tap in range(4):
            for column in range(4):
                lhs = table[frame, tap // 2 : tap // 2 + ROWS, tap % 2, :, column * CH : (column + 1) * CH]
                more = nt(lhs.reshape(ROWS * WIN, CH), weights[tap, column])
                part = more if part is None else part + more
        grad_act = part.reshape(ROWS, WIN, CH).astype(BF16).astype(F32)
        values = summed[frame]
        grad = grad_act * slope_of(values, jax.nn.sigmoid(values)) * mask[...]
        grad_sum[frame] = grad.astype(BF16)
        if frame < 2:
            head[frame] = grad.astype(BF16)


def up_grad_kernel(core_ref, act, mine, other, out, table, flipped):
    core = core_ref[0]
    border = jnp.zeros((FR, OWN, 4 * CH), BF16)
    table[:, 0, 0] = border
    table[:, ROWS, 1] = border
    for source, which in ((mine, core), (other, 1 - core)):
        for frame in range(2):
            slot = 2 * which + frame
            for parity in range(2):
                fine = source[:, frame, :, parity].reshape(ROWS, WIN, 2 * CH).astype(F32)
                even, odd = fine[:, :, :CH], fine[:, :, CH:]
                low = 0 if parity == 0 else 1
                put = (slot, slice(low, low + ROWS), 1 - parity)
                for column, (values, shift) in enumerate(((odd, -1), (even, 0), (odd, 0), (even, 1))):
                    moved = pltpu.roll(values, WIN - (EDGE + shift), axis=1)[:, :OWN].astype(BF16)
                    table[put + (slice(None), slice(column * CH, (column + 1) * CH))] = moved
    for frame in range(FR):
        rows = ROWS * OWN
        flipped[:, frame * rows : (frame + 1) * rows] = jnp.transpose(
            own_columns(act[frame]).reshape(rows, CH)
        ).astype(BF16)
    lanes = pl.ds(pl.multiple_of(core * 2 * CH, 2 * CH), 2 * CH)
    for tap in range(4):
        rhs = table[:, tap // 2 : tap // 2 + ROWS, tap % 2, :, lanes]
        result = nn(flipped[...], rhs.reshape(FR * ROWS * OWN, 2 * CH))
        for half in range(2):
            for piece in range(8):
                out[tap * 16 + half * 8 + piece] = result[
                    piece * 32 : (piece + 1) * 32, half * CH : (half + 1) * CH
                ].astype(BF16)


def tap_sums(frames, block, table, flipped, sums):
    clear_border(table)
    column = lax.broadcasted_iota(jnp.int32, (ROWS, WIN, CH), 1)
    own = (column >= EDGE) & (column < EDGE + OWN)
    for frame in range(FR):
        fill_table(table, frame, jnp.where(own, block[frame].astype(F32), 0.0).astype(BF16), False)
    rows = ROWS * WIN
    for slot, values in frames:
        lanes = pl.ds(pl.multiple_of(slot * rows, rows), rows)
        flipped[:, lanes] = jnp.transpose(values.astype(F32).reshape(rows, CH)).astype(BF16)
    sums[TAPS * CH :] = jnp.zeros((8, CH), F32)
    for tap_t in range(3):
        lhs = flipped[:, tap_t * rows : (tap_t + FR) * rows]
        for tap_h in range(3):
            rhs = table[:, 2 - tap_h : 2 - tap_h + ROWS]
            result = nn(lhs, rhs.reshape(FR * rows, 3 * CH))
            for tap_w in range(3):
                at = (tap_t * 9 + tap_h * 3 + tap_w) * CH
                sums[at : at + CH] = result[:, tap_w * CH : (tap_w + 1) * CH]


def piece_of(sums, owner, member):
    at = SHARE * member
    start = pl.multiple_of(16 * SHARE * owner + at // 8 * 8, 8)
    return sums[pl.ds(start, PIECE + 8)][at % 8 : at % 8 + PIECE]


def second_grad_kernel(place, act, block, up, out, table, flipped, sums):
    tap_sums([(frame, act[frame]) for frame in range(FR + 2)], block, table, flipped, sums)
    for step in range(4):
        group = lax.rem(place[1] + step, 4)
        for member in range(16):
            chunk = member * 4 + step
            out[chunk, :UP_ROWS] = up[group * 16 + member]
            out[chunk, UP_ROWS:] = piece_of(sums, 2 * group + place[0], member).astype(BF16)


def first_grad_kernel(place, mine, other, block, own, next_one, next_two, next_three, table, flipped, sums):
    core = place[0]
    frames = []
    for frame in range(2):
        before = jnp.where(core == 1, mine[:, frame].astype(F32), other[:, frame].astype(F32))
        frames.append((frame, before))
        frames.append((2 + 2 * core + frame, mine[:, 2 + frame]))
        frames.append((4 - 2 * core + frame, other[:, 2 + frame]))
    tap_sums(frames, block, table, flipped, sums)
    for step, out in enumerate((own, next_one, next_two, next_three)):
        group = lax.rem(place[1] + step, 4)
        for member in range(16):
            out[member] = piece_of(sums, 2 * group + place[0], member).astype(BF16)


def whole(shape):
    zeros = (0,) * len(shape)
    return pl.BlockSpec(shape, lambda *_: zeros)


SMEM = pl.BlockSpec(memory_space=pltpu.SMEM)


def tap_weights(begin=0):
    return pl.BlockSpec((1, 3, 3, CH, CH), lambda step: (jnp.clip(step - begin, 0, 2), 0, 0, 0, 0))


def call(kernel, grid, args, specs, outs, scratch, flops):
    shapes = [jax.ShapeDtypeStruct(shape, dtype) for shape, dtype in outs]
    moved = sum(math.prod(a.shape) * a.dtype.itemsize for a in args)
    moved += sum(math.prod(s.shape) * s.dtype.itemsize for s in shapes)
    single = len(shapes) == 1
    return pl.pallas_call(
        kernel,
        out_shape=shapes[0] if single else shapes,
        grid=grid,
        in_specs=specs,
        out_specs=whole(shapes[0].shape) if single else [whole(s.shape) for s in shapes],
        scratch_shapes=scratch,
        compiler_params=pltpu.CompilerParams(vmem_limit_bytes=VMEM_LIMIT),
        cost_estimate=pl.CostEstimate(flops=int(flops), bytes_accessed=moved, transcendentals=0),
    )(*args)


def shift(value, axis, step):
    count = lax.axis_size(axis)
    return lax.ppermute(value, axis, [(i, i + step) for i in range(count) if 0 <= i + step < count])


def over_y(value, step):
    return lax.ppermute(value, "y", [(i, (i + step) % 4) for i in range(4)])


def shards(features, conv_first, conv_second, up_kernel, cotangent):
    core = lax.axis_index("core")
    height = 2 * lax.axis_index("z") + lax.axis_index("x_hi")
    width = lax.axis_index("width")
    core_arg = core.astype(jnp.int32).reshape(1)
    place = jnp.stack([core, lax.axis_index("y")]).astype(jnp.int32)
    window = 8 * width + height
    columns = OWN * window - EDGE + jnp.arange(WIN)
    inside = ((columns >= 0) & (columns < 128)).astype(F32)
    mask = jnp.broadcast_to(inside[:, None], (WIN, CH))
    act_shape = (FR, ROWS, WIN, CH)
    two_frames = (2, ROWS, WIN, CH)
    six_frames = (FR + 2, ROWS, WIN, CH)
    table = pltpu.VMEM((FR + 2, ROWS + 2, WIN, 3 * CH), BF16)
    own_table = pltpu.VMEM((FR + 2, ROWS + 2, OWN, 3 * CH), BF16)
    total = pltpu.VMEM((FR * ROWS * WIN, CH), F32)
    tap_flops = 2 * FR * ROWS * WIN * CH * CH

    paired = cotangent.reshape(2, 4, 64, 2 * CH)
    edge = jnp.where(width == 0, paired[:, :, 64 - EDGE :], paired[:, :, :EDGE])
    edge = lax.ppermute(edge, "width", [(0, 1), (1, 0)])
    frames = features[:, 0]
    before, edge = lax.optimization_barrier((shift(frames, "y", 1), edge))
    frames = jnp.concatenate([before, frames], axis=0)
    padded = jnp.pad(frames, ((0, 0), (EDGE, EDGE), (0, 0))).reshape(4, 17, OWN, CH)
    windows = jnp.concatenate([padded[:, :-1], padded[:, 1:]], axis=2)
    windows = windows.reshape(4, 2, 8, WIN, CH).transpose(2, 1, 0, 3, 4).reshape(16, 4, WIN, CH)
    block = lax.all_to_all(windows, ("z", "x_hi", "width"), 0, 0, tiled=True)

    nothing = jnp.zeros_like(edge)
    low, high = jnp.where(width == 0, nothing, edge), jnp.where(width == 0, edge, nothing)
    paired = jnp.concatenate([low, paired, high], axis=2).reshape(2, 4, 9, OWN, 2 * CH)
    fine = jnp.concatenate([paired[:, :, :-1], paired[:, :, 1:]], axis=3).transpose(2, 0, 1, 3, 4)
    fine, block = lax.optimization_barrier((fine.reshape(64, WIN, 2 * CH), block))
    swap = [(0, 1), (1, 0)]
    other_block = lax.ppermute(block, "core", swap)
    mine = lax.all_to_all(fine.reshape(8, 8, WIN, 2 * CH), ("z", "x_hi"), 0, 0, tiled=True).reshape(8, 2, 2, 2, WIN, 2 * CH)

    first_act, first_slope, summed, up_act = call(
        forward_kernel, (6,), (core_arg, block, other_block, conv_first, conv_second, mask),
        [SMEM, whole(block.shape), whole(block.shape), tap_weights(0), tap_weights(3), whole(mask.shape)],
        [(six_frames, BF16), (act_shape, F32), (act_shape, F32), (act_shape, BF16)],
        [pltpu.VMEM((FR + 4, ROWS + 2, WIN, 3 * CH), BF16), pltpu.VMEM(((FR + 2) * ROWS * WIN, CH), F32)],
        67 * tap_flops,
    )
    mine, up_act = lax.optimization_barrier((mine, up_act))
    other = lax.ppermute(mine, "core", swap)
    grad_sum, sum_head = call(
        cotangent_kernel, (), (core_arg, mine, other, up_kernel, summed, mask),
        [SMEM, whole(mine.shape), whole(mine.shape), whole(up_kernel.shape), whole(act_shape), whole(mask.shape)],
        [(act_shape, BF16), (two_frames, BF16)], [pltpu.VMEM((FR, ROWS + 1, 2, WIN, 4 * CH), BF16)], 16 * tap_flops,
    )
    later = shift(sum_head, "y", -1)
    up_act, grad_sum = lax.optimization_barrier((up_act, grad_sum))
    up_part = call(
        up_grad_kernel, (), (core_arg, up_act, mine, other),
        [SMEM, whole(act_shape), whole(mine.shape), whole(mine.shape)],
        [((64, 32, CH), BF16)],
        [pltpu.VMEM((FR, ROWS + 1, 2, OWN, 4 * CH), BF16), pltpu.VMEM((CH, FR * ROWS * OWN), BF16)], 4 * tap_flops,
    )
    grad_table = pltpu.VMEM((FR, ROWS + 2, WIN, 3 * CH), BF16)
    grad_scratch = [grad_table, pltpu.VMEM((CH, (FR + 2) * ROWS * WIN), BF16), pltpu.VMEM((TAPS * CH + 8, CH), F32)]
    early = call(
        second_grad_kernel, (), (place, first_act, grad_sum, up_part),
        [SMEM, whole(six_frames), whole(act_shape), whole(up_part.shape)],
        [((64, UP_ROWS + PIECE, CH), BF16)], grad_scratch, 27 * tap_flops,
    )
    early, later = lax.optimization_barrier((early, later))
    early = lax.all_to_all(early, ("z", "x_hi", "width"), 0, 0, tiled=True)

    grad_hidden, hidden_head = call(
        hidden_kernel, (3,), (grad_sum, later, first_slope, conv_second, mask),
        [whole(act_shape), whole(later.shape), whole(act_shape), tap_weights(), whole(mask.shape)],
        [(act_shape, BF16), (two_frames, BF16)], [table, total], 27 * tap_flops,
    )
    later_hidden = lax.ppermute(hidden_head, ("y", "core"), [(2 * i + 1, 2 * i - 1) for i in range(1, 4)])
    blocks = call(
        first_grad_kernel, (), (place, block, other_block, grad_hidden),
        [SMEM, whole(block.shape), whole(block.shape), whole(act_shape)],
        [((16, PIECE, CH), BF16)] * 4, grad_scratch, 27 * tap_flops,
    )
    arrived = [blocks[0]]
    for step in (2, 1, 3):
        arrived.append(over_y(blocks[step], step))
    tied_hidden, _ = lax.optimization_barrier((grad_hidden, blocks[0]))
    rows_out = call(
        features_kernel, (3,), (core_arg, tied_hidden, later_hidden, grad_sum, conv_first),
        [SMEM, whole(act_shape), whole(later_hidden.shape), whole(act_shape), tap_weights()],
        [((ROWS, 2, OWN, CH), BF16)], [own_table, pltpu.VMEM((2 * ROWS * OWN, CH), F32)], 7 * tap_flops,
    )

    tied_rows, early = lax.optimization_barrier((rows_out, early))
    early = jnp.sum(early.reshape(16, 4, UP_ROWS + PIECE, CH).astype(F32), axis=0)
    early_total = early[0]
    for step in (2, 1, 3):
        early_total += over_y(early[step].astype(BF16), step).astype(F32)
    first_sum = sum(value.astype(F32) for value in arrived).astype(BF16)
    late = jnp.concatenate([tied_rows.reshape(16, 2 * OWN, CH), first_sum], axis=1)
    late = lax.all_to_all(late, ("z", "x_hi", "width"), 0, 0, tiled=True)

    factor = 1.0 / math.sqrt(32768)
    early = early_total * factor
    returned = late[:, : 2 * OWN].reshape(8, 2, 2, OWN, CH).transpose(2, 1, 0, 3, 4)
    first_share = jnp.sum(late[:, 2 * OWN : 2 * OWN + SHARE].astype(F32), axis=0) * factor
    return (
        returned.reshape(2, 1, 128, CH),
        first_share.reshape(-1),
        early[UP_ROWS : UP_ROWS + SHARE].reshape(-1),
        early[:UP_ROWS].reshape(-1),
    )


def solution(mesh):
    names = ("y", "core", "z", "x_hi", "width")
    split = Mesh(mesh.devices.reshape(4, 2, 4, 2, 2), names)
    tm, height = ("y", "core"), ("z", "x_hi")
    in_specs = (
        P(tm, (*height, "width"), None, None),
        P(),
        P(),
        P(),
        P(tm, height, "width", None),
    )
    flat = P(names)
    out_specs = (P(tm, (*height, "width"), None, None), flat, flat, flat)
    return jax.shard_map(shards, mesh=split, in_specs=in_specs, out_specs=out_specs, check_vma=False)
```

```python
import math

import jax
import jax.numpy as jnp
from jax import lax
from jax.experimental import pallas as pl
from jax.experimental.pallas import tpu as pltpu
from jax.sharding import Mesh, PartitionSpec as P

F32 = jnp.float32
BF16 = jnp.bfloat16
VMEM_LIMIT = 56 * 1024 * 1024

FR = 4
ROWS = 16
WIN = 16
OWN = 8
EDGE = 4
CH = 256
TAPS = 27
SHARE = 54
PIECE = 56
UP_ROWS = 32


def slope_of(values, sigma):
    return sigma * (1.0 + values * (1.0 - sigma))


def nt(lhs, rhs):
    return lax.dot_general(lhs, rhs, (((1,), (1,)), ((), ())), preferred_element_type=F32)


def nn(lhs, rhs):
    return jnp.dot(lhs, rhs, preferred_element_type=F32)


def fill_table(table, slot, block, forward):
    wide = block.astype(F32)
    before = pltpu.roll(wide, 1, axis=1).astype(BF16)
    after = pltpu.roll(wide, WIN - 1, axis=1).astype(BF16)
    table[slot, 1 : ROWS + 1, :, 0:CH] = before if forward else after
    table[slot, 1 : ROWS + 1, :, CH : 2 * CH] = block
    table[slot, 1 : ROWS + 1, :, 2 * CH : 3 * CH] = after if forward else before


def fill_own_table(table, slot, block):
    wide = block.astype(F32)
    for tap in range(3):
        moved = pltpu.roll(wide, WIN - (EDGE + 1 - tap), axis=1)
        table[slot, 1 : ROWS + 1, :, tap * CH : (tap + 1) * CH] = moved[:, :OWN].astype(BF16)


def clear_border(table):
    frames, _, columns, lanes = table.shape
    border = jnp.zeros((frames, columns, lanes), BF16)
    table[:, 0] = border
    table[:, ROWS + 1] = border


def own_columns(block):
    return pltpu.roll(block.astype(F32), WIN - EDGE, axis=1)[:, :OWN]


def forward_taps(table, step, frames, weights, total):
    rows = frames * ROWS * WIN
    for tap in range(3):
        lhs = table[pl.ds(step, frames), tap : tap + ROWS].reshape(rows, 3 * CH)
        total[:rows] += nn(lhs, weights[0, tap].reshape(3 * CH, CH))


def backward_taps(table, start, frames, columns, weights, total):
    step = pl.program_id(0)
    for tap_h in range(3):
        part = None
        for tap_w in range(3):
            lanes = slice(tap_w * CH, (tap_w + 1) * CH)
            lhs = table[pl.ds(start + 2 - step, frames), 2 - tap_h : 2 - tap_h + ROWS, :, lanes]
            more = nt(lhs.reshape(frames * ROWS * columns, CH), weights[0, tap_h, tap_w])
            part = more if part is None else part + more
        total[...] += part


def frame_of(total, frame, columns):
    rows = ROWS * columns
    return total[frame * rows : (frame + 1) * rows].reshape(ROWS, columns, CH)


def forward_kernel(core_ref, mine, other, first, second, mask, act, slope, summed, up_act, table, total):
    step = pl.program_id(0)
    core = core_ref[0]
    sources = ((mine, core), (other, 1 - core))

    @pl.when(step == 0)
    def _():
        clear_border(table)
        for source, which in sources:
            for frame in range(FR):
                slot = 2 * which + (frame if frame < 2 else frame + 2)
                fill_table(table, slot, source[:, frame], True)
        total[...] = jnp.zeros_like(total)

    @pl.when(step < 3)
    def _():
        forward_taps(table, step, FR + 2, first, total)

    @pl.when(step == 2)
    def _():
        for frame in range(FR + 2):
            values = frame_of(total, frame, WIN)
            sigma = jax.nn.sigmoid(values)
            result = (values * sigma * mask[...]).astype(BF16)
            act[frame] = result
            fill_table(table, frame, result, True)
            if frame >= 2:
                slope[frame - 2] = slope_of(values, sigma)
        total[...] = jnp.zeros_like(total)

    @pl.when(step >= 3)
    def _():
        forward_taps(table, step - 3, FR, second, total)

    @pl.when(step == 5)
    def _():
        rows = ROWS * WIN
        for source, which in sources:
            for frame in range(2):
                place = 2 * which + frame
                values = total[pl.ds(pl.multiple_of(place * rows, rows), rows)].reshape(ROWS, WIN, CH)
                values = values + source[:, 2 + frame].astype(F32)
                summed[place] = values
                up_act[place] = (values * jax.nn.sigmoid(values)).astype(BF16)


def hidden_kernel(block, later, slope, weights, mask, grad_hidden, head, table, total):
    @pl.when(pl.program_id(0) == 0)
    def _():
        clear_border(table)
        for frame in range(FR):
            fill_table(table, frame, block[frame], False)
        for frame in range(2):
            fill_table(table, FR + frame, later[frame], False)
        total[...] = jnp.zeros_like(total)

    backward_taps(table, 0, FR, WIN, weights, total)

    @pl.when(pl.program_id(0) == 2)
    def _():
        for frame in range(FR):
            result = (frame_of(total, frame, WIN) * slope[frame] * mask[...]).astype(BF16)
            grad_hidden[frame] = result
            if frame < 2:
                head[frame] = result


def features_kernel(core_ref, block, later, grad_sum, weights, grad_features, table, total):
    core = core_ref[0]

    @pl.when(pl.program_id(0) == 0)
    def _():
        clear_border(table)
        for frame in range(FR):
            fill_own_table(table, frame, block[frame])
        for frame in range(2):
            fill_own_table(table, FR + frame, later[frame])
        total[...] = jnp.zeros_like(total)

    backward_taps(table, 2 * core, 2, OWN, weights, total)

    @pl.when(pl.program_id(0) == 2)
    def _():
        for frame in range(2):
            values = frame_of(total, frame, OWN) + own_columns(grad_sum[2 * core + frame])
            grad_features[:, frame] = values.astype(BF16)


def cotangent_kernel(core_ref, mine, other, weights, summed, mask, grad_sum, head, table):
    core = core_ref[0]
    border = jnp.zeros((FR, WIN, 4 * CH), BF16)
    table[:, 0, 0] = border
    table[:, ROWS, 1] = border
    for source, which in ((mine, core), (other, 1 - core)):
        for frame in range(2):
            slot = 2 * which + frame
            for parity in range(2):
                fine = source[:, frame, :, parity].reshape(ROWS, WIN, 2 * CH)
                even, odd = fine[:, :, :CH], fine[:, :, CH:]
                before = pltpu.roll(odd.astype(F32), 1, axis=1).astype(BF16)
                after = pltpu.roll(even.astype(F32), WIN - 1, axis=1).astype(BF16)
                low = 0 if parity == 0 else 1
                put = (slot, slice(low, low + ROWS), 1 - parity)
                table[put + (slice(None), slice(0, CH))] = before
                table[put + (slice(None), slice(CH, 2 * CH))] = even
                table[put + (slice(None), slice(2 * CH, 3 * CH))] = odd
                table[put + (slice(None), slice(3 * CH, 4 * CH))] = after
    for frame in range(FR):
        part = None
        for tap in range(4):
            for column in range(4):
                lhs = table[frame, tap // 2 : tap // 2 + ROWS, tap % 2, :, column * CH : (column + 1) * CH]
                more = nt(lhs.reshape(ROWS * WIN, CH), weights[tap, column])
                part = more if part is None else part + more
        grad_act = part.reshape(ROWS, WIN, CH).astype(BF16).astype(F32)
        values = summed[frame]
        grad = grad_act * slope_of(values, jax.nn.sigmoid(values)) * mask[...]
        grad_sum[frame] = grad.astype(BF16)
        if frame < 2:
            head[frame] = grad.astype(BF16)


def up_grad_kernel(core_ref, act, mine, other, out, table, flipped):
    core = core_ref[0]
    border = jnp.zeros((FR, OWN, 4 * CH), BF16)
    table[:, 0, 0] = border
    table[:, ROWS, 1] = border
    for source, which in ((mine, core), (other, 1 - core)):
        for frame in range(2):
            slot = 2 * which + frame
            for parity in range(2):
                fine = source[:, frame, :, parity].reshape(ROWS, WIN, 2 * CH).astype(F32)
                even, odd = fine[:, :, :CH], fine[:, :, CH:]
                low = 0 if parity == 0 else 1
                put = (slot, slice(low, low + ROWS), 1 - parity)
                for column, (values, shift) in enumerate(((odd, -1), (even, 0), (odd, 0), (even, 1))):
                    moved = pltpu.roll(values, WIN - (EDGE + shift), axis=1)[:, :OWN].astype(BF16)
                    table[put + (slice(None), slice(column * CH, (column + 1) * CH))] = moved
    for frame in range(FR):
        rows = ROWS * OWN
        flipped[:, frame * rows : (frame + 1) * rows] = jnp.transpose(
            own_columns(act[frame]).reshape(rows, CH)
        ).astype(BF16)
    lanes = pl.ds(pl.multiple_of(core * 2 * CH, 2 * CH), 2 * CH)
    for tap in range(4):
        rhs = table[:, tap // 2 : tap // 2 + ROWS, tap % 2, :, lanes]
        result = nn(flipped[...], rhs.reshape(FR * ROWS * OWN, 2 * CH))
        for half in range(2):
            for piece in range(8):
                out[tap * 16 + half * 8 + piece] = result[
                    piece * 32 : (piece + 1) * 32, half * CH : (half + 1) * CH
                ].astype(BF16)


def tap_sums(frames, block, table, flipped, sums):
    clear_border(table)
    column = lax.broadcasted_iota(jnp.int32, (ROWS, WIN, CH), 1)
    own = (column >= EDGE) & (column < EDGE + OWN)
    for frame in range(FR):
        fill_table(table, frame, jnp.where(own, block[frame].astype(F32), 0.0).astype(BF16), False)
    rows = ROWS * WIN
    for slot, values in frames:
        lanes = pl.ds(pl.multiple_of(slot * rows, rows), rows)
        flipped[:, lanes] = jnp.transpose(values.astype(F32).reshape(rows, CH)).astype(BF16)
    sums[TAPS * CH :] = jnp.zeros((8, CH), F32)
    for tap_t in range(3):
        lhs = flipped[:, tap_t * rows : (tap_t + FR) * rows]
        for tap_h in range(3):
            rhs = table[:, 2 - tap_h : 2 - tap_h + ROWS]
            result = nn(lhs, rhs.reshape(FR * rows, 3 * CH))
            for tap_w in range(3):
                at = (tap_t * 9 + tap_h * 3 + tap_w) * CH
                sums[at : at + CH] = result[:, tap_w * CH : (tap_w + 1) * CH]


def piece_of(sums, owner, member):
    at = SHARE * member
    start = pl.multiple_of(16 * SHARE * owner + at // 8 * 8, 8)
    return sums[pl.ds(start, PIECE + 8)][at % 8 : at % 8 + PIECE]


def second_grad_kernel(place, act, block, up, out, table, flipped, sums):
    tap_sums([(frame, act[frame]) for frame in range(FR + 2)], block, table, flipped, sums)
    for step in range(4):
        group = lax.rem(place[1] + step, 4)
        for member in range(16):
            chunk = member * 4 + step
            out[chunk, :UP_ROWS] = up[group * 16 + member]
            out[chunk, UP_ROWS:] = piece_of(sums, 2 * group + place[0], member).astype(BF16)


def first_grad_kernel(place, mine, other, block, own, next_one, next_two, next_three, table, flipped, sums):
    core = place[0]
    frames = []
    for frame in range(2):
        before = jnp.where(core == 1, mine[:, frame].astype(F32), other[:, frame].astype(F32))
        frames.append((frame, before))
        frames.append((2 + 2 * core + frame, mine[:, 2 + frame]))
        frames.append((4 - 2 * core + frame, other[:, 2 + frame]))
    tap_sums(frames, block, table, flipped, sums)
    for step, out in enumerate((own, next_one, next_two, next_three)):
        group = lax.rem(place[1] + step, 4)
        for member in range(16):
            out[member] = piece_of(sums, 2 * group + place[0], member).astype(BF16)


def whole(shape):
    zeros = (0,) * len(shape)
    return pl.BlockSpec(shape, lambda *_: zeros)


SMEM = pl.BlockSpec(memory_space=pltpu.SMEM)


def tap_weights(begin=0):
    return pl.BlockSpec((1, 3, 3, CH, CH), lambda step: (jnp.clip(step - begin, 0, 2), 0, 0, 0, 0))


def call(kernel, grid, args, specs, outs, scratch, flops):
    shapes = [jax.ShapeDtypeStruct(shape, dtype) for shape, dtype in outs]
    moved = sum(math.prod(a.shape) * a.dtype.itemsize for a in args)
    moved += sum(math.prod(s.shape) * s.dtype.itemsize for s in shapes)
    single = len(shapes) == 1
    return pl.pallas_call(
        kernel,
        out_shape=shapes[0] if single else shapes,
        grid=grid,
        in_specs=specs,
        out_specs=whole(shapes[0].shape) if single else [whole(s.shape) for s in shapes],
        scratch_shapes=scratch,
        compiler_params=pltpu.CompilerParams(vmem_limit_bytes=VMEM_LIMIT),
        cost_estimate=pl.CostEstimate(flops=int(flops), bytes_accessed=moved, transcendentals=0),
    )(*args)


def shift(value, axis, step):
    count = lax.axis_size(axis)
    return lax.ppermute(value, axis, [(i, i + step) for i in range(count) if 0 <= i + step < count])


def over_y(value, step):
    return lax.ppermute(value, "y", [(i, (i + step) % 4) for i in range(4)])


def shards(features, conv_first, conv_second, up_kernel, cotangent):
    core = lax.axis_index("core")
    height = 2 * lax.axis_index("z") + lax.axis_index("x_hi")
    width = lax.axis_index("width")
    core_arg = core.astype(jnp.int32).reshape(1)
    place = jnp.stack([core, lax.axis_index("y")]).astype(jnp.int32)
    window = 8 * width + height
    columns = OWN * window - EDGE + jnp.arange(WIN)
    inside = ((columns >= 0) & (columns < 128)).astype(F32)
    mask = jnp.broadcast_to(inside[:, None], (WIN, CH))
    act_shape = (FR, ROWS, WIN, CH)
    two_frames = (2, ROWS, WIN, CH)
    six_frames = (FR + 2, ROWS, WIN, CH)
    table = pltpu.VMEM((FR + 2, ROWS + 2, WIN, 3 * CH), BF16)
    own_table = pltpu.VMEM((FR + 2, ROWS + 2, OWN, 3 * CH), BF16)
    total = pltpu.VMEM((FR * ROWS * WIN, CH), F32)
    tap_flops = 2 * FR * ROWS * WIN * CH * CH

    paired = cotangent.reshape(2, 4, 64, 2 * CH)
    edge = jnp.where(width == 0, paired[:, :, 64 - EDGE :], paired[:, :, :EDGE])
    edge = lax.ppermute(edge, "width", [(0, 1), (1, 0)])
    frames = features[:, 0]
    before, edge = lax.optimization_barrier((shift(frames, "y", 1), edge))
    frames = jnp.concatenate([before, frames], axis=0)
    padded = jnp.pad(frames, ((0, 0), (EDGE, EDGE), (0, 0))).reshape(4, 17, OWN, CH)
    windows = jnp.concatenate([padded[:, :-1], padded[:, 1:]], axis=2)
    windows = windows.reshape(4, 2, 8, WIN, CH).transpose(2, 1, 0, 3, 4).reshape(16, 4, WIN, CH)
    block = lax.all_to_all(windows, ("z", "x_hi", "width"), 0, 0, tiled=True)

    nothing = jnp.zeros_like(edge)
    low, high = jnp.where(width == 0, nothing, edge), jnp.where(width == 0, edge, nothing)
    paired = jnp.concatenate([low, paired, high], axis=2).reshape(2, 4, 9, OWN, 2 * CH)
    fine = jnp.concatenate([paired[:, :, :-1], paired[:, :, 1:]], axis=3).transpose(2, 0, 1, 3, 4)
    fine, block = lax.optimization_barrier((fine.reshape(64, WIN, 2 * CH), block))
    swap = [(0, 1), (1, 0)]
    other_block = lax.ppermute(block, "core", swap)
    mine = lax.all_to_all(fine.reshape(8, 8, WIN, 2 * CH), ("z", "x_hi"), 0, 0, tiled=True).reshape(8, 2, 2, 2, WIN, 2 * CH)

    first_act, first_slope, summed, up_act = call(
        forward_kernel, (6,), (core_arg, block, other_block, conv_first, conv_second, mask),
        [SMEM, whole(block.shape), whole(block.shape), tap_weights(0), tap_weights(3), whole(mask.shape)],
        [(six_frames, BF16), (act_shape, F32), (act_shape, F32), (act_shape, BF16)],
        [pltpu.VMEM((FR + 4, ROWS + 2, WIN, 3 * CH), BF16), pltpu.VMEM(((FR + 2) * ROWS * WIN, CH), F32)],
        67 * tap_flops,
    )
    mine, up_act = lax.optimization_barrier((mine, up_act))
    other = lax.ppermute(mine, "core", swap)
    grad_sum, sum_head = call(
        cotangent_kernel, (), (core_arg, mine, other, up_kernel, summed, mask),
        [SMEM, whole(mine.shape), whole(mine.shape), whole(up_kernel.shape), whole(act_shape), whole(mask.shape)],
        [(act_shape, BF16), (two_frames, BF16)], [pltpu.VMEM((FR, ROWS + 1, 2, WIN, 4 * CH), BF16)], 16 * tap_flops,
    )
    later = shift(sum_head, "y", -1)
    up_act, grad_sum = lax.optimization_barrier((up_act, grad_sum))
    up_part = call(
        up_grad_kernel, (), (core_arg, up_act, mine, other),
        [SMEM, whole(act_shape), whole(mine.shape), whole(mine.shape)],
        [((64, 32, CH), BF16)],
        [pltpu.VMEM((FR, ROWS + 1, 2, OWN, 4 * CH), BF16), pltpu.VMEM((CH, FR * ROWS * OWN), BF16)], 4 * tap_flops,
    )
    grad_table = pltpu.VMEM((FR, ROWS + 2, WIN, 3 * CH), BF16)
    grad_scratch = [grad_table, pltpu.VMEM((CH, (FR + 2) * ROWS * WIN), BF16), pltpu.VMEM((TAPS * CH + 8, CH), F32)]
    early = call(
        second_grad_kernel, (), (place, first_act, grad_sum, up_part),
        [SMEM, whole(six_frames), whole(act_shape), whole(up_part.shape)],
        [((64, UP_ROWS + PIECE, CH), BF16)], grad_scratch, 27 * tap_flops,
    )
    early, later = lax.optimization_barrier((early, later))
    early = lax.all_to_all(early, ("z", "x_hi", "width"), 0, 0, tiled=True)

    grad_hidden, hidden_head = call(
        hidden_kernel, (3,), (grad_sum, later, first_slope, conv_second, mask),
        [whole(act_shape), whole(later.shape), whole(act_shape), tap_weights(), whole(mask.shape)],
        [(act_shape, BF16), (two_frames, BF16)], [table, total], 27 * tap_flops,
    )
    later_hidden = lax.ppermute(hidden_head, ("y", "core"), [(2 * i + 1, 2 * i - 1) for i in range(1, 4)])
    blocks = call(
        first_grad_kernel, (), (place, block, other_block, grad_hidden),
        [SMEM, whole(block.shape), whole(block.shape), whole(act_shape)],
        [((16, PIECE, CH), BF16)] * 4, grad_scratch, 27 * tap_flops,
    )
    arrived = [blocks[0]]
    for step in (2, 1, 3):
        arrived.append(over_y(blocks[step], step))
    tied_hidden, _ = lax.optimization_barrier((grad_hidden, blocks[0]))
    rows_out = call(
        features_kernel, (3,), (core_arg, tied_hidden, later_hidden, grad_sum, conv_first),
        [SMEM, whole(act_shape), whole(later_hidden.shape), whole(act_shape), tap_weights()],
        [((ROWS, 2, OWN, CH), BF16)], [own_table, pltpu.VMEM((2 * ROWS * OWN, CH), F32)], 7 * tap_flops,
    )

    tied_rows, early = lax.optimization_barrier((rows_out, early))
    early = jnp.sum(early.reshape(16, 4, UP_ROWS + PIECE, CH).astype(F32), axis=0)
    early_total = early[0]
    for step in (2, 1, 3):
        early_total += over_y(early[step].astype(BF16), step).astype(F32)
    first_sum = sum(value.astype(F32) for value in arrived).astype(BF16)
    late = jnp.concatenate([tied_rows.reshape(16, 2 * OWN, CH), first_sum], axis=1)
    late = lax.all_to_all(late, ("z", "x_hi", "width"), 0, 0, tiled=True)

    factor = 1.0 / math.sqrt(32768)
    early = early_total * factor
    returned = late[:, : 2 * OWN].reshape(8, 2, 2, OWN, CH).transpose(2, 1, 0, 3, 4)
    first_share = jnp.sum(late[:, 2 * OWN : 2 * OWN + SHARE].astype(F32), axis=0) * factor
    return (
        returned.reshape(2, 1, 128, CH),
        first_share.reshape(-1),
        early[UP_ROWS : UP_ROWS + SHARE].reshape(-1),
        early[:UP_ROWS].reshape(-1),
    )


def solution(mesh):
    names = ("y", "core", "z", "x_hi", "width")
    split = Mesh(mesh.devices.reshape(4, 2, 4, 2, 2), names)
    tm, height = ("y", "core"), ("z", "x_hi")
    in_specs = (
        P(tm, (*height, "width"), None, None),
        P(),
        P(),
        P(),
        P(tm, height, "width", None),
    )
    flat = P(names)
    out_specs = (P(tm, (*height, "width"), None, None), flat, flat, flat)
    return jax.shard_map(shards, mesh=split, in_specs=in_specs, out_specs=out_specs, check_vma=False)
```
